32 devices in a mesh: fsdp: 32 (over z, y, x, core).
Axes of the slice: x: 2, y: 2, z: 4, core: 2. Of those that a mesh axis runs over, the one named last changes fastest.
Arguments:
- tokens: bfloat16 [4096, 1536], P('fsdp'), may hold values from -6 to 6
- segment: int32 [4096], P('fsdp'), may hold values from -1 to 3, as said below
- position: int32 [4096], P('fsdp'), may hold values from 0 to 127, as said below
- first_gain: bfloat16 [1536], P('fsdp'), may hold values from 0.25 to 1.75
- query_weight: bfloat16 [1536, 1536], P('fsdp'), may hold values from -0.15625 to 0.15625
- query_bias: bfloat16 [1536], P('fsdp'), may hold values from -3 to 3
- key_weight: bfloat16 [1536, 256], P('fsdp'), may hold values from -0.15625 to 0.15625
- key_bias: bfloat16 [256], P('fsdp'), may hold values from -3 to 3
- value_weight: bfloat16 [1536, 256], P('fsdp'), may hold values from -0.15625 to 0.15625
- value_bias: bfloat16 [256], P('fsdp'), may hold values from -3 to 3
- out_weight: bfloat16 [1536, 1536], P('fsdp'), may hold values from -1.25 to 1.25
- second_gain: bfloat16 [1536], P('fsdp'), may hold values from 0.25 to 1.75
- gate_weight: bfloat16 [1536, 8960], P('fsdp'), may hold values from -0.15625 to 0.15625
- up_weight: bfloat16 [1536, 8960], P('fsdp'), may hold values from -0.15625 to 0.15625
- down_weight: bfloat16 [1536, 8960], P('fsdp'), may hold values from -0.0625 to 0.0625
- cotangent: bfloat16 [4096, 1536], P('fsdp'), may hold values from -6 to 6
Outputs:
- block_output: bfloat16 [4096, 1536], P('fsdp')
- input_gradient: bfloat16 [4096, 1536], P('fsdp')
- first_gain_gradient: float32 [1536], P('fsdp')
- query_weight_gradient: float32 [1536, 1536], P('fsdp')
- query_bias_gradient: float32 [1536], P('fsdp')
- key_weight_gradient: float32 [1536, 256], P('fsdp')
- key_bias_gradient: float32 [256], replicated
- value_weight_gradient: float32 [1536, 256], P('fsdp')
- value_bias_gradient: float32 [256], P('fsdp')
- out_weight_gradient: float32 [1536, 1536], P('fsdp')
- second_gain_gradient: float32 [1536], P('fsdp')
- gate_weight_gradient: float32 [1536, 8960], P('fsdp')
- up_weight_gradient: float32 [1536, 8960], P('fsdp')
- down_weight_gradient: float32 [1536, 8960], P('fsdp')
The draws below stay inside these ranges and needn't reach their ends.
Inputs may be any that keep to these rules, and one draw needn't show every extreme that they name: `segment`: within a block of 128 slots the live tokens come first: each of at most 4 sequences stands in one run of slots and carries one number, numbers never fall along a block, and -1 marks the padding after the last live token; in every draw some block holds a single sequence of 128 tokens. `position`: A live token's offset within its sequence, counted from 0; a padding slot's offset counted from 0 at the block's first padding slot.
All inputs are finite; a program needn't handle non-finite values.
Results may differ from the reference program's by a relative error of at most 0.025.
Values may be sent and summed in bfloat16 or wider, within the bound.
A program may use at most 640 MiB of HBM per device.

```python
import math
import jax
import jax.numpy as jnp
from jax import lax

D = 1536
H = 12
KV = 2
HD = 128
FF = 8960
BLOCK = 128
SEQ_DEV = 4
KVD = 256
TOKENS = 4096


def layout(key):
    blocks = TOKENS // BLOCK
    device_ids = jnp.arange(blocks)
    fill = jax.random.randint(jax.random.fold_in(key, 11), (blocks,), BLOCK // 2, BLOCK + 1)
    full_device = jax.random.randint(jax.random.fold_in(key, 13), (), 0, blocks)
    fill = jnp.where(device_ids == full_device, BLOCK, fill)
    raw_cuts = jax.random.randint(jax.random.fold_in(key, 12), (blocks, SEQ_DEV - 1), 0, 1048576)
    cuts = raw_cuts % (fill[:, None] - 1) + 1
    cuts = jnp.where((device_ids == full_device)[:, None], fill[:, None], cuts)
    slots = jnp.arange(BLOCK)
    passed = cuts[:, None, :] <= slots[None, :, None]
    segment_ids = jnp.sum(passed.astype(jnp.int32), axis=-1)
    starts = jnp.max(jnp.where(passed, cuts[:, None, :], 0), axis=-1)
    live = slots[None, :] < fill[:, None]
    segment_ids = jnp.where(live, segment_ids, -1)
    offsets = jnp.where(live, slots[None, :] - starts, slots[None, :] - fill[:, None])
    return (segment_ids.reshape(-1).astype(jnp.int32), offsets.reshape(-1).astype(jnp.int32))


def draw_segment(key, part):
    return layout(key)[0]


def draw_position(key, part):
    return layout(key)[1]


def with_spikes(values, rng, source, target, shards_of, factor):
    owner, partner = [(jnp.arange(values.shape[dim]) // (values.shape[dim] // shards_of)).reshape([-1 if axis == dim else 1 for axis in range(values.ndim)]) for dim in (source, target)]
    chosen = jax.random.permutation(rng, shards_of)[partner]
    strong = (owner == chosen) | (owner == (partner + shards_of // 2) % shards_of)
    return jnp.where(strong, factor * values, values)


def block_levels(key, shape, cuts, least, top_value):
    def one(dim, parts):
        steps = jax.random.uniform(jax.random.fold_in(jax.random.fold_in(key, 6), dim), (parts,), jnp.float32, least / len(cuts), top_value / len(cuts))
        return jnp.repeat(jnp.exp(steps), shape[dim] // parts).reshape((-1,) + (1,) * (len(shape) - dim - 1))

    gain = one(*cuts[0])
    for cut in cuts[1:]:
        gain = gain * one(*cut)
    return gain


def normal_values(own_key, dims, deviation, reach, cuts=(), held_as=jnp.bfloat16):
    values = jax.random.normal(own_key, dims, jnp.float32) * deviation
    if len(cuts) > 0:
        values = block_levels(own_key, dims, cuts, -0.22, 0.18) * values
    return jnp.clip(values, min=-reach, max=reach).astype(held_as)


def bell_draw_with(stream_key, shape, width, most, split, heavy, held_as=jnp.bfloat16):
    drawn = width * jax.random.normal(stream_key, shape, jnp.float32)
    if split:
        drawn = drawn * block_levels(stream_key, shape, split, -0.22, 0.18)
    return jnp.clip(with_spikes(drawn, jax.random.fold_in(stream_key, 3), *heavy), -most, most).astype(held_as)


def setup_inputs(seed: int = 0) -> dict:
    splits = jax.random.split(jax.random.key(seed), 17)
    return {
        "tokens": bell_draw_with(splits[0], (TOKENS, D), 1.0, 6.0, ((0, 32),), (0, 1, 32, 2.75)),
        "segment": draw_segment(jax.random.fold_in(splits[16], 71), 0),
        "position": draw_position(jax.random.fold_in(splits[16], 71), 0),
        "first_gain": jnp.clip(1.0 + 0.15 * jax.random.normal(splits[3], (D,), jnp.float32), 0.25, 1.75).astype(jnp.bfloat16),
        "query_weight": normal_values(splits[4], (D, D), D ** -0.5, 0.15625, ((0, 32),)),
        "query_bias": normal_values(splits[5], (D,), 0.5, 3.0, ((0, 32),)),
        "key_weight": normal_values(splits[6], (D, KVD), D ** -0.5, 0.15625, ((0, 32),)),
        "key_bias": normal_values(splits[7], (KVD,), 0.5, 3.0, ((0, 32),)),
        "value_weight": normal_values(splits[8], (D, KVD), D ** -0.5, 0.15625, ((0, 32),)),
        "value_bias": normal_values(splits[9], (KVD,), 0.5, 3.0, ((0, 32),)),
        "out_weight": normal_values(splits[10], (D, D), (D // 64) ** -0.5, 1.25, ((0, 32),)),
        "second_gain": jnp.clip(1.0 + 0.15 * jax.random.normal(splits[11], (D,), jnp.float32), 0.25, 1.75).astype(jnp.bfloat16),
        "gate_weight": normal_values(splits[12], (D, FF), D ** -0.5, 0.15625, ((0, 32),)),
        "up_weight": normal_values(splits[13], (D, FF), D ** -0.5, 0.15625, ((0, 32),)),
        "down_weight": normal_values(splits[14], (D, FF), FF ** -0.5, 0.0625, ((0, 32),)),
        "cotangent": bell_draw_with(splits[15], (TOKENS, D), 1.0, 6.0, ((0, 32),), (0, 1, 32, 2.75)),
    }


EPSILON = 1e-06
ROPE_BASE = 1000000.0
precise = lax.Precision.HIGHEST

@jax.custom_vjp
def low(v):
    return lax.optimization_barrier(v.astype(jnp.bfloat16)).astype(jnp.float32)

@jax.custom_vjp
def low_back(v):
    return v

def low_keep(v):
    return (low(v), None)

def low_pass(kept, grad):
    return (grad,)

def back_keep(v):
    return (v, None)

def back_low(kept, grad):
    return (low(grad),)
low.defvjp(low_keep, low_pass)
low_back.defvjp(back_keep, back_low)

def tables(position):
    freq_index = jnp.arange(HD // 2).astype(jnp.float32)
    frequency = jnp.exp(freq_index * (-2.0 * math.log(ROPE_BASE) / HD))
    angles = position.astype(jnp.float32)[:, None] * frequency[None, :]
    angles = jnp.concatenate([angles, angles], axis=-1)
    return (jnp.cos(angles)[:, None, :], jnp.sin(angles)[:, None, :])

def rotary(values, cosine_table, sine_table):
    middle = values.shape[-1] // 2
    turned = jnp.concatenate([-values[..., middle:], values[..., :middle]], axis=-1)
    return values * cosine_table + turned * sine_table

def attend(operands):
    queries, key_rows, value_rows, segment = operands
    length = segment.shape[0]
    slot_order = jnp.arange(length)
    visible = (segment[:, None] == segment[None, :]) & (slot_order[None, :] <= slot_order[:, None])
    scores = jnp.einsum('qkgd,skd->kgqs', queries, key_rows, precision=precise) * (1.0 / math.sqrt(HD))
    scores = low_back(scores)
    scores = jnp.where(visible, scores, -jnp.inf)
    attention = low(jax.nn.softmax(scores, axis=-1))
    mixed_heads = jnp.einsum('kgqs,skd->qkgd', attention, value_rows, precision=precise)
    return mixed_heads.reshape(length, H * HD)

def forward(tokens, first_gain, query_weight, query_bias, key_weight, key_bias, value_weight, value_bias, out_weight, second_gain, gate_weight, up_weight, down_weight, segment, position):
    length = tokens.shape[0]
    blocks = length // BLOCK
    live_rows = (segment >= 0).astype(jnp.float32)[:, None]
    cosine_table, sine_table = tables(position)
    scale_one = lax.rsqrt(lax.optimization_barrier(jnp.mean(tokens * tokens, axis=-1, keepdims=True)) + EPSILON)
    normed_one = low(tokens * scale_one * first_gain)
    query_pre = low_back(jnp.dot(normed_one, query_weight, precision=precise) + query_bias)
    key_pre = low_back(jnp.dot(normed_one, key_weight, precision=precise) + key_bias)
    value_rows = low(low_back(jnp.dot(normed_one, value_weight, precision=precise) + value_bias))
    queries = low(rotary(query_pre.reshape(length, H, HD), cosine_table, sine_table))
    key_rows = low(rotary(key_pre.reshape(length, KV, HD), cosine_table, sine_table))
    mixed_heads = lax.map(jax.checkpoint(attend), (queries.reshape(blocks, BLOCK, KV, H // KV, HD), key_rows.reshape(blocks, BLOCK, KV, HD), value_rows.reshape(blocks, BLOCK, KV, HD), segment.reshape(blocks, BLOCK)))
    mixed_heads = low(low_back(mixed_heads.reshape(length, H * HD)))
    branch = low_back(jnp.dot(mixed_heads, out_weight.T, precision=precise))
    hidden_state = tokens + branch
    scale_two = lax.rsqrt(lax.optimization_barrier(jnp.mean(hidden_state * hidden_state, axis=-1, keepdims=True)) + EPSILON)
    normed_two = low(hidden_state * scale_two * second_gain)
    gate_value = low_back(jnp.dot(normed_two, gate_weight, precision=precise))
    up_value = low_back(jnp.dot(normed_two, up_weight, precision=precise))
    activated = low(jax.nn.silu(gate_value) * up_value)
    feed_out = low_back(jnp.dot(activated, down_weight.T, precision=precise))
    return live_rows * (hidden_state + feed_out)

def reference(tokens, segment, position, first_gain, query_weight, query_bias, key_weight, key_bias, value_weight, value_bias, out_weight, second_gain, gate_weight, up_weight, down_weight, cotangent):
    as_float = [array.astype(jnp.float32) for array in (tokens, first_gain, query_weight, query_bias, key_weight, key_bias, value_weight, value_bias, out_weight, second_gain, gate_weight, up_weight, down_weight)]

    def closed(*params):
        return forward(*params, segment, position)
    result, pullback = jax.vjp(closed, *as_float)
    gradients = pullback(cotangent.astype(jnp.float32))
    return (result.astype(jnp.bfloat16), gradients[0].astype(jnp.bfloat16), gradients[1], gradients[2], gradients[3], gradients[4], gradients[5], gradients[6], gradients[7], gradients[8], gradients[9], gradients[10], gradients[11], gradients[12])
```

```python
import math

import jax
import jax.numpy as jnp
from jax import lax
from jax.sharding import PartitionSpec as P

H = 12
KV = 2
HD = 128
GROUP = 8

EPSILON = 1e-06
ROPE_BASE = 1000000.0
AXIS = "fsdp"
F32 = jnp.float32
BF16 = jnp.bfloat16


def tables(position):
    freq_index = jnp.arange(HD // 2).astype(F32)
    frequency = jnp.exp(freq_index * (-2.0 * math.log(ROPE_BASE) / HD))
    angles = position.astype(F32)[:, None] * frequency[None, :]
    angles = jnp.concatenate([angles, angles], axis=-1)
    return (jnp.cos(angles)[:, None, :], jnp.sin(angles)[:, None, :])


def rotary(values, cosine_table, sine_table):
    middle = values.shape[-1] // 2
    turned = jnp.concatenate([-values[..., middle:], values[..., :middle]], axis=-1)
    return values * cosine_table + turned * sine_table


def rotary_back(gradient, cosine_table, sine_table):
    middle = gradient.shape[-1] // 2
    weighted = gradient * sine_table
    return gradient * cosine_table + jnp.concatenate(
        [weighted[..., middle:], -weighted[..., :middle]], axis=-1
    )


def norm_back(weighted, values, row_scale):
    return row_scale * weighted - values * row_scale**3 * jnp.mean(
        weighted * values, axis=-1, keepdims=True
    )


def dot(left, right, dims):
    return lax.dot_general(left, right, ((dims[:1], dims[1:]), ((), ())), preferred_element_type=F32)


def groups_of(count):
    plane = count // GROUP
    lines = GROUP // 2
    token = [[(z * plane + p) * 2 + c for z in range(lines) for c in range(2)] for p in range(plane)]
    other = [[(z * plane + p) * 2 + c for p in range(plane)] for z in range(lines) for c in range(2)]
    return token, other


def array_body(
    tokens,
    segment,
    position,
    first_gain,
    query_weight,
    query_bias,
    key_weight,
    key_bias,
    value_weight,
    value_bias,
    out_weight,
    second_gain,
    gate_weight,
    up_weight,
    down_weight,
    cotangent,
):
    count = lax.axis_size(AXIS)
    me = lax.axis_index(AXIS)
    token_groups, plane_groups = groups_of(count)
    plane = count // GROUP
    lines = GROUP // 2
    rows, width = query_weight.shape
    hidden = gate_weight.shape[1]
    shard = hidden // GROUP
    key_width = key_weight.shape[1]
    length = tokens.shape[0]
    heads_per_key = H // KV
    factor = 1.0 / math.sqrt(HD)

    gain_one = first_gain.astype(F32)[:, None]
    gain_two = second_gain.astype(F32)[:, None]

    def scaled(weight, gain):
        return (weight.astype(F32) * gain).astype(BF16)

    attention_own = jnp.concatenate(
        [scaled(query_weight, gain_one), scaled(key_weight, gain_one), scaled(value_weight, gain_one), out_weight], axis=1
    )
    attention_all = lax.all_gather(attention_own, AXIS, axis=0, tiled=True)
    input_width = width + 2 * key_width
    weight_input = attention_all[:, :input_width]
    weight_out = attention_all[:, input_width:]
    biases = lax.all_gather(jnp.concatenate([query_bias, key_bias, value_bias]), AXIS, axis=0, tiled=False).astype(F32)
    cut = (rows, rows + key_bias.shape[0])
    bias_input = jnp.concatenate(
        [biases[:, : cut[0]].reshape(-1), biases[:, cut[0] : cut[1]].reshape(-1), biases[:, cut[1] :].reshape(-1)]
    )

    def spread(weight):
        pieces = weight.reshape(rows, GROUP, shard).transpose(1, 0, 2)
        got = lax.all_to_all(pieces, AXIS, split_axis=0, concat_axis=0, tiled=True, axis_index_groups=token_groups)
        full = lax.all_gather(got, AXIS, axis=0, tiled=False, axis_index_groups=plane_groups)
        full = full.reshape(plane, lines, 2, rows, shard).transpose(1, 0, 2, 3, 4)
        return full.reshape(count * rows, shard)

    weight_gate = spread(scaled(gate_weight, gain_two))
    weight_up = spread(scaled(up_weight, gain_two))
    weight_down = spread(down_weight)

    live_rows = (segment >= 0).astype(F32)[:, None]
    slot_order = jnp.arange(length)
    visible = (segment[:, None] == segment[None, :]) & (slot_order[None, :] <= slot_order[:, None])
    cosine_table, sine_table = tables(position)
    token_float = tokens.astype(F32)
    scale_one = lax.rsqrt(jnp.mean(token_float * token_float, axis=-1, keepdims=True) + EPSILON)
    normed_one = (token_float * scale_one).astype(BF16)
    projected = dot(normed_one, weight_input, (1, 0)) + bias_input
    queries = rotary(projected[:, :width].reshape(length, H, HD), cosine_table, sine_table).astype(BF16)
    queries = queries.reshape(length, KV, heads_per_key, HD)
    key_rows = rotary(
        projected[:, width : width + key_width].reshape(length, KV, HD), cosine_table, sine_table
    ).astype(BF16)
    value_rows = projected[:, width + key_width :].astype(BF16).reshape(length, KV, HD)
    scores = jnp.einsum("qkgd,skd->kgqs", queries, key_rows, preferred_element_type=F32) * factor
    probs = jax.nn.softmax(jnp.where(visible, scores, -jnp.inf), axis=-1)
    probs_low = probs.astype(BF16)
    mixed_heads = jnp.einsum("kgqs,skd->qkgd", probs_low, value_rows, preferred_element_type=F32)
    mixed_heads = mixed_heads.reshape(length, H * HD).astype(BF16)
    hidden_state = token_float + dot(mixed_heads, weight_out, (1, 1))
    scale_two = lax.rsqrt(jnp.mean(hidden_state * hidden_state, axis=-1, keepdims=True) + EPSILON)
    normed_two = (hidden_state * scale_two).astype(BF16)
    upstream = cotangent.astype(F32) * live_rows
    group_tokens = lax.all_gather(normed_two, AXIS, axis=0, tiled=True, axis_index_groups=token_groups)
    group_upstream = lax.all_gather(
        upstream.astype(BF16), AXIS, axis=0, tiled=True, axis_index_groups=token_groups
    )

    gate_value = dot(group_tokens, weight_gate, (1, 0))
    up_value = dot(group_tokens, weight_up, (1, 0))
    sigmoid_gate = jax.nn.sigmoid(gate_value)
    activated = (gate_value * sigmoid_gate * up_value).astype(BF16)
    act_grad = dot(group_upstream, weight_down, (1, 0))
    gate_grad = (act_grad * up_value * sigmoid_gate * (1.0 + gate_value * (1.0 - sigmoid_gate))).astype(BF16)
    up_grad = (act_grad * gate_value * sigmoid_gate).astype(BF16)

    def fold_tokens(term):
        return lax.psum_scatter(
            term.astype(BF16), AXIS, scatter_dimension=0, tiled=True, axis_index_groups=token_groups
        ).astype(F32)

    weighted_two = fold_tokens(dot(gate_grad, weight_gate, (1, 1)) + dot(up_grad, weight_up, (1, 1)))
    feed_out = fold_tokens(dot(activated, weight_down, (1, 1)))
    block_output = (live_rows * (hidden_state + feed_out)).astype(BF16)

    def fold_feed(term):
        pieces = term.astype(BF16).reshape(lines, plane, 2, rows, shard).transpose(1, 0, 2, 3, 4)
        pieces = lax.all_to_all(
            pieces.reshape(plane, GROUP * rows, shard), AXIS, split_axis=0, concat_axis=0, tiled=True,
            axis_index_groups=plane_groups,
        )
        mine = jnp.sum(pieces.astype(F32), axis=0).astype(BF16).reshape(GROUP, rows, shard)
        mine = lax.all_to_all(mine, AXIS, split_axis=0, concat_axis=0, tiled=True, axis_index_groups=token_groups)
        return mine.transpose(1, 0, 2).reshape(rows, hidden).astype(F32)

    down_sum = fold_feed(dot(group_upstream, activated, (0, 0)))
    gate_raw = fold_feed(dot(group_tokens, gate_grad, (0, 0)))
    up_raw = fold_feed(dot(group_tokens, up_grad, (0, 0)))
    gain_two_sum = jnp.sum(gate_raw * gate_weight.astype(F32) + up_raw * up_weight.astype(F32), axis=1)

    hidden_grad = upstream + norm_back(weighted_two, hidden_state, scale_two)
    branch_grad = hidden_grad.astype(BF16)
    mixed_grad = dot(branch_grad, weight_out, (1, 0)).astype(BF16).reshape(length, KV, heads_per_key, HD)
    prob_grad = jnp.einsum("qkgd,skd->kgqs", mixed_grad, value_rows, preferred_element_type=F32)
    value_grad = jnp.einsum("kgqs,qkgd->skd", probs_low, mixed_grad, preferred_element_type=F32)
    score_grad = probs * (prob_grad - jnp.sum(probs * prob_grad, axis=-1, keepdims=True))
    score_grad = score_grad.astype(BF16)
    query_grad = jnp.einsum("kgqs,skd->qkgd", score_grad, key_rows, preferred_element_type=F32) * factor
    key_grad = jnp.einsum("kgqs,qkgd->skd", score_grad, queries, preferred_element_type=F32) * factor
    query_low = rotary_back(query_grad.reshape(length, H, HD), cosine_table, sine_table)
    key_low = rotary_back(key_grad, cosine_table, sine_table)
    input_low = jnp.concatenate(
        [query_low.reshape(length, width), key_low.reshape(length, key_width), value_grad.reshape(length, key_width)],
        axis=1,
    ).astype(BF16)
    attention_term = jnp.concatenate(
        [dot(normed_one, input_low, (0, 0)), dot(branch_grad, mixed_heads, (0, 0))], axis=1
    ).astype(BF16)
    attention_sum = lax.psum_scatter(attention_term, AXIS, scatter_dimension=0, tiled=True).astype(F32)
    bias_sum = lax.psum(jnp.sum(input_low, axis=0, dtype=F32), AXIS)
    input_raw = attention_sum[:, :input_width]
    out_sum = attention_sum[:, input_width:]
    input_sum = input_raw * gain_one
    own_weight = jnp.concatenate([query_weight, key_weight, value_weight], axis=1).astype(F32)
    gain_one_sum = jnp.sum(input_raw * own_weight, axis=1)
    weighted_one = dot(input_low, weight_input, (1, 1))
    token_grad = hidden_grad + norm_back(weighted_one, token_float, scale_one)
    query_bias_sum = lax.dynamic_slice(bias_sum, (me * rows,), (rows,))
    value_bias_sum = lax.dynamic_slice(
        bias_sum, (width + key_width + me * value_bias.shape[0],), (value_bias.shape[0],)
    )
    return (
        block_output,
        token_grad.astype(BF16),
        gain_one_sum,
        input_sum[:, :width],
        query_bias_sum,
        input_sum[:, width : width + key_width],
        bias_sum[width : width + key_width],
        input_sum[:, width + key_width :],
        value_bias_sum,
        out_sum,
        gain_two_sum,
        gate_raw * gain_two,
        up_raw * gain_two,
        down_sum,
    )


def solution(mesh):
    split = P(AXIS)
    split_rows = P(AXIS, None)
    return jax.shard_map(
        array_body,
        mesh=mesh,
        in_specs=(
            split_rows, split, split, split, split_rows, split, split_rows, split,
            split_rows, split, split_rows, split, split_rows, split_rows, split_rows, split_rows,
        ),
        out_specs=(
            split_rows, split_rows, split, split_rows, split, split_rows, P(),
            split_rows, split, split_rows, split, split_rows, split_rows, split_rows,
        ),
        check_vma=False,
    )
```

```python
import functools
import math

import jax
import jax.numpy as jnp
from jax import lax
from jax.experimental import pallas as pl
from jax.experimental.pallas import tpu as pltpu
from jax.sharding import PartitionSpec as P

H = 12
KV = 2
HD = 128
GROUP = 8
LINES = GROUP // 2

EPSILON = 1e-06
ROPE_BASE = 1000000.0
AXIS = "fsdp"
F32 = jnp.float32
BF16 = jnp.bfloat16


def tables(position):
    freq_index = jnp.arange(HD // 2).astype(F32)
    frequency = jnp.exp(freq_index * (-2.0 * math.log(ROPE_BASE) / HD))
    angles = position.astype(F32)[:, None] * frequency[None, :]
    angles = jnp.concatenate([angles, angles], axis=-1)
    return (jnp.cos(angles)[:, None, :], jnp.sin(angles)[:, None, :])


def rotary(values, cosine_table, sine_table):
    middle = values.shape[-1] // 2
    turned = jnp.concatenate([-values[..., middle:], values[..., :middle]], axis=-1)
    return values * cosine_table + turned * sine_table


def rotary_back(gradient, cosine_table, sine_table):
    middle = gradient.shape[-1] // 2
    weighted = gradient * sine_table
    return gradient * cosine_table + jnp.concatenate(
        [weighted[..., middle:], -weighted[..., :middle]], axis=-1
    )


def norm_back(weighted, values, row_scale):
    return row_scale * weighted - values * row_scale**3 * jnp.mean(
        weighted * values, axis=-1, keepdims=True
    )


def dot(left, right, dims):
    return lax.dot_general(left, right, ((dims[:1], dims[1:]), ((), ())), preferred_element_type=F32)


def groups_of(count):
    plane = count // GROUP
    lines = GROUP // 2
    token = [[(z * plane + p) * 2 + c for z in range(lines) for c in range(2)] for p in range(plane)]
    other = [[(z * plane + p) * 2 + c for p in range(plane)] for z in range(lines) for c in range(2)]
    return token, other


def array_body(
    tokens,
    segment,
    position,
    first_gain,
    query_weight,
    query_bias,
    key_weight,
    key_bias,
    value_weight,
    value_bias,
    out_weight,
    second_gain,
    gate_weight,
    up_weight,
    down_weight,
    cotangent,
):
    count = lax.axis_size(AXIS)
    me = lax.axis_index(AXIS)
    token_groups, plane_groups = groups_of(count)
    plane = count // GROUP
    lines = GROUP // 2
    rows, width = query_weight.shape
    hidden = gate_weight.shape[1]
    shard = hidden // GROUP
    key_width = key_weight.shape[1]
    length = tokens.shape[0]
    heads_per_key = H // KV
    factor = 1.0 / math.sqrt(HD)

    gain_one = first_gain.astype(F32)[:, None]
    gain_two = second_gain.astype(F32)[:, None]

    def scaled(weight, gain):
        return (weight.astype(F32) * gain).astype(BF16)

    attention_own = jnp.concatenate(
        [scaled(query_weight, gain_one), scaled(key_weight, gain_one), scaled(value_weight, gain_one), out_weight], axis=1
    )
    attention_all = lax.all_gather(attention_own, AXIS, axis=0, tiled=True)
    input_width = width + 2 * key_width
    weight_input = attention_all[:, :input_width]
    weight_out = attention_all[:, input_width:]
    biases = lax.all_gather(jnp.concatenate([query_bias, key_bias, value_bias]), AXIS, axis=0, tiled=False).astype(F32)
    cut = (rows, rows + key_bias.shape[0])
    bias_input = jnp.concatenate(
        [biases[:, : cut[0]].reshape(-1), biases[:, cut[0] : cut[1]].reshape(-1), biases[:, cut[1] :].reshape(-1)]
    )

    def spread(weight):
        pieces = weight.reshape(rows, GROUP, shard).transpose(1, 0, 2)
        got = lax.all_to_all(pieces, AXIS, split_axis=0, concat_axis=0, tiled=True, axis_index_groups=token_groups)
        full = lax.all_gather(got, AXIS, axis=0, tiled=False, axis_index_groups=plane_groups)
        full = full.reshape(plane, lines, 2, rows, shard).transpose(1, 0, 2, 3, 4)
        return full.reshape(count * rows, shard)

    weight_gate = spread(scaled(gate_weight, gain_two))
    weight_up = spread(scaled(up_weight, gain_two))
    weight_down = spread(down_weight)

    live_rows = (segment >= 0).astype(F32)[:, None]
    slot_order = jnp.arange(length)
    visible = (segment[:, None] == segment[None, :]) & (slot_order[None, :] <= slot_order[:, None])
    cosine_table, sine_table = tables(position)
    token_float = tokens.astype(F32)
    scale_one = lax.rsqrt(jnp.mean(token_float * token_float, axis=-1, keepdims=True) + EPSILON)
    normed_one = (token_float * scale_one).astype(BF16)
    projected = dot(normed_one, weight_input, (1, 0)) + bias_input
    queries = rotary(projected[:, :width].reshape(length, H, HD), cosine_table, sine_table).astype(BF16)
    queries = queries.reshape(length, KV, heads_per_key, HD)
    key_rows = rotary(
        projected[:, width : width + key_width].reshape(length, KV, HD), cosine_table, sine_table
    ).astype(BF16)
    value_rows = projected[:, width + key_width :].astype(BF16).reshape(length, KV, HD)
    scores = jnp.einsum("qkgd,skd->kgqs", queries, key_rows, preferred_element_type=F32) * factor
    probs = jax.nn.softmax(jnp.where(visible, scores, -jnp.inf), axis=-1)
    probs_low = probs.astype(BF16)
    mixed_heads = jnp.einsum("kgqs,skd->qkgd", probs_low, value_rows, preferred_element_type=F32)
    mixed_heads = mixed_heads.reshape(length, H * HD).astype(BF16)
    hidden_state = token_float + dot(mixed_heads, weight_out, (1, 1))
    scale_two = lax.rsqrt(jnp.mean(hidden_state * hidden_state, axis=-1, keepdims=True) + EPSILON)
    normed_two = (hidden_state * scale_two).astype(BF16)
    upstream = cotangent.astype(F32) * live_rows
    group_tokens = lax.all_gather(normed_two, AXIS, axis=0, tiled=True, axis_index_groups=token_groups)
    group_upstream = lax.all_gather(
        upstream.astype(BF16), AXIS, axis=0, tiled=True, axis_index_groups=token_groups
    )

    gate_value = dot(group_tokens, weight_gate, (1, 0))
    up_value = dot(group_tokens, weight_up, (1, 0))
    sigmoid_gate = jax.nn.sigmoid(gate_value)
    activated = (gate_value * sigmoid_gate * up_value).astype(BF16)
    act_grad = dot(group_upstream, weight_down, (1, 0))
    gate_grad = (act_grad * up_value * sigmoid_gate * (1.0 + gate_value * (1.0 - sigmoid_gate))).astype(BF16)
    up_grad = (act_grad * gate_value * sigmoid_gate).astype(BF16)

    def fold_tokens(term):
        return lax.psum_scatter(
            term.astype(BF16), AXIS, scatter_dimension=0, tiled=True, axis_index_groups=token_groups
        ).astype(F32)

    weighted_two = fold_tokens(dot(gate_grad, weight_gate, (1, 1)) + dot(up_grad, weight_up, (1, 1)))
    feed_out = fold_tokens(dot(activated, weight_down, (1, 1)))
    block_output = (live_rows * (hidden_state + feed_out)).astype(BF16)

    def fold_feed(term):
        pieces = term.astype(BF16).reshape(lines, plane, 2, rows, shard).transpose(1, 0, 2, 3, 4)
        pieces = lax.all_to_all(
            pieces.reshape(plane, GROUP * rows, shard), AXIS, split_axis=0, concat_axis=0, tiled=True,
            axis_index_groups=plane_groups,
        )
        mine = jnp.sum(pieces.astype(F32), axis=0).astype(BF16).reshape(GROUP, rows, shard)
        mine = lax.all_to_all(mine, AXIS, split_axis=0, concat_axis=0, tiled=True, axis_index_groups=token_groups)
        return mine.transpose(1, 0, 2).reshape(rows, hidden).astype(F32)

    down_sum = fold_feed(dot(group_upstream, activated, (0, 0)))
    gate_raw = fold_feed(dot(group_tokens, gate_grad, (0, 0)))
    up_raw = fold_feed(dot(group_tokens, up_grad, (0, 0)))
    gain_two_sum = jnp.sum(gate_raw * gate_weight.astype(F32) + up_raw * up_weight.astype(F32), axis=1)

    hidden_grad = upstream + norm_back(weighted_two, hidden_state, scale_two)
    branch_grad = hidden_grad.astype(BF16)
    mixed_grad = dot(branch_grad, weight_out, (1, 0)).astype(BF16).reshape(length, KV, heads_per_key, HD)
    prob_grad = jnp.einsum("qkgd,skd->kgqs", mixed_grad, value_rows, preferred_element_type=F32)
    value_grad = jnp.einsum("kgqs,qkgd->skd", probs_low, mixed_grad, preferred_element_type=F32)
    score_grad = probs * (prob_grad - jnp.sum(probs * prob_grad, axis=-1, keepdims=True))
    score_grad = score_grad.astype(BF16)
    query_grad = jnp.einsum("kgqs,skd->qkgd", score_grad, key_rows, preferred_element_type=F32) * factor
    key_grad = jnp.einsum("kgqs,qkgd->skd", score_grad, queries, preferred_element_type=F32) * factor
    query_low = rotary_back(query_grad.reshape(length, H, HD), cosine_table, sine_table)
    key_low = rotary_back(key_grad, cosine_table, sine_table)
    input_low = jnp.concatenate(
        [query_low.reshape(length, width), key_low.reshape(length, key_width), value_grad.reshape(length, key_width)],
        axis=1,
    ).astype(BF16)
    attention_term = jnp.concatenate(
        [dot(normed_one, input_low, (0, 0)), dot(branch_grad, mixed_heads, (0, 0))], axis=1
    ).astype(BF16)
    attention_sum = lax.psum_scatter(attention_term, AXIS, scatter_dimension=0, tiled=True).astype(F32)
    bias_sum = lax.psum(jnp.sum(input_low, axis=0, dtype=F32), AXIS)
    input_raw = attention_sum[:, :input_width]
    out_sum = attention_sum[:, input_width:]
    input_sum = input_raw * gain_one
    own_weight = jnp.concatenate([query_weight, key_weight, value_weight], axis=1).astype(F32)
    gain_one_sum = jnp.sum(input_raw * own_weight, axis=1)
    weighted_one = dot(input_low, weight_input, (1, 1))
    token_grad = hidden_grad + norm_back(weighted_one, token_float, scale_one)
    query_bias_sum = lax.dynamic_slice(bias_sum, (me * rows,), (rows,))
    value_bias_sum = lax.dynamic_slice(
        bias_sum, (width + key_width + me * value_bias.shape[0],), (value_bias.shape[0],)
    )
    return (
        block_output,
        token_grad.astype(BF16),
        gain_one_sum,
        input_sum[:, :width],
        query_bias_sum,
        input_sum[:, width : width + key_width],
        bias_sum[width : width + key_width],
        input_sum[:, width + key_width :],
        value_bias_sum,
        out_sum,
        gain_two_sum,
        gate_raw * gain_two,
        up_raw * gain_two,
        down_sum,
    )


def mega(rows, plane, *refs):
    (
        x_in, cot_in, aux_in, bias_in, wq_in, wk_in, wv_in, wo_in, wg_in, wu_in, wd_in,
        o1, o2, o3, o4, o5, fo_out, bg_out, tg_out, h_out,
        xs, xh, aux, sa, wgs, wus, w1, w2, w3, w4, w5, g5,
        r1, r2, r3, r4, hn, gb, gt, up, act, pb, rb, rt,
        zb, zr, dh, dz, ob, qr, kr, vr, pr, dob, dq, cos, sin, msk, ba, bp, bgp, bsum,
        lsem, a_s, a_r, p_s, p_r, r_s, r_r, o_s, o_r, t_s, t_r, d_s, d_r, b_s, b_r, e_s, e_r, credit, pair_credit,
    ) = refs
    weights = (w1, w2, w3, w4, w5)
    grads = (w1, w2, w3, w4, g5)
    landing = (r1, r2, r3, r4, r4)
    outs = (o1, o2, o3, o4, o5)
    block, width = x_in.shape
    shard = w3.shape[1]
    half = w2.shape[1]
    heads = half // HD
    strip = width // LINES
    hidden = wg_in.shape[1]
    short = GROUP * shard - hidden
    factor = 1.0 / math.sqrt(HD)

    me = lax.axis_index(AXIS)
    c = lax.rem(me, 2)
    p = lax.rem(lax.div(me, 2), plane)
    z = lax.div(me, 2 * plane)
    f = z * 2 + c
    xbit, ybit = lax.rem(p, 2), lax.div(p, 2)
    px = p + 1 - 2 * xbit
    py = p + 2 - 4 * ybit
    pd = px + 2 - 4 * ybit
    zlow, zhigh = lax.rem(z, 2), lax.div(z, 2)

    def flip(bit, on):
        return bit + on - 2 * bit * on

    def zf(high, low):
        return flip(zhigh, high) * 2 + flip(zlow, low)

    def zj(j):
        if isinstance(j, int):
            return zf(j // 2, j % 2)
        return zf(lax.div(j, 2), lax.rem(j, 2))

    def dev(zz, pp, cc):
        return (zz * plane + pp) * 2 + cc

    sib, xnb, ynb = dev(z, p, 1 - c), dev(z, px, c), dev(z, py, c)

    def unit(zz, pp):
        return pl.ds(pl.multiple_of((zz * plane + pp) * 2 * rows, 16), 2 * rows)

    def piece(zz, pp, cc):
        return pl.ds(pl.multiple_of(((zz * plane + pp) * 2 + cc) * rows, 16), rows)

    def slot(s):
        return pl.ds(pl.multiple_of(s * 2 * rows, 16), 2 * rows)

    def tokens_of(zz, cc):
        return pl.ds(pl.multiple_of((zz * 2 + cc) * block, block), block)

    def chunk_of(zz):
        return pl.ds(pl.multiple_of(zz * 2 * block, 2 * block), 2 * block)

    def remote(src, dst, send, recv, target):
        return pltpu.make_async_remote_copy(
            src_ref=src, dst_ref=dst, send_sem=send, recv_sem=recv,
            device_id=(target,), device_id_type=pl.DeviceIdType.MESH,
        )

    def dot_nn(a, b):
        return lax.dot_general(a, b, (((1,), (0,)), ((), ())), preferred_element_type=F32)

    def dot_nt(a, b):
        return lax.dot_general(a, b, (((1,), (1,)), ((), ())), preferred_element_type=F32)

    def dot_tn(a, b):
        return lax.dot_general(a, b, (((0,), (0,)), ((), ())), preferred_element_type=F32)

    def local(n, src, dst):
        return pltpu.make_async_copy(src, dst, lsem.at[n])

    loads = [local(0, aux_in, aux.at[c]), local(1, x_in, xs.at[c])]
    for side in range(2):
        loads.append(local(2 + side, wq_in.at[:, pl.ds(side * half, half)], sa.at[side, :, pl.ds(0, half)]))
        loads.append(local(4 + side, wk_in.at[:, pl.ds(side * HD, HD)], sa.at[side, :, pl.ds(half, HD)]))
        loads.append(local(6 + side, wv_in.at[:, pl.ds(side * HD, HD)], sa.at[side, :, pl.ds(half + HD, HD)]))
    late = [local(8, wg_in, wgs), local(9, wu_in, wus), local(10, cot_in, gb.at[tokens_of(z, c)])]
    for copy in loads + late:
        copy.start()

    barrier = pltpu.get_barrier_semaphore()
    friends = [dev(zj(j // 2), p, flip(c, j % 2)) for j in range(1, GROUP)] + [xnb, ynb, dev(z, pd, c)]
    for friend in friends:
        pl.semaphore_signal(barrier, inc=1, device_id=(friend,), device_id_type=pl.DeviceIdType.MESH)

    for copy in loads:
        copy.wait()
    row_id = lax.broadcasted_iota(jnp.int32, (block, block), 0)
    lane_id = lax.broadcasted_iota(jnp.int32, (block, block), 1)

    def column(row):
        return jnp.sum(jnp.where(row_id == lane_id, row, 0.0), axis=1, keepdims=True)

    own_aux = aux[c]
    gain_one = column(own_aux[2:3])[:rows]
    gain_two = column(own_aux[3:4])[:rows]
    for side in range(2):
        sa[side] = (sa[side].astype(F32) * gain_one).astype(BF16)
    pl.semaphore_wait(barrier, len(friends))

    def source(k, ff, cc):
        if k == 0:
            return sa.at[cc]
        if k == 1:
            return wo_in.at[:, pl.ds(pl.multiple_of(cc * half, 128), half)]
        start = pl.multiple_of((ff * (shard // 128) - lax.div(ff, GROUP - 1) * (short // 128)) * 128, 128)
        return (wgs, wus, wd_in)[k - 2].at[:, pl.ds(start, shard)]

    def a_copy(k, j):
        zz, cc = zj(j // 2), flip(c, j % 2)
        return remote(
            source(k, zz * 2 + cc, cc), weights[k].at[piece(z, p, c)], a_s.at[k, j], a_r.at[k, j], dev(zz, p, cc)
        )

    def a_own(k):
        return local(11 + k, source(k, f, c), weights[k].at[piece(z, p, c)])

    def a_send(k):
        a_own(k).start()
        for j in range(1, GROUP):
            a_copy(k, j).start()

    def a_wait(k, jz):
        if jz == 0:
            a_own(k).wait()
        else:
            a_copy(k, 2 * jz).wait_recv()
        a_copy(k, 2 * jz + 1).wait_recv()

    def ag_copy(k, s):
        j = s % 4
        if s < 4:
            part, target = unit(zj(j), p), xnb
        elif s < 8:
            part, target = unit(zj(j), p), ynb
        elif j < 2:
            part, target = unit(zj(j), px), ynb
        else:
            part, target = unit(zj(j), py), xnb
        return remote(weights[k].at[part], weights[k].at[part], p_s.at[k, s], p_r.at[k, s], target)

    def ag_send(k):
        for j in range(LINES):
            a_wait(k, j)
            ag_copy(k, j).start()
            ag_copy(k, 4 + j).start()

    def ag_relay(k):
        for j in range(4):
            ag_copy(k, j if j < 2 else 4 + j).wait_recv()
            ag_copy(k, 8 + j).start()

    def ag_finish(k):
        for s in (2, 3, 4, 5, 8, 9, 10, 11):
            ag_copy(k, s).wait_recv()

    def ag_sent(k):
        for s in range(12):
            ag_copy(k, s).wait_send()

    def tok_copy(which, s):
        buf = (hn, gb)[which]
        if s < 3:
            part, target = tokens_of(z, c), dev(zj(s + 1), p, c)
        elif s == 3:
            part, target = tokens_of(z, c), sib
        else:
            part, target = tokens_of(zj(s - 3), c), sib
        return remote(buf.at[part], buf.at[part], t_s.at[which, s], t_r.at[which, s], target)

    def tok_send(which):
        for s in range(4):
            tok_copy(which, s).start()

    def tok_forward(which):
        for s in range(3):
            tok_copy(which, s).wait_recv()
            tok_copy(which, 4 + s).start()

    def tok_finish(which):
        for s in range(3, 7):
            tok_copy(which, s).wait_recv()

    def e_copy(n, src, dst):
        return remote(src, dst, e_s.at[n], e_r.at[n], sib)

    send_aux = e_copy(0, aux.at[c], aux.at[c])
    send_x = e_copy(1, xs.at[c], xs.at[c])
    send_z = e_copy(2, zb.at[1 - c], zr)
    send_dz = e_copy(3, dz.at[pl.ds(pl.multiple_of(c * block, block), block)], dz.at[pl.ds(pl.multiple_of(c * block, block), block)])
    send_u = e_copy(4, zb.at[1 - c], zr)

    def bias_copy(s):
        zz, cc = zj(s // 2), flip(c, s % 2)
        return remote(bias_in.at[cc], ba.at[f], b_s.at[s], b_r.at[s], dev(zz, p, cc))

    def plane_copy(base, n, buf):
        target = dev(z, (px, py, pd)[n], c)
        return remote(buf.at[p], buf.at[p], b_s.at[base + n], b_r.at[base + n], target)

    def bias_out(s):
        zz, cc = zj(s // 2), flip(c, s % 2)
        return remote(bsum, bg_out.at[f], b_s.at[16 + s], b_r.at[16 + s], dev(zz, p, cc))

    send_aux.start()
    send_x.start()
    a_send(0)
    bias_own = local(16, bias_in.at[c], ba.at[f])
    bias_own.start()
    for s in range(1, GROUP):
        bias_copy(s).start()
    a_send(1)

    late[0].wait()
    late[1].wait()
    late[2].wait()
    for ref in (wgs, wus):
        for n in range(0, hidden, 1792):
            cols = pl.ds(n, min(1792, hidden - n))
            ref[:, cols] = (ref[:, cols].astype(F32) * gain_two).astype(BF16)
    live = jnp.where(column(own_aux[1:2]) >= 0.0, 1.0, 0.0)
    gb[tokens_of(z, c)] = (gb[tokens_of(z, c)].astype(F32) * live).astype(BF16)

    ag_send(0)
    a_send(2)

    send_x.wait_recv()
    send_aux.wait_recv()
    lanes = lax.broadcasted_iota(jnp.int32, (1, HD), 1)
    freq_index = jnp.where(lanes < HD // 2, lanes, lanes - HD // 2).astype(F32)
    frequency = jnp.exp(freq_index * (-2.0 * math.log(ROPE_BASE) / HD))
    for b in range(2):
        values = xs[b].astype(F32)
        scale = lax.rsqrt(jnp.mean(values * values, axis=1, keepdims=True) + EPSILON)
        xh[pl.ds(b * block, block)] = (values * scale).astype(BF16)
        info = aux[b]
        angles = column(info[0:1]) * frequency
        cos[b] = jnp.cos(angles)
        sine = jnp.sin(angles)
        sin[b] = jnp.where(lane_id < HD // 2, -sine, sine)
        same = column(info[1:2]) == info[1:2]
        msk[b] = jnp.where(same & (lane_id <= row_id), 1.0, 0.0)

    ag_relay(0)
    for s in range(1, GROUP):
        bias_copy(s).wait_recv()
    bias_own.wait()
    total = ba[0]
    for s in range(1, GROUP):
        total = total + ba[s]
    bp[p] = total
    for n in range(3):
        plane_copy(8, n, bp).start()
    ag_send(1)
    a_send(3)

    for n in range(3):
        plane_copy(8, n, bp).wait_recv()
    bias_row = (bp[0] + bp[1]) + (bp[2] + bp[3])
    ag_finish(0)

    def rope(v, b):
        return v * cos[b] + pltpu.roll(v, HD // 2, 1) * sin[b]

    def rope_back(v, b):
        return v * cos[b] + pltpu.roll(v * sin[b], HD // 2, 1)

    for n in range(heads // 2 + 1):
        cols = pl.ds(n * 2 * HD, 2 * HD)
        out = dot_nn(xh[...], w1[:, cols]) + bias_row[:, n * 2 * HD : (n + 1) * 2 * HD]
        for b in range(2):
            part = out[b * block : (b + 1) * block]
            if n < heads // 2:
                for i in range(2):
                    qr[b, pl.ds((2 * n + i) * block, block)] = rope(part[:, i * HD : (i + 1) * HD], b).astype(BF16)
            else:
                kr[b] = rope(part[:, :HD], b).astype(BF16)
                vr[b] = part[:, HD:].astype(BF16)

    ag_relay(1)
    ag_send(2)
    a_send(4)

    for b in range(2):
        scores = dot_nt(qr[b], kr[b]) * factor
        scores = jnp.where(msk[b][None] > 0.0, scores.reshape(heads, block, block), -jnp.inf)
        weight = jnp.exp(scores - jnp.max(scores, axis=-1, keepdims=True))
        weight = weight / jnp.sum(weight, axis=-1, keepdims=True)
        weight = weight.reshape(heads * block, block)
        pr[b] = weight
        mixed = dot_nn(weight.astype(BF16), vr[b]).astype(BF16)
        for i in range(heads):
            ob[pl.ds(b * block, block), pl.ds(i * HD, HD)] = mixed[i * block : (i + 1) * block]

    ag_finish(1)
    for n in range(0, width, 512):
        part = dot_nt(ob[...], w2[pl.ds(n, 512), :])
        zb[0, :, pl.ds(n, 512)] = part[:block]
        zb[1, :, pl.ds(n, 512)] = part[block:]
    send_z.start()
    ag_relay(2)
    send_z.wait_recv()
    state = xs[c].astype(F32) + zb[c] + zr[...]
    h_out[...] = state
    scale_two = lax.rsqrt(jnp.mean(state * state, axis=1, keepdims=True) + EPSILON)
    hn[tokens_of(z, c)] = (state * scale_two).astype(BF16)
    tok_send(0)
    ag_send(3)
    tok_send(1)
    tok_forward(0)
    ag_relay(3)
    tok_finish(0)
    ag_finish(2)
    ag_finish(3)

    tile = 3 * HD
    last = lax.div(f, GROUP - 1)
    tile_lane = lax.broadcasted_iota(jnp.int32, (1, tile), 1)
    keep = jnp.where(tile_lane < last * short, 0.0, 1.0)

    @pl.loop(0, LINES)
    def forward_chunk(i):
        rows_here = chunk_of(i)
        left = hn[rows_here]
        for n in range(0, shard, tile):
            cols = pl.ds(n, tile)
            gate = dot_nn(left, w3[:, cols])
            lift = dot_nn(left, w4[:, cols])
            if n == 0:
                gate = gate * keep
                lift = lift * keep
            gt[rows_here, cols] = gate.astype(BF16)
            up[rows_here, cols] = lift.astype(BF16)
            act[rows_here, cols] = (gate * jax.nn.sigmoid(gate) * lift).astype(BF16)

    tok_forward(1)
    ag_send(4)
    tok_finish(1)

    def rs_copy(k, s, h):
        ref = grads[k]
        high = (0, 1, 1, 0, 0, 1)[s]
        zz = zf(high, h)
        part = unit(zz, (pd, pd, px, py, px, py)[s])
        place = (0, 2, 6, 8, 4, 10)[s] + h
        target = (ynb, xnb, xnb, ynb, xnb, ynb)[s]
        return remote(ref.at[part], landing[k].at[slot(place)], r_s.at[k, place], r_r.at[k, place], target)

    def rs_start(k, left_ref, right_ref):
        @pl.loop(0, 2)
        def both(h):
            for high in range(2):
                zz = zf(high, h)
                at = pl.multiple_of(zz * strip, 128)
                left = left_ref[:, pl.ds(at, strip)]
                grads[k][pl.ds(at, strip), :] = dot_tn(left, right_ref[...]).astype(BF16)
                for s in ((0, 3), (1, 2))[high]:
                    rs_copy(k, s, h).start()

    def rs_middle(k):
        @pl.loop(0, 2)
        def both(h):
            for high in range(2):
                rs_copy(k, high, h).wait_recv()
                part = unit(zf(high, h), (px, py)[high])
                got = landing[k][slot(2 * high + h)]
                grads[k][part] = (grads[k][part].astype(F32) + got.astype(F32)).astype(BF16)
                rs_copy(k, 4 + high, h).start()

    def out_copy(k, j, other):
        zz, cc = zj(j), flip(c, other)
        return remote(
            grads[k].at[piece(zz, p, cc)], outs[k].at[f], o_s.at[k, 2 * j + other], o_r.at[k, 2 * j + other], dev(zz, p, cc)
        )

    def out_own(k):
        return local(17 + k, grads[k].at[piece(z, p, c)], outs[k].at[f])

    def rs_finish(k):
        for j in (3, 2, 1, 0):
            h, high = j % 2, j // 2
            rs_copy(k, (4, 2)[high], h).wait_recv()
            rs_copy(k, (3, 5)[high], h).wait_recv()
            part = unit(zj(j), p)
            got = landing[k][slot(4 + j)].astype(F32) + landing[k][slot(8 + j)].astype(F32)
            grads[k][part] = (grads[k][part].astype(F32) + got).astype(BF16)
            out_copy(k, j, 1).start()
            if j == 0:
                out_own(k).start()
            else:
                out_copy(k, j, 0).start()

    rs_start(4, gb, act)
    ag_relay(4)
    ag_finish(4)

    def pair_copy(which, j):
        return remote(
            pb.at[tokens_of(zj(j), 1 - c)], rb.at[pl.ds(pl.multiple_of(j * block, block), block)],
            d_s.at[which, j], d_r.at[which, j], sib,
        )

    def line_copy(which, j):
        dst = (rt, fo_out)[which]
        return remote(
            pb.at[tokens_of(zj(j), c)], dst.at[j], d_s.at[which, 4 + j], d_r.at[which, 4 + j], dev(zj(j), p, c)
        )

    def pair_add(which, j):
        pair_copy(which, j).wait_recv()
        part = tokens_of(zj(j), c)
        got = rb[pl.ds(pl.multiple_of(j * block, block), block)].astype(F32)
        pb[part] = (pb[part].astype(F32) + got).astype(BF16)

    @pl.loop(0, LINES)
    def backward_chunk(i):
        j = LINES - 1 - i
        rows_here = chunk_of(zj(j))
        left = gb[rows_here]
        for n in range(0, shard, tile):
            cols = pl.ds(n, tile)
            d_act = dot_nn(left, w5[:, cols])
            gate = gt[rows_here, cols].astype(F32)
            lift = up[rows_here, cols].astype(F32)
            sig = jax.nn.sigmoid(gate)
            gt[rows_here, cols] = (d_act * lift * sig * (1.0 + gate * (1.0 - sig))).astype(BF16)
            up[rows_here, cols] = (d_act * gate * sig).astype(BF16)
        for n in range(0, width, 512):
            part = pl.ds(n, 512)
            back = dot_nt(gt[rows_here], w3[part, :]) + dot_nt(up[rows_here], w4[part, :])
            pb[rows_here, part] = back.astype(BF16)
        pair_copy(0, j).start()

        @pl.when(i > 0)
        def _():
            pair_add(0, j + 1)
            line_copy(0, j + 1).start()

    pair_add(0, 0)
    pl.semaphore_signal(pair_credit, inc=1, device_id=(sib,), device_id_type=pl.DeviceIdType.MESH)

    rs_middle(4)
    ag_sent(2)
    rs_start(2, hn, gt)
    rs_finish(4)
    for target in (xnb, ynb):
        pl.semaphore_signal(credit, inc=1, device_id=(target,), device_id_type=pl.DeviceIdType.MESH)
    ag_sent(3)
    pl.semaphore_wait(credit, 2)
    rs_start(3, hn, up)
    rs_middle(2)

    for j in range(1, LINES):
        line_copy(0, j).wait_recv()
    weighted = pb[tokens_of(z, c)].astype(F32)
    for j in range(1, LINES):
        weighted = weighted + rt[j].astype(F32)
    state = h_out[...]
    scale_two = lax.rsqrt(jnp.mean(state * state, axis=1, keepdims=True) + EPSILON)
    spread = jnp.mean(weighted * state, axis=1, keepdims=True)
    grad = gb[tokens_of(z, c)].astype(F32) + scale_two * weighted - state * (scale_two * scale_two * scale_two) * spread
    dh[...] = grad
    dz[pl.ds(pl.multiple_of(c * block, block), block)] = grad.astype(BF16)
    send_dz.start()

    for j in range(LINES):
        pair_copy(0, j).wait_send()
    for j in range(1, LINES):
        line_copy(0, j).wait_send()
    pl.semaphore_wait(pair_credit, 1)

    @pl.loop(0, LINES)
    def output_chunk(i):
        j = LINES - 1 - i
        rows_here = chunk_of(zj(j))
        for n in range(0, width, 512):
            part = pl.ds(n, 512)
            pb[rows_here, part] = dot_nt(act[rows_here], w5[part, :]).astype(BF16)
        pair_copy(1, j).start()

        @pl.when(i > 0)
        def _():
            pair_add(1, j + 1)
            line_copy(1, j + 1).start()

    pair_add(1, 0)
    fo_own = local(22, pb.at[tokens_of(z, c)], fo_out.at[0])
    fo_own.start()
    rs_middle(3)
    rs_finish(2)

    send_dz.wait_recv()
    for n in range(0, heads, 2):
        part = dot_nn(dz[...], w2[:, pl.ds(n * HD, 2 * HD)]).astype(BF16)
        for b in range(2):
            for i in range(2):
                dob[b, pl.ds((n + i) * block, block)] = part[b * block : (b + 1) * block, i * HD : (i + 1) * HD]
    ag_sent(1)
    rs_start(1, dz, ob)
    for b in range(2):
        weight = pr[b]
        d_weight = dot_nt(dob[b], vr[b])
        d_score = weight * (d_weight - jnp.sum(weight * d_weight, axis=-1, keepdims=True))
        d_score = d_score.astype(BF16)
        d_query = dot_nn(d_score, kr[b]) * factor
        here = pl.ds(b * block, block)
        for i in range(heads):
            dq[here, pl.ds(i * HD, HD)] = rope_back(d_query[i * block : (i + 1) * block], b).astype(BF16)
        dq[here, pl.ds(half, HD)] = rope_back(dot_tn(d_score, qr[b]) * factor, b).astype(BF16)
        dq[here, pl.ds(half + HD, HD)] = dot_tn(weight.astype(BF16), dob[b]).astype(BF16)

    rs_middle(1)
    send_z.wait_send()
    for n in range(0, width, 512):
        part = dot_nt(dq[...], w1[pl.ds(n, 512), :])
        zb[0, :, pl.ds(n, 512)] = part[:block]
        zb[1, :, pl.ds(n, 512)] = part[block:]
    send_u.start()
    ag_sent(0)
    rs_start(0, xh, dq)
    bgp[p] = jnp.sum(dq[...].astype(F32), axis=0, keepdims=True)
    for n in range(3):
        plane_copy(11, n, bgp).start()

    send_u.wait_recv()
    weighted = zb[c] + zr[...]
    values = xs[c].astype(F32)
    scale = lax.rsqrt(jnp.mean(values * values, axis=1, keepdims=True) + EPSILON)
    spread = jnp.mean(weighted * values, axis=1, keepdims=True)
    tg_out[...] = (dh[...] + scale * weighted - values * (scale * scale * scale) * spread).astype(BF16)

    for n in range(3):
        plane_copy(11, n, bgp).wait_recv()
    bsum[...] = (bgp[0] + bgp[1]) + (bgp[2] + bgp[3])
    bg_own = local(23, bsum, bg_out.at[f])
    bg_own.start()
    for s in range(1, GROUP):
        bias_out(s).start()
    rs_finish(3)
    rs_finish(1)
    rs_middle(0)
    rs_finish(0)

    for s in range(1, GROUP):
        bias_out(s).wait()
        bias_copy(s).wait_send()
    for n in range(3):
        plane_copy(8, n, bp).wait_send()
        plane_copy(11, n, bgp).wait_send()
    bg_own.wait()
    fo_own.wait()
    for j in range(LINES):
        pair_copy(1, j).wait_send()
    for j in range(1, LINES):
        line_copy(1, j).wait()
    for copy in (send_aux, send_x, send_dz, send_u):
        copy.wait_send()
    for which in range(2):
        for s in range(7):
            tok_copy(which, s).wait_send()
    ag_sent(4)
    for k in range(5):
        out_own(k).wait()
        for j in range(1, GROUP):
            a_copy(k, j).wait_send()
            out_copy(k, j // 2, j % 2).wait()
        for h in range(2):
            for s in range(6):
                rs_copy(k, s, h).wait_send()


def kernel_call(rows, plane, block, width, hidden, aux, bias, tokens, cotangent, *weights):
    half = width // 2
    blocks = hidden // 128
    shard = -(-blocks // GROUP) * 128
    inner = half + 2 * HD
    heads = half // HD
    columns = (inner, half, shard, shard, shard)
    dma = pltpu.SemaphoreType.DMA
    vm = pltpu.VMEM
    group_tokens = GROUP * block
    any_space = pl.BlockSpec(memory_space=pl.ANY)
    vmem_space = pl.BlockSpec(memory_space=pltpu.VMEM)
    out_shape = [jax.ShapeDtypeStruct((GROUP, rows, n), BF16) for n in columns]
    out_shape += [
        jax.ShapeDtypeStruct((LINES, block, width), BF16),
        jax.ShapeDtypeStruct((GROUP, 1, inner), F32),
        jax.ShapeDtypeStruct((block, width), BF16),
        jax.ShapeDtypeStruct((block, width), F32),
    ]
    scratch = [
        vm((2, block, width), BF16), vm((2 * block, width), BF16), vm((2, 8, 128), F32), vm((2, rows, inner), BF16),
        vm((rows, hidden), BF16), vm((rows, hidden), BF16),
    ]
    scratch += [vm((width, n), BF16) for n in columns] + [vm((width, shard), BF16)]
    scratch += [vm((12 * 2 * rows, n), BF16) for n in columns[:4]]
    scratch += [vm((group_tokens, width), BF16)] * 2 + [vm((group_tokens, shard), BF16)] * 3
    scratch += [
        vm((group_tokens, width), BF16), vm((LINES * block, width), BF16), vm((LINES, block, width), BF16),
        vm((2, block, width), F32), vm((block, width), F32), vm((block, width), F32), vm((2 * block, width), BF16),
        vm((2 * block, half), BF16), vm((2, heads * block, HD), BF16), vm((2, block, HD), BF16), vm((2, block, HD), BF16),
        vm((2, heads * block, block), F32), vm((2, heads * block, HD), BF16), vm((2 * block, inner), BF16),
        vm((2, block, HD), F32), vm((2, block, HD), F32), vm((2, block, block), F32),
        vm((GROUP, 1, inner), F32), vm((4, 1, inner), F32), vm((4, 1, inner), F32), vm((1, inner), F32),
    ]
    scratch += [dma((24,))]
    scratch += [dma((5, 8))] * 2 + [dma((5, 12))] * 4 + [dma((5, 8))] * 2 + [dma((2, 8))] * 4 + [dma((24,))] * 2 + [dma((8,))] * 2
    scratch += [pltpu.SemaphoreType.REGULAR] * 2
    return pl.pallas_call(
        functools.partial(mega, rows, plane),
        out_shape=out_shape,
        in_specs=[any_space] * 11,
        out_specs=[any_space] * 7 + [vmem_space] * 2,
        scratch_shapes=scratch,
        compiler_params=pltpu.CompilerParams(
            collective_id=0, has_side_effects=True, vmem_limit_bytes=64 * 2**20 - 2**17
        ),
        name="layer",
    )(tokens, cotangent, aux, bias, *weights)


def kernel_body(
    tokens, segment, position, first_gain, query_weight, query_bias, key_weight, key_bias, value_weight, value_bias,
    out_weight, second_gain, gate_weight, up_weight, down_weight, cotangent,
):
    count = lax.axis_size(AXIS)
    me = lax.axis_index(AXIS)
    plane = count // GROUP
    rows, width = query_weight.shape
    block = tokens.shape[0]
    hidden = gate_weight.shape[1]
    key_width = key_weight.shape[1]
    half = width // 2

    def wide(v):
        return jnp.pad(v.astype(F32), (0, 128 - v.shape[0]))

    aux = jnp.stack([wide(position), wide(segment), wide(first_gain), wide(second_gain)] + [jnp.zeros((128,), F32)] * 4)

    def placed(v):
        full = jnp.zeros((v.shape[0] * count,), F32)
        return lax.dynamic_update_slice(full, v.astype(F32), (me * v.shape[0],)).reshape(2, -1)

    bias = jnp.concatenate([placed(query_bias), placed(key_bias), placed(value_bias)], axis=1)[:, None, :]
    pieces_in, pieces_out, gate_raw, up_raw, down_raw, feed, bias_sum, token_grad, state = kernel_call(
        rows, plane, block, width, hidden, aux, bias, tokens, cotangent,
        query_weight, key_weight, value_weight, out_weight, gate_weight, up_weight, down_weight,
    )
    live_rows = (segment >= 0).astype(F32)[:, None]
    gain_one = first_gain.astype(F32)[:, None]
    gain_two = second_gain.astype(F32)[:, None]
    block_output = (live_rows * (state + jnp.sum(feed.astype(F32), axis=0))).astype(BF16)

    def sides(pieces):
        total = jnp.sum(pieces.astype(F32).reshape(LINES, 2, rows, -1), axis=0)
        return total[0], total[1]

    def join(pieces):
        shard = pieces.shape[2]
        short = GROUP * shard - hidden
        parts = [pieces[i] for i in range(GROUP - 1)] + [pieces[GROUP - 1][:, short:]]
        return jnp.concatenate(parts, axis=1).astype(F32)

    left, right = sides(pieces_in)
    query_raw = jnp.concatenate([left[:, :half], right[:, :half]], axis=1)
    key_raw = jnp.concatenate([left[:, half : half + HD], right[:, half : half + HD]], axis=1)
    value_raw = jnp.concatenate([left[:, half + HD :], right[:, half + HD :]], axis=1)
    gain_one_sum = (
        jnp.sum(query_raw * query_weight.astype(F32), axis=1)
        + jnp.sum(key_raw * key_weight.astype(F32), axis=1)
        + jnp.sum(value_raw * value_weight.astype(F32), axis=1)
    )
    gate_raw, up_raw, down_raw = join(gate_raw), join(up_raw), join(down_raw)
    gain_two_sum = jnp.sum(gate_raw * gate_weight.astype(F32) + up_raw * up_weight.astype(F32), axis=1)
    bias_total = jnp.sum(bias_sum.reshape(LINES, 2, -1), axis=0)
    query_bias_all = bias_total[:, :half].reshape(-1)
    key_bias_all = bias_total[:, half : half + HD].reshape(-1)
    value_bias_all = bias_total[:, half + HD :].reshape(-1)
    return (
        block_output,
        token_grad,
        gain_one_sum,
        query_raw * gain_one,
        lax.dynamic_slice(query_bias_all, (me * rows,), (rows,)),
        key_raw * gain_one,
        key_bias_all,
        value_raw * gain_one,
        lax.dynamic_slice(value_bias_all, (me * value_bias.shape[0],), (value_bias.shape[0],)),
        jnp.concatenate(sides(pieces_out), axis=1),
        gain_two_sum,
        gate_raw * gain_two,
        up_raw * gain_two,
        down_raw,
    )


def layer(*args):
    tokens, query_weight, key_weight, gate_weight = args[0], args[4], args[6], args[12]
    rows, width = query_weight.shape
    fits = (
        lax.axis_size(AXIS) == 4 * GROUP
        and rows % 16 == 0
        and rows * lax.axis_size(AXIS) == width
        and width == H * HD
        and key_weight.shape[1] == KV * HD
        and KV == 2
        and tokens.shape[0] == 128
        and gate_weight.shape[1] % 128 == 0
    )
    return kernel_body(*args) if fits else array_body(*args)


def solution(mesh):
    split = P(AXIS)
    split_rows = P(AXIS, None)
    return jax.shard_map(
        layer,
        mesh=mesh,
        in_specs=(
            split_rows, split, split, split, split_rows, split, split_rows, split,
            split_rows, split, split_rows, split, split_rows, split_rows, split_rows, split_rows,
        ),
        out_specs=(
            split_rows, split_rows, split, split_rows, split, split_rows, P(),
            split_rows, split, split_rows, split, split_rows, split_rows, split_rows,
        ),
        check_vma=False,
    )
```

```python
import functools
import math

import jax
import jax.numpy as jnp
from jax import lax
from jax.experimental import pallas as pl
from jax.experimental.pallas import tpu as pltpu
from jax.sharding import PartitionSpec as P

H = 12
KV = 2
HD = 128
GROUP = 8
LINES = GROUP // 2

EPSILON = 1e-06
ROPE_BASE = 1000000.0
AXIS = "fsdp"
F32 = jnp.float32
BF16 = jnp.bfloat16


def tables(position):
    freq_index = jnp.arange(HD // 2).astype(F32)
    frequency = jnp.exp(freq_index * (-2.0 * math.log(ROPE_BASE) / HD))
    angles = position.astype(F32)[:, None] * frequency[None, :]
    angles = jnp.concatenate([angles, angles], axis=-1)
    return (jnp.cos(angles)[:, None, :], jnp.sin(angles)[:, None, :])


def rotary(values, cosine_table, sine_table):
    middle = values.shape[-1] // 2
    turned = jnp.concatenate([-values[..., middle:], values[..., :middle]], axis=-1)
    return values * cosine_table + turned * sine_table


def rotary_back(gradient, cosine_table, sine_table):
    middle = gradient.shape[-1] // 2
    weighted = gradient * sine_table
    return gradient * cosine_table + jnp.concatenate(
        [weighted[..., middle:], -weighted[..., :middle]], axis=-1
    )


def norm_back(weighted, values, row_scale):
    return row_scale * weighted - values * row_scale**3 * jnp.mean(
        weighted * values, axis=-1, keepdims=True
    )


def dot(left, right, dims):
    return lax.dot_general(left, right, ((dims[:1], dims[1:]), ((), ())), preferred_element_type=F32)


def groups_of(count):
    plane = count // GROUP
    lines = GROUP // 2
    token = [[(z * plane + p) * 2 + c for z in range(lines) for c in range(2)] for p in range(plane)]
    other = [[(z * plane + p) * 2 + c for p in range(plane)] for z in range(lines) for c in range(2)]
    return token, other


def array_body(
    tokens,
    segment,
    position,
    first_gain,
    query_weight,
    query_bias,
    key_weight,
    key_bias,
    value_weight,
    value_bias,
    out_weight,
    second_gain,
    gate_weight,
    up_weight,
    down_weight,
    cotangent,
):
    count = lax.axis_size(AXIS)
    me = lax.axis_index(AXIS)
    token_groups, plane_groups = groups_of(count)
    plane = count // GROUP
    lines = GROUP // 2
    rows, width = query_weight.shape
    hidden = gate_weight.shape[1]
    shard = hidden // GROUP
    key_width = key_weight.shape[1]
    length = tokens.shape[0]
    heads_per_key = H // KV
    factor = 1.0 / math.sqrt(HD)

    gain_one = first_gain.astype(F32)[:, None]
    gain_two = second_gain.astype(F32)[:, None]

    def scaled(weight, gain):
        return (weight.astype(F32) * gain).astype(BF16)

    attention_own = jnp.concatenate(
        [scaled(query_weight, gain_one), scaled(key_weight, gain_one), scaled(value_weight, gain_one), out_weight], axis=1
    )
    attention_all = lax.all_gather(attention_own, AXIS, axis=0, tiled=True)
    input_width = width + 2 * key_width
    weight_input = attention_all[:, :input_width]
    weight_out = attention_all[:, input_width:]
    biases = lax.all_gather(jnp.concatenate([query_bias, key_bias, value_bias]), AXIS, axis=0, tiled=False).astype(F32)
    cut = (rows, rows + key_bias.shape[0])
    bias_input = jnp.concatenate(
        [biases[:, : cut[0]].reshape(-1), biases[:, cut[0] : cut[1]].reshape(-1), biases[:, cut[1] :].reshape(-1)]
    )

    def spread(weight):
        pieces = weight.reshape(rows, GROUP, shard).transpose(1, 0, 2)
        got = lax.all_to_all(pieces, AXIS, split_axis=0, concat_axis=0, tiled=True, axis_index_groups=token_groups)
        full = lax.all_gather(got, AXIS, axis=0, tiled=False, axis_index_groups=plane_groups)
        full = full.reshape(plane, lines, 2, rows, shard).transpose(1, 0, 2, 3, 4)
        return full.reshape(count * rows, shard)

    weight_gate = spread(scaled(gate_weight, gain_two))
    weight_up = spread(scaled(up_weight, gain_two))
    weight_down = spread(down_weight)

    live_rows = (segment >= 0).astype(F32)[:, None]
    slot_order = jnp.arange(length)
    visible = (segment[:, None] == segment[None, :]) & (slot_order[None, :] <= slot_order[:, None])
    cosine_table, sine_table = tables(position)
    token_float = tokens.astype(F32)
    scale_one = lax.rsqrt(jnp.mean(token_float * token_float, axis=-1, keepdims=True) + EPSILON)
    normed_one = (token_float * scale_one).astype(BF16)
    projected = dot(normed_one, weight_input, (1, 0)) + bias_input
    queries = rotary(projected[:, :width].reshape(length, H, HD), cosine_table, sine_table).astype(BF16)
    queries = queries.reshape(length, KV, heads_per_key, HD)
    key_rows = rotary(
        projected[:, width : width + key_width].reshape(length, KV, HD), cosine_table, sine_table
    ).astype(BF16)
    value_rows = projected[:, width + key_width :].astype(BF16).reshape(length, KV, HD)
    scores = jnp.einsum("qkgd,skd->kgqs", queries, key_rows, preferred_element_type=F32) * factor
    probs = jax.nn.softmax(jnp.where(visible, scores, -jnp.inf), axis=-1)
    probs_low = probs.astype(BF16)
    mixed_heads = jnp.einsum("kgqs,skd->qkgd", probs_low, value_rows, preferred_element_type=F32)
    mixed_heads = mixed_heads.reshape(length, H * HD).astype(BF16)
    hidden_state = token_float + dot(mixed_heads, weight_out, (1, 1))
    scale_two = lax.rsqrt(jnp.mean(hidden_state * hidden_state, axis=-1, keepdims=True) + EPSILON)
    normed_two = (hidden_state * scale_two).astype(BF16)
    upstream = cotangent.astype(F32) * live_rows
    group_tokens = lax.all_gather(normed_two, AXIS, axis=0, tiled=True, axis_index_groups=token_groups)
    group_upstream = lax.all_gather(
        upstream.astype(BF16), AXIS, axis=0, tiled=True, axis_index_groups=token_groups
    )

    gate_value = dot(group_tokens, weight_gate, (1, 0))
    up_value = dot(group_tokens, weight_up, (1, 0))
    sigmoid_gate = jax.nn.sigmoid(gate_value)
    activated = (gate_value * sigmoid_gate * up_value).astype(BF16)
    act_grad = dot(group_upstream, weight_down, (1, 0))
    gate_grad = (act_grad * up_value * sigmoid_gate * (1.0 + gate_value * (1.0 - sigmoid_gate))).astype(BF16)
    up_grad = (act_grad * gate_value * sigmoid_gate).astype(BF16)

    def fold_tokens(term):
        return lax.psum_scatter(
            term.astype(BF16), AXIS, scatter_dimension=0, tiled=True, axis_index_groups=token_groups
        ).astype(F32)

    weighted_two = fold_tokens(dot(gate_grad, weight_gate, (1, 1)) + dot(up_grad, weight_up, (1, 1)))
    feed_out = fold_tokens(dot(activated, weight_down, (1, 1)))
    block_output = (live_rows * (hidden_state + feed_out)).astype(BF16)

    def fold_feed(term):
        pieces = term.astype(BF16).reshape(lines, plane, 2, rows, shard).transpose(1, 0, 2, 3, 4)
        pieces = lax.all_to_all(
            pieces.reshape(plane, GROUP * rows, shard), AXIS, split_axis=0, concat_axis=0, tiled=True,
            axis_index_groups=plane_groups,
        )
        mine = jnp.sum(pieces.astype(F32), axis=0).astype(BF16).reshape(GROUP, rows, shard)
        mine = lax.all_to_all(mine, AXIS, split_axis=0, concat_axis=0, tiled=True, axis_index_groups=token_groups)
        return mine.transpose(1, 0, 2).reshape(rows, hidden).astype(F32)

    down_sum = fold_feed(dot(group_upstream, activated, (0, 0)))
    gate_raw = fold_feed(dot(group_tokens, gate_grad, (0, 0)))
    up_raw = fold_feed(dot(group_tokens, up_grad, (0, 0)))
    gain_two_sum = jnp.sum(gate_raw * gate_weight.astype(F32) + up_raw * up_weight.astype(F32), axis=1)

    hidden_grad = upstream + norm_back(weighted_two, hidden_state, scale_two)
    branch_grad = hidden_grad.astype(BF16)
    mixed_grad = dot(branch_grad, weight_out, (1, 0)).astype(BF16).reshape(length, KV, heads_per_key, HD)
    prob_grad = jnp.einsum("qkgd,skd->kgqs", mixed_grad, value_rows, preferred_element_type=F32)
    value_grad = jnp.einsum("kgqs,qkgd->skd", probs_low, mixed_grad, preferred_element_type=F32)
    score_grad = probs * (prob_grad - jnp.sum(probs * prob_grad, axis=-1, keepdims=True))
    score_grad = score_grad.astype(BF16)
    query_grad = jnp.einsum("kgqs,skd->qkgd", score_grad, key_rows, preferred_element_type=F32) * factor
    key_grad = jnp.einsum("kgqs,qkgd->skd", score_grad, queries, preferred_element_type=F32) * factor
    query_low = rotary_back(query_grad.reshape(length, H, HD), cosine_table, sine_table)
    key_low = rotary_back(key_grad, cosine_table, sine_table)
    input_low = jnp.concatenate(
        [query_low.reshape(length, width), key_low.reshape(length, key_width), value_grad.reshape(length, key_width)],
        axis=1,
    ).astype(BF16)
    attention_term = jnp.concatenate(
        [dot(normed_one, input_low, (0, 0)), dot(branch_grad, mixed_heads, (0, 0))], axis=1
    ).astype(BF16)
    attention_sum = lax.psum_scatter(attention_term, AXIS, scatter_dimension=0, tiled=True).astype(F32)
    bias_sum = lax.psum(jnp.sum(input_low, axis=0, dtype=F32), AXIS)
    input_raw = attention_sum[:, :input_width]
    out_sum = attention_sum[:, input_width:]
    input_sum = input_raw * gain_one
    own_weight = jnp.concatenate([query_weight, key_weight, value_weight], axis=1).astype(F32)
    gain_one_sum = jnp.sum(input_raw * own_weight, axis=1)
    weighted_one = dot(input_low, weight_input, (1, 1))
    token_grad = hidden_grad + norm_back(weighted_one, token_float, scale_one)
    query_bias_sum = lax.dynamic_slice(bias_sum, (me * rows,), (rows,))
    value_bias_sum = lax.dynamic_slice(
        bias_sum, (width + key_width + me * value_bias.shape[0],), (value_bias.shape[0],)
    )
    return (
        block_output,
        token_grad.astype(BF16),
        gain_one_sum,
        input_sum[:, :width],
        query_bias_sum,
        input_sum[:, width : width + key_width],
        bias_sum[width : width + key_width],
        input_sum[:, width + key_width :],
        value_bias_sum,
        out_sum,
        gain_two_sum,
        gate_raw * gain_two,
        up_raw * gain_two,
        down_sum,
    )


def mega(rows, plane, *refs):
    (
        x_in, cot_in, aux_in, bias_in, wq_in, wk_in, wv_in, wo_in, wg_in, wu_in, wd_in,
        o1, o2, o3, o4, o5, fo_out, bg_out, tg_out, h_out,
        xs, xh, aux, sa, wgs, wus, w1, w2, w3, w4, w5, g5,
        r1, r2, r3, r4, hn, gb, gt, up, act, pb, rb, rt,
        zb, zr, dh, dz, ob, qr, kr, vr, pr, dob, dq, cos, sin, msk, ba, bp, bgp, bsum,
        lsem, a_s, a_r, p_s, p_r, r_s, r_r, o_s, o_r, t_s, t_r, d_s, d_r, b_s, b_r, e_s, e_r, credit, pair_credit, line_credit,
    ) = refs
    weights = (w1, w2, w3, w4, w5)
    grads = (w1, w2, w3, w4, g5)
    landing = (r1, r2, r3, r4, r4)
    outs = (o1, o2, o3, o4, o5)
    block, width = x_in.shape
    shard = w3.shape[1]
    half = w2.shape[1]
    heads = half // HD
    strip = width // LINES
    hidden = wg_in.shape[1]
    short = GROUP * shard - hidden
    factor = 1.0 / math.sqrt(HD)

    me = lax.axis_index(AXIS)
    c = lax.rem(me, 2)
    p = lax.rem(lax.div(me, 2), plane)
    z = lax.div(me, 2 * plane)
    f = z * 2 + c
    xbit, ybit = lax.rem(p, 2), lax.div(p, 2)
    px = p + 1 - 2 * xbit
    py = p + 2 - 4 * ybit
    pd = px + 2 - 4 * ybit
    zlow, zhigh = lax.rem(z, 2), lax.div(z, 2)
    inner = zlow + zhigh - 2 * zlow * zhigh

    def flip(bit, on):
        return bit + on - 2 * bit * on

    def zf(high, low):
        return flip(zhigh, high) * 2 + flip(zlow, low)

    def zj(j):
        if isinstance(j, int):
            return zf(j // 2, j % 2)
        return zf(lax.div(j, 2), lax.rem(j, 2))

    def dev(zz, pp, cc):
        return (zz * plane + pp) * 2 + cc

    sib, xnb, ynb = dev(z, p, 1 - c), dev(z, px, c), dev(z, py, c)

    def unit(zz, pp):
        return pl.ds(pl.multiple_of((zz * plane + pp) * 2 * rows, 16), 2 * rows)

    def piece(zz, pp, cc):
        return pl.ds(pl.multiple_of(((zz * plane + pp) * 2 + cc) * rows, 16), rows)

    def slot(s):
        return pl.ds(pl.multiple_of(s * 2 * rows, 16), 2 * rows)

    def tokens_of(zz, cc):
        return pl.ds(pl.multiple_of((zz * 2 + cc) * block, block), block)

    def chunk_of(zz):
        return pl.ds(pl.multiple_of(zz * 2 * block, 2 * block), 2 * block)

    def remote(src, dst, send, recv, target):
        return pltpu.make_async_remote_copy(
            src_ref=src, dst_ref=dst, send_sem=send, recv_sem=recv,
            device_id=(target,), device_id_type=pl.DeviceIdType.MESH,
        )

    def dot_nn(a, b):
        return lax.dot_general(a, b, (((1,), (0,)), ((), ())), preferred_element_type=F32)

    def dot_nt(a, b):
        return lax.dot_general(a, b, (((1,), (1,)), ((), ())), preferred_element_type=F32)

    def dot_tn(a, b):
        return lax.dot_general(a, b, (((0,), (0,)), ((), ())), preferred_element_type=F32)

    pending = {}

    def begin(key, copy, leave=True, arrive=True):
        copy.start()
        if leave:
            pending[key + ("leave",)] = copy.wait_send
        if arrive:
            pending[key + ("arrive",)] = copy.wait_recv

    def begin_local(key, copy):
        copy.start()
        pending[key] = copy.wait

    def settle(*keys):
        for key in keys:
            pending.pop(key)()

    def settle_all(match):
        settle(*[key for key in pending if match(key)])

    def local(n, src, dst):
        return pltpu.make_async_copy(src, dst, lsem.at[n])

    def signal(semaphore, target):
        pl.semaphore_signal(semaphore, inc=1, device_id=(target,), device_id_type=pl.DeviceIdType.MESH)

    def source(k, ff, cc):
        if k == 0:
            return sa.at[cc]
        if k == 1:
            return wo_in.at[:, pl.ds(pl.multiple_of(cc * half, 128), half)]
        start = pl.multiple_of((ff * (shard // 128) - lax.div(ff, GROUP - 1) * (short // 128)) * 128, 128)
        return (wgs, wus, wd_in)[k - 2].at[:, pl.ds(start, shard)]

    def a_copy(k, j):
        zz, cc = zj(j // 2), flip(c, j % 2)
        return remote(
            source(k, zz * 2 + cc, cc), weights[k].at[piece(z, p, c)], a_s.at[k, j], a_r.at[k, j], dev(zz, p, cc)
        )

    def a_send(k):
        begin_local(("a_own", k), local(11 + k, source(k, f, c), weights[k].at[piece(z, p, c)]))
        for j in range(1, GROUP):
            begin(("a", k, j), a_copy(k, j))

    def a_wait(k, jz):
        settle(("a_own", k) if jz == 0 else ("a", k, 2 * jz, "arrive"), ("a", k, 2 * jz + 1, "arrive"))

    def ag_copy(k, s):
        j = s % 4
        if s < 4:
            part, target = unit(zj(j), p), xnb
        elif s < 8:
            part, target = unit(zj(j), p), ynb
        elif j < 2:
            part, target = unit(zj(j), px), ynb
        else:
            part, target = unit(zj(j), py), xnb
        return remote(weights[k].at[part], weights[k].at[part], p_s.at[k, s], p_r.at[k, s], target)

    def ag_send(k):
        for j in range(LINES):
            a_wait(k, j)
            begin(("ag", k, j), ag_copy(k, j))
            begin(("ag", k, 4 + j), ag_copy(k, 4 + j))

    def ag_relay(k):
        for j in range(4):
            settle(("ag", k, j if j < 2 else 4 + j, "arrive"))
            begin(("ag", k, 8 + j), ag_copy(k, 8 + j))

    def ag_finish(k):
        for s in (2, 3, 4, 5, 8, 9, 10, 11):
            settle(("ag", k, s, "arrive"))

    def ag_sent(k):
        settle_all(lambda key: key[:2] == ("ag", k) and key[-1] == "leave")

    def tok_copy(which, kind, j):
        buf = (hn, gb)[which]
        part = tokens_of(zj(0 if kind == "own" else j), c)
        if kind == "own":
            send, recv, target = j, j, dev(zj(j), p, c)
        elif kind == "pair":
            send, recv, target = 4 + j, 4 + j, sib
        else:
            send, recv, target = 6 + j, 5 - j, dev(zj(1), p, c)
        return remote(buf.at[part], buf.at[part], t_s.at[which, send], t_r.at[which, recv], target)

    def tok_send(which):
        begin(("tok", which, 1), tok_copy(which, "own", 1))
        begin(("tok", which, 2), tok_copy(which, "own", 2 + inner))
        pending["tok", which, 3, "arrive"] = lambda: tok_copy(which, "own", 3 - inner).wait_recv()
        begin(("pair", which, 0), tok_copy(which, "pair", 0))

    def tok_forward(which):
        for n, j in ((1, 1), (2, 2 + inner), (3, 3 - inner)):
            settle(("tok", which, n, "arrive"))
            if n > 1:

                @pl.when(inner == 1)
                def _(j=j):
                    tok_copy(which, "pass", j).start()

            begin(("pair", which, n), tok_copy(which, "pair", j))

        def passed():
            @pl.when(inner == 1)
            def _():
                for j in (2, 3):
                    tok_copy(which, "pass", j).wait_send()

        pending["pass", which, "leave"] = passed

    def tok_finish(which):
        for n in range(4):
            settle(("pair", which, n, "arrive"))

    def e_copy(n, src, dst):
        return remote(src, dst, e_s.at[n], e_r.at[n], sib)

    own_rows = pl.ds(pl.multiple_of(c * block, block), block)

    def bias_in_copy(s):
        zz, cc = zj(s // 2), flip(c, s % 2)
        return remote(bias_in.at[cc], ba.at[f], b_s.at[s], b_r.at[s], dev(zz, p, cc))

    def bias_plane_copy(base, n, buf):
        target = dev(z, (px, py, pd)[n], c)
        return remote(buf.at[p], buf.at[p], b_s.at[base + n], b_r.at[base + n], target)

    def bias_out_copy(s):
        zz, cc = zj(s // 2), flip(c, s % 2)
        return remote(bsum, bg_out.at[f], b_s.at[16 + s], b_r.at[16 + s], dev(zz, p, cc))

    def rs_copy(k, s, h):
        ref = grads[k]
        zz = zf((0, 1, 1, 0, 0, 1)[s], h)
        part = unit(zz, (pd, pd, px, py, px, py)[s])
        place = (0, 2, 6, 8, 4, 10)[s] + h
        target = (ynb, xnb, xnb, ynb, xnb, ynb)[s]
        return remote(ref.at[part], landing[k].at[slot(place)], r_s.at[k, place], r_r.at[k, place], target)

    def rs_note(k, kinds):
        for s in kinds:
            for h in range(2):
                pending["rs", k, s, h, "leave"] = lambda s=s, h=h: rs_copy(k, s, h).wait_send()
                pending["rs", k, s, h, "arrive"] = lambda s=s, h=h: rs_copy(k, s, h).wait_recv()

    def rs_start(k, left_ref, right_ref):
        @pl.loop(0, 2)
        def both(i):
            h = 1 - i
            for high in (1, 0):
                zz = zf(high, h)
                at = pl.multiple_of(zz * strip, 128)
                left = left_ref[:, pl.ds(at, strip)]
                grads[k][pl.ds(at, strip), :] = dot_tn(left, right_ref[...]).astype(BF16)
                for s in ((0, 3), (1, 2))[high]:
                    rs_copy(k, s, h).start()

        rs_note(k, (0, 1, 2, 3))

    def rs_middle(k):
        @pl.loop(0, 2)
        def both(i):
            h = 1 - i
            for high in (1, 0):
                rs_copy(k, high, h).wait_recv()
                part = unit(zf(high, h), (px, py)[high])
                got = landing[k][slot(2 * high + h)]
                grads[k][part] = (grads[k][part].astype(F32) + got.astype(F32)).astype(BF16)
                rs_copy(k, 4 + high, h).start()

        for s in (0, 1):
            for h in range(2):
                pending.pop(("rs", k, s, h, "arrive"))
        rs_note(k, (4, 5))

    def out_copy(k, j, other):
        zz, cc = zj(j), flip(c, other)
        return remote(
            grads[k].at[piece(zz, p, cc)], outs[k].at[f], o_s.at[k, 2 * j + other], o_r.at[k, 2 * j + other], dev(zz, p, cc)
        )

    def rs_finish(k):
        for j in (3, 1, 2, 0):
            h, high = j % 2, j // 2
            settle(("rs", k, (4, 2)[high], h, "arrive"), ("rs", k, (3, 5)[high], h, "arrive"))
            part = unit(zj(j), p)
            got = landing[k][slot(4 + j)].astype(F32) + landing[k][slot(8 + j)].astype(F32)
            grads[k][part] = (grads[k][part].astype(F32) + got).astype(BF16)
            begin(("out", k, j, 1), out_copy(k, j, 1))
            if j == 0:
                begin_local(("out_own", k), local(17 + k, grads[k].at[piece(z, p, c)], outs[k].at[f]))
            else:
                begin(("out", k, j, 0), out_copy(k, j, 0))

    def pair_copy(which, j):
        return remote(
            pb.at[tokens_of(zj(j), 1 - c)], rb.at[pl.ds(pl.multiple_of(j * block, block), block)],
            d_s.at[which, j], d_r.at[which, j], sib,
        )

    def line_copy(which, j):
        dst = fo_out.at[1] if which == 1 and isinstance(j, int) and j == 1 else rt.at[j - 1]
        return remote(
            pb.at[tokens_of(zj(j), c)], dst, d_s.at[which, 4 + j], d_r.at[which, 4 + j], dev(zj(1), p, c)
        )

    def far_copy(which, j):
        dst = fo_out.at[2] if which == 1 else rt.at[3]
        return remote(pb.at[tokens_of(zj(j), c)], dst, d_s.at[which, 6 + j], d_r.at[which, 4], dev(zj(j), p, c))

    def far_add(which, j):
        @pl.when(inner == 1)
        def _():
            line_copy(which, 5 - j).wait_recv()
            part = tokens_of(zj(j), c)
            pb[part] = (pb[part].astype(F32) + rt[4 - j].astype(F32)).astype(BF16)
            far_copy(which, j).start()

    def pair_add(which, j):
        pair_copy(which, j).wait_recv()
        part = tokens_of(zj(j), c)
        got = rb[pl.ds(pl.multiple_of(j * block, block), block)].astype(F32)
        pb[part] = (pb[part].astype(F32) + got).astype(BF16)

    def sum_loop(which, compute):
        @pl.loop(0, LINES)
        def chunk(i):
            j = LINES - 1 - i
            compute(chunk_of(zj(j)))
            pair_copy(which, j).start()

            @pl.when((i > 0) & (i < LINES - 1))
            def _():
                pair_add(which, j + 1)

                @pl.when(inner == 0)
                def _():
                    line_copy(which, j + 1).start()

            @pl.when(i == LINES - 1)
            def _():
                pair_add(which, 1)
                line_copy(which, 1).start()

        pair_add(which, 0)

        def sent():
            for j in range(LINES):
                pair_copy(which, j).wait_send()
            line_copy(which, 1).wait_send()
            for j in (2, 3):
                @pl.when(inner == 0)
                def _():
                    line_copy(which, j).wait_send()

                @pl.when(inner == 1)
                def _():
                    far_copy(which, j).wait_send()

        pending["sum", which, "leave"] = sent
        pending["sum", which, 1, "arrive"] = lambda: line_copy(which, 1).wait_recv()
        pending["sum", which, 2, "arrive"] = lambda: far_copy(which, 2).wait_recv()

    def rope(v, b):
        return v * cos[b] + pltpu.roll(v, HD // 2, 1) * sin[b]

    def rope_back(v, b):
        return v * cos[b] + pltpu.roll(v * sin[b], HD // 2, 1)

    row_id = lax.broadcasted_iota(jnp.int32, (block, block), 0)
    lane_id = lax.broadcasted_iota(jnp.int32, (block, block), 1)

    def column(row):
        return jnp.sum(jnp.where(row_id == lane_id, row, 0.0), axis=1, keepdims=True)

    tile = 3 * HD
    last = lax.div(f, GROUP - 1)
    keep = jnp.where(lax.broadcasted_iota(jnp.int32, (1, tile), 1) < last * short, 0.0, 1.0)

    def enter():
        begin_local(("aux",), local(0, aux_in, aux.at[c]))
        begin_local(("x",), local(1, x_in, xs.at[c]))
        for side in range(2):
            begin_local(("wq", side), local(2 + side, wq_in.at[:, pl.ds(side * half, half)], sa.at[side, :, pl.ds(0, half)]))
            begin_local(("wk", side), local(4 + side, wk_in.at[:, pl.ds(side * HD, HD)], sa.at[side, :, pl.ds(half, HD)]))
            begin_local(("wv", side), local(6 + side, wv_in.at[:, pl.ds(side * HD, HD)], sa.at[side, :, pl.ds(half + HD, HD)]))
        begin_local(("wg",), local(8, wg_in, wgs))
        begin_local(("wu",), local(9, wu_in, wus))
        begin_local(("cot",), local(10, cot_in, gb.at[tokens_of(z, c)]))
        barrier = pltpu.get_barrier_semaphore()
        friends = [dev(zj(j // 2), p, flip(c, j % 2)) for j in range(1, GROUP)] + [xnb, ynb, dev(z, pd, c)]
        for friend in friends:
            signal(barrier, friend)
        settle(("aux",), ("x",), *[(name, side) for side in range(2) for name in ("wq", "wk", "wv")])
        gain_one = column(aux[c][2:3])[:rows]
        for side in range(2):
            sa[side] = (sa[side].astype(F32) * gain_one).astype(BF16)
        pl.semaphore_wait(barrier, len(friends))

    def exchange_inputs():
        begin(("e", 0), e_copy(0, aux.at[c], aux.at[c]))
        begin(("e", 1), e_copy(1, xs.at[c], xs.at[c]))

    def bias_first():
        begin_local(("bias_own",), local(16, bias_in.at[c], ba.at[f]))
        for s in range(1, GROUP):
            begin(("bias_in", s), bias_in_copy(s))

    def bias_second():
        settle(("bias_own",), *[("bias_in", s, "arrive") for s in range(1, GROUP)])
        total = ba[0]
        for s in range(1, GROUP):
            total = total + ba[s]
        bp[p] = total
        for n in range(3):
            begin(("bias_plane", n), bias_plane_copy(8, n, bp))

    def scale_feed():
        gain_two = column(aux[c][3:4])[:rows]
        for name, ref in (("wg", wgs), ("wu", wus)):
            settle((name,))
            for n in range(0, hidden, 1792):
                cols = pl.ds(n, min(1792, hidden - n))
                ref[:, cols] = (ref[:, cols].astype(F32) * gain_two).astype(BF16)

    def mask_upstream():
        settle(("cot",))
        live = jnp.where(column(aux[c][1:2]) >= 0.0, 1.0, 0.0)
        gb[tokens_of(z, c)] = (gb[tokens_of(z, c)].astype(F32) * live).astype(BF16)

    def norm_tokens():
        settle(("e", 0, "arrive"), ("e", 1, "arrive"))
        lanes = lax.broadcasted_iota(jnp.int32, (1, HD), 1)
        freq_index = jnp.where(lanes < HD // 2, lanes, lanes - HD // 2).astype(F32)
        frequency = jnp.exp(freq_index * (-2.0 * math.log(ROPE_BASE) / HD))
        for b in range(2):
            values = xs[b].astype(F32)
            scale = lax.rsqrt(jnp.mean(values * values, axis=1, keepdims=True) + EPSILON)
            xh[pl.ds(b * block, block)] = (values * scale).astype(BF16)
            info = aux[b]
            angles = column(info[0:1]) * frequency
            cos[b] = jnp.cos(angles)
            sine = jnp.sin(angles)
            sin[b] = jnp.where(lane_id < HD // 2, -sine, sine)
            same = column(info[1:2]) == info[1:2]
            msk[b] = jnp.where(same & (lane_id <= row_id), 1.0, 0.0)

    def project():
        settle(*[("bias_plane", n, "arrive") for n in range(3)])
        bias_row = (bp[0] + bp[1]) + (bp[2] + bp[3])
        for n in range(heads // 2 + 1):
            cols = pl.ds(n * 2 * HD, 2 * HD)
            out = dot_nn(xh[...], w1[:, cols]) + bias_row[:, n * 2 * HD : (n + 1) * 2 * HD]
            for b in range(2):
                part = out[b * block : (b + 1) * block]
                if n < heads // 2:
                    for i in range(2):
                        qr[b, pl.ds((2 * n + i) * block, block)] = rope(part[:, i * HD : (i + 1) * HD], b).astype(BF16)
                else:
                    kr[b] = rope(part[:, :HD], b).astype(BF16)
                    vr[b] = part[:, HD:].astype(BF16)

    def attend():
        for b in range(2):
            scores = dot_nt(qr[b], kr[b]) * factor
            scores = jnp.where(msk[b][None] > 0.0, scores.reshape(heads, block, block), -jnp.inf)
            weight = jnp.exp(scores - jnp.max(scores, axis=-1, keepdims=True))
            weight = weight / jnp.sum(weight, axis=-1, keepdims=True)
            weight = weight.reshape(heads * block, block)
            pr[b] = weight
            mixed = dot_nn(weight.astype(BF16), vr[b]).astype(BF16)
            for i in range(heads):
                ob[pl.ds(b * block, block), pl.ds(i * HD, HD)] = mixed[i * block : (i + 1) * block]

    def attend_out():
        for n in range(0, width, 512):
            part = dot_nt(ob[...], w2[pl.ds(n, 512), :])
            zb[0, :, pl.ds(n, 512)] = part[:block]
            zb[1, :, pl.ds(n, 512)] = part[block:]
        begin(("e", 2), e_copy(2, zb.at[1 - c], zr))

    def hidden_state():
        settle(("e", 2, "arrive"))
        state = xs[c].astype(F32) + zb[c] + zr[...]
        h_out[...] = state
        scale_two = lax.rsqrt(jnp.mean(state * state, axis=1, keepdims=True) + EPSILON)
        hn[tokens_of(z, c)] = (state * scale_two).astype(BF16)

    def feed_forward():
        @pl.loop(0, LINES)
        def chunk(i):
            rows_here = chunk_of(i)
            left = hn[rows_here]
            for n in range(0, shard, tile):
                cols = pl.ds(n, tile)
                gate = dot_nn(left, w3[:, cols])
                lift = dot_nn(left, w4[:, cols])
                if n == 0:
                    gate = gate * keep
                    lift = lift * keep
                gt[rows_here, cols] = gate.astype(BF16)
                up[rows_here, cols] = lift.astype(BF16)
                act[rows_here, cols] = (gate * jax.nn.sigmoid(gate) * lift).astype(BF16)

    def feed_backward():
        def compute(rows_here):
            left = gb[rows_here]
            for n in range(0, shard, tile):
                cols = pl.ds(n, tile)
                d_act = dot_nn(left, w5[:, cols])
                gate = gt[rows_here, cols].astype(F32)
                lift = up[rows_here, cols].astype(F32)
                sig = jax.nn.sigmoid(gate)
                gt[rows_here, cols] = (d_act * lift * sig * (1.0 + gate * (1.0 - sig))).astype(BF16)
                up[rows_here, cols] = (d_act * gate * sig).astype(BF16)
            for n in range(0, width, 512):
                part = pl.ds(n, 512)
                back = dot_nt(gt[rows_here], w3[part, :]) + dot_nt(up[rows_here], w4[part, :])
                pb[rows_here, part] = back.astype(BF16)

        sum_loop(0, compute)
        signal(pair_credit, sib)

    def line_ready():
        @pl.when(inner == 1)
        def _():
            signal(line_credit, dev(zj(1), p, c))

    def feed_output():
        settle(("sum", 0, "leave"))
        pl.semaphore_wait(pair_credit, 1)

        @pl.when(inner == 0)
        def _():
            pl.semaphore_wait(line_credit, 1)

        def compute(rows_here):
            for n in range(0, width, 512):
                part = pl.ds(n, 512)
                pb[rows_here, part] = dot_nt(act[rows_here], w5[part, :]).astype(BF16)

        sum_loop(1, compute)
        begin_local(("fo_own",), local(22, pb.at[tokens_of(z, c)], fo_out.at[0]))

    def landing_free():
        for target in (xnb, ynb):
            signal(credit, target)

    def landing_wait():
        pl.semaphore_wait(credit, 2)

    def hidden_gradient():
        settle(("sum", 0, 1, "arrive"), ("sum", 0, 2, "arrive"))
        weighted = pb[tokens_of(z, c)].astype(F32) + rt[0].astype(F32) + rt[3].astype(F32)
        state = h_out[...]
        scale_two = lax.rsqrt(jnp.mean(state * state, axis=1, keepdims=True) + EPSILON)
        spread = jnp.mean(weighted * state, axis=1, keepdims=True)
        grad = (
            gb[tokens_of(z, c)].astype(F32)
            + scale_two * weighted
            - state * (scale_two * scale_two * scale_two) * spread
        )
        dh[...] = grad
        dz[own_rows] = grad.astype(BF16)
        begin(("e", 3), e_copy(3, dz.at[own_rows], dz.at[own_rows]))

    def attend_out_back():
        settle(("e", 3, "arrive"))
        for n in range(0, heads, 2):
            part = dot_nn(dz[...], w2[:, pl.ds(n * HD, 2 * HD)]).astype(BF16)
            for b in range(2):
                for i in range(2):
                    dob[b, pl.ds((n + i) * block, block)] = part[b * block : (b + 1) * block, i * HD : (i + 1) * HD]

    def attend_back():
        for b in range(2):
            weight = pr[b]
            d_weight = dot_nt(dob[b], vr[b])
            d_score = weight * (d_weight - jnp.sum(weight * d_weight, axis=-1, keepdims=True))
            d_score = d_score.astype(BF16)
            d_query = dot_nn(d_score, kr[b]) * factor
            here = pl.ds(b * block, block)
            for i in range(heads):
                dq[here, pl.ds(i * HD, HD)] = rope_back(d_query[i * block : (i + 1) * block], b).astype(BF16)
            dq[here, pl.ds(half, HD)] = rope_back(dot_tn(d_score, qr[b]) * factor, b).astype(BF16)
            dq[here, pl.ds(half + HD, HD)] = dot_tn(weight.astype(BF16), dob[b]).astype(BF16)

    def project_back():
        settle(("e", 2, "leave"))
        for n in range(0, width, 512):
            part = dot_nt(dq[...], w1[pl.ds(n, 512), :])
            zb[0, :, pl.ds(n, 512)] = part[:block]
            zb[1, :, pl.ds(n, 512)] = part[block:]
        begin(("e", 4), e_copy(4, zb.at[1 - c], zr))

    def bias_back():
        bgp[p] = jnp.sum(dq[...].astype(F32), axis=0, keepdims=True)
        for n in range(3):
            begin(("bias_back", n), bias_plane_copy(11, n, bgp))

    def bias_last():
        settle(*[("bias_back", n, "arrive") for n in range(3)])
        bsum[...] = (bgp[0] + bgp[1]) + (bgp[2] + bgp[3])
        begin_local(("bias_sum",), local(23, bsum, bg_out.at[f]))
        for s in range(1, GROUP):
            begin(("bias_out", s), bias_out_copy(s))

    def token_gradient():
        settle(("e", 4, "arrive"))
        weighted = zb[c] + zr[...]
        values = xs[c].astype(F32)
        scale = lax.rsqrt(jnp.mean(values * values, axis=1, keepdims=True) + EPSILON)
        spread = jnp.mean(weighted * values, axis=1, keepdims=True)
        tg_out[...] = (dh[...] + scale * weighted - values * (scale * scale * scale) * spread).astype(BF16)

    enter()
    exchange_inputs()
    a_send(0)
    bias_first()
    a_send(1)
    scale_feed()
    mask_upstream()
    ag_send(0)
    a_send(2)
    norm_tokens()
    ag_relay(0)
    bias_second()
    ag_send(1)
    a_send(3)
    ag_finish(0)
    project()
    ag_relay(1)
    ag_send(2)
    attend()
    ag_finish(1)
    attend_out()
    hidden_state()
    tok_send(0)
    ag_send(3)
    a_send(4)
    tok_send(1)
    ag_relay(2)
    ag_relay(3)
    tok_forward(0)
    ag_send(4)
    tok_finish(0)
    ag_finish(2)
    ag_finish(3)
    feed_forward()
    ag_relay(4)
    tok_forward(1)
    ag_finish(4)
    tok_finish(1)
    rs_start(4, gb, act)
    feed_backward()
    far_add(0, 2)
    rs_middle(4)
    ag_sent(2)
    rs_start(2, hn, gt)
    far_add(0, 3)
    line_ready()
    rs_finish(4)
    landing_free()
    ag_sent(3)
    landing_wait()
    rs_start(3, hn, up)
    hidden_gradient()
    rs_middle(2)
    feed_output()
    far_add(1, 2)
    attend_out_back()
    ag_sent(1)
    rs_start(1, dz, ob)
    far_add(1, 3)
    rs_finish(2)
    rs_middle(3)
    attend_back()
    project_back()
    ag_sent(0)
    rs_start(0, xh, dq)
    rs_middle(1)
    rs_finish(3)
    bias_back()
    token_gradient()
    rs_finish(1)
    bias_last()
    rs_middle(0)
    rs_finish(0)
    settle(*list(pending))


def kernel_call(rows, plane, block, width, hidden, aux, bias, tokens, cotangent, *weights):
    half = width // 2
    blocks = hidden // 128
    shard = -(-blocks // GROUP) * 128
    inner = half + 2 * HD
    heads = half // HD
    columns = (inner, half, shard, shard, shard)
    dma = pltpu.SemaphoreType.DMA
    vm = pltpu.VMEM
    group_tokens = GROUP * block
    any_space = pl.BlockSpec(memory_space=pl.ANY)
    vmem_space = pl.BlockSpec(memory_space=pltpu.VMEM)
    out_shape = [jax.ShapeDtypeStruct((GROUP, rows, n), BF16) for n in columns]
    out_shape += [
        jax.ShapeDtypeStruct((3, block, width), BF16),
        jax.ShapeDtypeStruct((GROUP, 1, inner), F32),
        jax.ShapeDtypeStruct((block, width), BF16),
        jax.ShapeDtypeStruct((block, width), F32),
    ]
    scratch = [
        vm((2, block, width), BF16), vm((2 * block, width), BF16), vm((2, 8, 128), F32), vm((2, rows, inner), BF16),
        vm((rows, hidden), BF16), vm((rows, hidden), BF16),
    ]
    scratch += [vm((width, n), BF16) for n in columns] + [vm((width, shard), BF16)]
    scratch += [vm((12 * 2 * rows, n), BF16) for n in columns[:4]]
    scratch += [vm((group_tokens, width), BF16)] * 2 + [vm((group_tokens, shard), BF16)] * 3
    scratch += [
        vm((group_tokens, width), BF16), vm((LINES * block, width), BF16), vm((LINES, block, width), BF16),
        vm((2, block, width), F32), vm((block, width), F32), vm((block, width), F32), vm((2 * block, width), BF16),
        vm((2 * block, half), BF16), vm((2, heads * block, HD), BF16), vm((2, block, HD), BF16), vm((2, block, HD), BF16),
        vm((2, heads * block, block), F32), vm((2, heads * block, HD), BF16), vm((2 * block, inner), BF16),
        vm((2, block, HD), F32), vm((2, block, HD), F32), vm((2, block, block), F32),
        vm((GROUP, 1, inner), F32), vm((4, 1, inner), F32), vm((4, 1, inner), F32), vm((1, inner), F32),
    ]
    scratch += [dma((24,))]
    scratch += [dma((5, 8))] * 2 + [dma((5, 12))] * 4 + [dma((5, 8))] * 2 + [dma((2, 12))] * 4 + [dma((24,))] * 2 + [dma((8,))] * 2
    scratch += [pltpu.SemaphoreType.REGULAR] * 3
    return pl.pallas_call(
        functools.partial(mega, rows, plane),
        out_shape=out_shape,
        in_specs=[any_space] * 11,
        out_specs=[any_space] * 7 + [vmem_space] * 2,
        scratch_shapes=scratch,
        compiler_params=pltpu.CompilerParams(
            collective_id=0, has_side_effects=True, vmem_limit_bytes=64 * 2**20 - 2**17
        ),
        name="layer",
    )(tokens, cotangent, aux, bias, *weights)


def kernel_body(
    tokens, segment, position, first_gain, query_weight, query_bias, key_weight, key_bias, value_weight, value_bias,
    out_weight, second_gain, gate_weight, up_weight, down_weight, cotangent,
):
    count = lax.axis_size(AXIS)
    me = lax.axis_index(AXIS)
    plane = count // GROUP
    rows, width = query_weight.shape
    block = tokens.shape[0]
    hidden = gate_weight.shape[1]
    key_width = key_weight.shape[1]
    half = width // 2

    def wide(v):
        return jnp.pad(v.astype(F32), (0, 128 - v.shape[0]))

    aux = jnp.stack([wide(position), wide(segment), wide(first_gain), wide(second_gain)] + [jnp.zeros((128,), F32)] * 4)

    def placed(v):
        full = jnp.zeros((v.shape[0] * count,), F32)
        return lax.dynamic_update_slice(full, v.astype(F32), (me * v.shape[0],)).reshape(2, -1)

    bias = jnp.concatenate([placed(query_bias), placed(key_bias), placed(value_bias)], axis=1)[:, None, :]
    pieces_in, pieces_out, gate_raw, up_raw, down_raw, feed, bias_sum, token_grad, state = kernel_call(
        rows, plane, block, width, hidden, aux, bias, tokens, cotangent,
        query_weight, key_weight, value_weight, out_weight, gate_weight, up_weight, down_weight,
    )
    live_rows = (segment >= 0).astype(F32)[:, None]
    gain_one = first_gain.astype(F32)[:, None]
    gain_two = second_gain.astype(F32)[:, None]
    block_output = (live_rows * (state + jnp.sum(feed.astype(F32), axis=0))).astype(BF16)

    def sides(pieces):
        total = jnp.sum(pieces.astype(F32).reshape(LINES, 2, rows, -1), axis=0)
        return total[0], total[1]

    def join(pieces):
        shard = pieces.shape[2]
        short = GROUP * shard - hidden
        parts = [pieces[i] for i in range(GROUP - 1)] + [pieces[GROUP - 1][:, short:]]
        return jnp.concatenate(parts, axis=1).astype(F32)

    left, right = sides(pieces_in)
    query_raw = jnp.concatenate([left[:, :half], right[:, :half]], axis=1)
    key_raw = jnp.concatenate([left[:, half : half + HD], right[:, half : half + HD]], axis=1)
    value_raw = jnp.concatenate([left[:, half + HD :], right[:, half + HD :]], axis=1)
    gain_one_sum = (
        jnp.sum(query_raw * query_weight.astype(F32), axis=1)
        + jnp.sum(key_raw * key_weight.astype(F32), axis=1)
        + jnp.sum(value_raw * value_weight.astype(F32), axis=1)
    )
    gate_raw, up_raw, down_raw = join(gate_raw), join(up_raw), join(down_raw)
    gain_two_sum = jnp.sum(gate_raw * gate_weight.astype(F32) + up_raw * up_weight.astype(F32), axis=1)
    bias_total = jnp.sum(bias_sum.reshape(LINES, 2, -1), axis=0)
    query_bias_all = bias_total[:, :half].reshape(-1)
    key_bias_all = bias_total[:, half : half + HD].reshape(-1)
    value_bias_all = bias_total[:, half + HD :].reshape(-1)
    return (
        block_output,
        token_grad,
        gain_one_sum,
        query_raw * gain_one,
        lax.dynamic_slice(query_bias_all, (me * rows,), (rows,)),
        key_raw * gain_one,
        key_bias_all,
        value_raw * gain_one,
        lax.dynamic_slice(value_bias_all, (me * value_bias.shape[0],), (value_bias.shape[0],)),
        jnp.concatenate(sides(pieces_out), axis=1),
        gain_two_sum,
        gate_raw * gain_two,
        up_raw * gain_two,
        down_raw,
    )


def layer(*args):
    tokens, query_weight, key_weight, gate_weight = args[0], args[4], args[6], args[12]
    rows, width = query_weight.shape
    fits = (
        lax.axis_size(AXIS) == 4 * GROUP
        and rows % 16 == 0
        and rows * lax.axis_size(AXIS) == width
        and width == H * HD
        and key_weight.shape[1] == KV * HD
        and KV == 2
        and tokens.shape[0] == 128
        and gate_weight.shape[1] % 128 == 0
    )
    return kernel_body(*args) if fits else array_body(*args)


def solution(mesh):
    split = P(AXIS)
    split_rows = P(AXIS, None)
    return jax.shard_map(
        layer,
        mesh=mesh,
        in_specs=(
            split_rows, split, split, split, split_rows, split, split_rows, split,
            split_rows, split, split_rows, split, split_rows, split_rows, split_rows, split_rows,
        ),
        out_specs=(
            split_rows, split_rows, split, split_rows, split, split_rows, P(),
            split_rows, split, split_rows, split, split_rows, split_rows, split_rows,
        ),
        check_vma=False,
    )
```

```python
import functools
import math

import jax
import jax.numpy as jnp
from jax import lax
from jax.experimental import pallas as pl
from jax.experimental.pallas import tpu as pltpu
from jax.sharding import PartitionSpec as P

H = 12
KV = 2
HD = 128
GROUP = 8
LINES = GROUP // 2
KEYS = H // KV

EPSILON = 1e-06
ROPE_BASE = 1000000.0
AXIS = "fsdp"
F32 = jnp.float32
BF16 = jnp.bfloat16


def tables(position):
    freq_index = jnp.arange(HD // 2).astype(F32)
    frequency = jnp.exp(freq_index * (-2.0 * math.log(ROPE_BASE) / HD))
    angles = position.astype(F32)[:, None] * frequency[None, :]
    angles = jnp.concatenate([angles, angles], axis=-1)
    return (jnp.cos(angles)[:, None, :], jnp.sin(angles)[:, None, :])


def rotary(values, cosine_table, sine_table):
    middle = values.shape[-1] // 2
    turned = jnp.concatenate([-values[..., middle:], values[..., :middle]], axis=-1)
    return values * cosine_table + turned * sine_table


def rotary_back(gradient, cosine_table, sine_table):
    middle = gradient.shape[-1] // 2
    weighted = gradient * sine_table
    return gradient * cosine_table + jnp.concatenate(
        [weighted[..., middle:], -weighted[..., :middle]], axis=-1
    )


def norm_back(weighted, values, row_scale):
    return row_scale * weighted - values * row_scale**3 * jnp.mean(
        weighted * values, axis=-1, keepdims=True
    )


def dot(left, right, dims):
    return lax.dot_general(left, right, ((dims[:1], dims[1:]), ((), ())), preferred_element_type=F32)


def groups_of(count):
    plane = count // GROUP
    lines = GROUP // 2
    token = [[(z * plane + p) * 2 + c for z in range(lines) for c in range(2)] for p in range(plane)]
    other = [[(z * plane + p) * 2 + c for p in range(plane)] for z in range(lines) for c in range(2)]
    return token, other


def array_body(
    tokens,
    segment,
    position,
    first_gain,
    query_weight,
    query_bias,
    key_weight,
    key_bias,
    value_weight,
    value_bias,
    out_weight,
    second_gain,
    gate_weight,
    up_weight,
    down_weight,
    cotangent,
):
    count = lax.axis_size(AXIS)
    me = lax.axis_index(AXIS)
    token_groups, plane_groups = groups_of(count)
    plane = count // GROUP
    lines = GROUP // 2
    rows, width = query_weight.shape
    hidden = gate_weight.shape[1]
    shard = hidden // GROUP
    key_width = key_weight.shape[1]
    length = tokens.shape[0]
    heads_per_key = H // KV
    factor = 1.0 / math.sqrt(HD)

    gain_one = first_gain.astype(F32)[:, None]
    gain_two = second_gain.astype(F32)[:, None]

    def scaled(weight, gain):
        return (weight.astype(F32) * gain).astype(BF16)

    attention_own = jnp.concatenate(
        [scaled(query_weight, gain_one), scaled(key_weight, gain_one), scaled(value_weight, gain_one), out_weight], axis=1
    )
    attention_all = lax.all_gather(attention_own, AXIS, axis=0, tiled=True)
    input_width = width + 2 * key_width
    weight_input = attention_all[:, :input_width]
    weight_out = attention_all[:, input_width:]
    biases = lax.all_gather(jnp.concatenate([query_bias, key_bias, value_bias]), AXIS, axis=0, tiled=False).astype(F32)
    cut = (rows, rows + key_bias.shape[0])
    bias_input = jnp.concatenate(
        [biases[:, : cut[0]].reshape(-1), biases[:, cut[0] : cut[1]].reshape(-1), biases[:, cut[1] :].reshape(-1)]
    )

    def spread(weight):
        pieces = weight.reshape(rows, GROUP, shard).transpose(1, 0, 2)
        got = lax.all_to_all(pieces, AXIS, split_axis=0, concat_axis=0, tiled=True, axis_index_groups=token_groups)
        full = lax.all_gather(got, AXIS, axis=0, tiled=False, axis_index_groups=plane_groups)
        full = full.reshape(plane, lines, 2, rows, shard).transpose(1, 0, 2, 3, 4)
        return full.reshape(count * rows, shard)

    weight_gate = spread(scaled(gate_weight, gain_two))
    weight_up = spread(scaled(up_weight, gain_two))
    weight_down = spread(down_weight)

    live_rows = (segment >= 0).astype(F32)[:, None]
    slot_order = jnp.arange(length)
    visible = (segment[:, None] == segment[None, :]) & (slot_order[None, :] <= slot_order[:, None])
    cosine_table, sine_table = tables(position)
    token_float = tokens.astype(F32)
    scale_one = lax.rsqrt(jnp.mean(token_float * token_float, axis=-1, keepdims=True) + EPSILON)
    normed_one = (token_float * scale_one).astype(BF16)
    projected = dot(normed_one, weight_input, (1, 0)) + bias_input
    queries = rotary(projected[:, :width].reshape(length, H, HD), cosine_table, sine_table).astype(BF16)
    queries = queries.reshape(length, KV, heads_per_key, HD)
    key_rows = rotary(
        projected[:, width : width + key_width].reshape(length, KV, HD), cosine_table, sine_table
    ).astype(BF16)
    value_rows = projected[:, width + key_width :].astype(BF16).reshape(length, KV, HD)
    scores = jnp.einsum("qkgd,skd->kgqs", queries, key_rows, preferred_element_type=F32) * factor
    probs = jax.nn.softmax(jnp.where(visible, scores, -jnp.inf), axis=-1)
    probs_low = probs.astype(BF16)
    mixed_heads = jnp.einsum("kgqs,skd->qkgd", probs_low, value_rows, preferred_element_type=F32)
    mixed_heads = mixed_heads.reshape(length, H * HD).astype(BF16)
    hidden_state = token_float + dot(mixed_heads, weight_out, (1, 1))
    scale_two = lax.rsqrt(jnp.mean(hidden_state * hidden_state, axis=-1, keepdims=True) + EPSILON)
    normed_two = (hidden_state * scale_two).astype(BF16)
    upstream = cotangent.astype(F32) * live_rows
    group_tokens = lax.all_gather(normed_two, AXIS, axis=0, tiled=True, axis_index_groups=token_groups)
    group_upstream = lax.all_gather(
        upstream.astype(BF16), AXIS, axis=0, tiled=True, axis_index_groups=token_groups
    )

    gate_value = dot(group_tokens, weight_gate, (1, 0))
    up_value = dot(group_tokens, weight_up, (1, 0))
    sigmoid_gate = jax.nn.sigmoid(gate_value)
    activated = (gate_value * sigmoid_gate * up_value).astype(BF16)
    act_grad = dot(group_upstream, weight_down, (1, 0))
    gate_grad = (act_grad * up_value * sigmoid_gate * (1.0 + gate_value * (1.0 - sigmoid_gate))).astype(BF16)
    up_grad = (act_grad * gate_value * sigmoid_gate).astype(BF16)

    def fold_tokens(term):
        return lax.psum_scatter(
            term.astype(BF16), AXIS, scatter_dimension=0, tiled=True, axis_index_groups=token_groups
        ).astype(F32)

    weighted_two = fold_tokens(dot(gate_grad, weight_gate, (1, 1)) + dot(up_grad, weight_up, (1, 1)))
    feed_out = fold_tokens(dot(activated, weight_down, (1, 1)))
    block_output = (live_rows * (hidden_state + feed_out)).astype(BF16)

    def fold_feed(term):
        pieces = term.astype(BF16).reshape(lines, plane, 2, rows, shard).transpose(1, 0, 2, 3, 4)
        pieces = lax.all_to_all(
            pieces.reshape(plane, GROUP * rows, shard), AXIS, split_axis=0, concat_axis=0, tiled=True,
            axis_index_groups=plane_groups,
        )
        mine = jnp.sum(pieces.astype(F32), axis=0).astype(BF16).reshape(GROUP, rows, shard)
        mine = lax.all_to_all(mine, AXIS, split_axis=0, concat_axis=0, tiled=True, axis_index_groups=token_groups)
        return mine.transpose(1, 0, 2).reshape(rows, hidden).astype(F32)

    down_sum = fold_feed(dot(group_upstream, activated, (0, 0)))
    gate_raw = fold_feed(dot(group_tokens, gate_grad, (0, 0)))
    up_raw = fold_feed(dot(group_tokens, up_grad, (0, 0)))
    gain_two_sum = jnp.sum(gate_raw * gate_weight.astype(F32) + up_raw * up_weight.astype(F32), axis=1)

    hidden_grad = upstream + norm_back(weighted_two, hidden_state, scale_two)
    branch_grad = hidden_grad.astype(BF16)
    mixed_grad = dot(branch_grad, weight_out, (1, 0)).astype(BF16).reshape(length, KV, heads_per_key, HD)
    prob_grad = jnp.einsum("qkgd,skd->kgqs", mixed_grad, value_rows, preferred_element_type=F32)
    value_grad = jnp.einsum("kgqs,qkgd->skd", probs_low, mixed_grad, preferred_element_type=F32)
    score_grad = probs * (prob_grad - jnp.sum(probs * prob_grad, axis=-1, keepdims=True))
    score_grad = score_grad.astype(BF16)
    query_grad = jnp.einsum("kgqs,skd->qkgd", score_grad, key_rows, preferred_element_type=F32) * factor
    key_grad = jnp.einsum("kgqs,qkgd->skd", score_grad, queries, preferred_element_type=F32) * factor
    query_low = rotary_back(query_grad.reshape(length, H, HD), cosine_table, sine_table)
    key_low = rotary_back(key_grad, cosine_table, sine_table)
    input_low = jnp.concatenate(
        [query_low.reshape(length, width), key_low.reshape(length, key_width), value_grad.reshape(length, key_width)],
        axis=1,
    ).astype(BF16)
    attention_term = jnp.concatenate(
        [dot(normed_one, input_low, (0, 0)), dot(branch_grad, mixed_heads, (0, 0))], axis=1
    ).astype(BF16)
    attention_sum = lax.psum_scatter(attention_term, AXIS, scatter_dimension=0, tiled=True).astype(F32)
    bias_sum = lax.psum(jnp.sum(input_low, axis=0, dtype=F32), AXIS)
    input_raw = attention_sum[:, :input_width]
    out_sum = attention_sum[:, input_width:]
    input_sum = input_raw * gain_one
    own_weight = jnp.concatenate([query_weight, key_weight, value_weight], axis=1).astype(F32)
    gain_one_sum = jnp.sum(input_raw * own_weight, axis=1)
    weighted_one = dot(input_low, weight_input, (1, 1))
    token_grad = hidden_grad + norm_back(weighted_one, token_float, scale_one)
    query_bias_sum = lax.dynamic_slice(bias_sum, (me * rows,), (rows,))
    value_bias_sum = lax.dynamic_slice(
        bias_sum, (width + key_width + me * value_bias.shape[0],), (value_bias.shape[0],)
    )
    return (
        block_output,
        token_grad.astype(BF16),
        gain_one_sum,
        input_sum[:, :width],
        query_bias_sum,
        input_sum[:, width : width + key_width],
        bias_sum[width : width + key_width],
        input_sum[:, width + key_width :],
        value_bias_sum,
        out_sum,
        gain_two_sum,
        gate_raw * gain_two,
        up_raw * gain_two,
        down_sum,
    )


def mega(rows, plane, *refs):
    (
        x_in, cot_in, pos_in, seg_in, aux_in, wq_in, wk_in, wv_in, wo_in, wg_in, wu_in, wd_in,
        o1, o2, o3, o4, o5, fo_out, bg_out, tg_out, bo_out,
        xs, xh, aux, ids, sa, wgs, wus, w1, w2, w3, w4, w5, g5,
        r1, r2, r3, r4, hn, gb, gt, up, act, pb, rb, rt,
        zb, zr, dh, hs, dz, ob, qr, kr, vr, pr, dob, dq, cos, sin, msk, bias_in, ba, bp, bgp, bsum,
        lsem, a_s, a_r, p_s, p_r, r_s, r_r, o_s, o_r, t_s, t_r, d_s, d_r, b_s, b_r, e_s, e_r, credit, pair_credit, line_credit,
    ) = refs
    weights = (w1, w2, w3, w4, w5)
    block, width = x_in.shape
    shard = w3.shape[1]
    half = w2.shape[1]
    heads = half // HD
    every = pl.ds(0, shard)
    parts = (
        (w1, pl.ds(0, 512), r1, o1), (w2, pl.ds(0, half), r2, o2), (w3, every, r3, o3), (w4, every, r4, o4),
        (g5, every, r4, o5), (w1, pl.ds(512, half - 512), r1, o1), (w1, pl.ds(half, 2 * HD), r1, o1),
    )
    strip = width // LINES
    hidden = wg_in.shape[1]
    short = GROUP * shard - hidden
    factor = 1.0 / math.sqrt(HD)

    me = lax.axis_index(AXIS)
    c = lax.rem(me, 2)
    p = lax.rem(lax.div(me, 2), plane)
    z = lax.div(me, 2 * plane)
    f = z * 2 + c
    xbit, ybit = lax.rem(p, 2), lax.div(p, 2)
    px = p + 1 - 2 * xbit
    py = p + 2 - 4 * ybit
    pd = px + 2 - 4 * ybit
    zlow, zhigh = lax.rem(z, 2), lax.div(z, 2)
    inner = zlow + zhigh - 2 * zlow * zhigh

    def flip(bit, on):
        return bit + on - 2 * bit * on

    def zf(high, low):
        return flip(zhigh, high) * 2 + flip(zlow, low)

    def zj(j):
        if isinstance(j, int):
            return zf(j // 2, j % 2)
        return zf(lax.div(j, 2), lax.rem(j, 2))

    def dev(zz, pp, cc):
        return (zz * plane + pp) * 2 + cc

    sib, xnb, ynb = dev(z, p, 1 - c), dev(z, px, c), dev(z, py, c)

    def unit(zz, pp):
        return pl.ds(pl.multiple_of((zz * plane + pp) * 2 * rows, 16), 2 * rows)

    def piece(zz, pp, cc):
        return pl.ds(pl.multiple_of(((zz * plane + pp) * 2 + cc) * rows, 16), rows)

    def slot(s):
        return pl.ds(pl.multiple_of(s * 2 * rows, 16), 2 * rows)

    def tokens_of(zz, cc):
        return pl.ds(pl.multiple_of((zz * 2 + cc) * block, block), block)

    def chunk_of(zz):
        return pl.ds(pl.multiple_of(zz * 2 * block, 2 * block), 2 * block)

    def remote(src, dst, send, recv, target):
        return pltpu.make_async_remote_copy(
            src_ref=src, dst_ref=dst, send_sem=send, recv_sem=recv,
            device_id=(target,), device_id_type=pl.DeviceIdType.MESH,
        )

    def dot_nn(a, b):
        return lax.dot_general(a, b, (((1,), (0,)), ((), ())), preferred_element_type=F32)

    def dot_nt(a, b):
        return lax.dot_general(a, b, (((1,), (1,)), ((), ())), preferred_element_type=F32)

    def dot_tn(a, b):
        return lax.dot_general(a, b, (((0,), (0,)), ((), ())), preferred_element_type=F32)

    pending = {}

    def begin(key, copy, leave=True, arrive=True):
        copy.start()
        if leave:
            pending[key + ("leave",)] = copy.wait_send
        if arrive:
            pending[key + ("arrive",)] = copy.wait_recv

    def left(ref, send):
        remote(ref, ref, send, send, sib).wait_send()

    def landed(ref, recv):
        remote(ref, ref, recv, recv, sib).wait_recv()

    def begin_local(key, copy):
        copy.start()
        pending[key] = copy.wait

    def settle(*keys):
        for key in keys:
            pending.pop(key)()

    def settle_all(match):
        settle(*[key for key in pending if match(key)])

    def local(n, src, dst):
        return pltpu.make_async_copy(src, dst, lsem.at[n])

    def signal(semaphore, target):
        pl.semaphore_signal(semaphore, inc=1, device_id=(target,), device_id_type=pl.DeviceIdType.MESH)

    def source(k, ff, cc):
        if k == 0:
            return sa.at[cc]
        if k == 1:
            return wo_in.at[:, pl.ds(pl.multiple_of(cc * half, 128), half)]
        start = pl.multiple_of((ff * (shard // 128) - lax.div(ff, GROUP - 1) * (short // 128)) * 128, 128)
        return (wgs, wus, wd_in)[k - 2].at[:, pl.ds(start, shard)]

    def a_copy(k, j):
        zz, cc = zj(j // 2 if isinstance(j, int) else lax.div(j, 2)), flip(c, j % 2 if isinstance(j, int) else lax.rem(j, 2))
        return remote(
            source(k, zz * 2 + cc, cc), weights[k].at[piece(z, p, c)], a_s.at[k],
            a_r.at[k, j // 2 if isinstance(j, int) else lax.div(j, 2)], dev(zz, p, cc),
        )

    def a_unit(k, j):
        return weights[k].at[unit(zj(j), p)]

    def a_pass(k, j):
        return remote(a_unit(k, j), a_unit(k, j), a_s.at[5 + k], a_r.at[k, 5 - j], dev(zj(1), p, c))

    def a_pair(k):
        begin_local(("a_own", k), local(11 + k, source(k, f, c), weights[k].at[piece(z, p, c)]))
        a_copy(k, 1).start()

    def a_line(k):
        through = k < 2
        for j in (2, 3):
            a_copy(k, j).start()
        if through:
            for j in (0, 1):
                a_copy(k, 4 + 2 * inner + j).start()
        else:
            for j in (4, 5, 6, 7):
                a_copy(k, j).start()
        pending["a", k, "leave"] = lambda: left(weights[k].at[pl.ds(0, (5 if through else 7) * rows)], a_s.at[k])
        if through:

            def passed():
                @pl.when(inner == 1)
                def _():
                    left(weights[k].at[pl.ds(0, 4 * rows)], a_s.at[5 + k])

            pending["a_pass", k, "leave"] = passed

    def a_wait(k, n):
        if n == 0:
            settle(("a_own", k))
            landed(weights[k].at[piece(z, p, 1 - c)], a_r.at[k, 0])
            return 0
        j = n if k >= 2 or n == 1 else (2 + inner if n == 2 else 3 - inner)
        landed(a_unit(k, j), a_r.at[k, j])
        if k < 2 and n > 1:

            @pl.when(inner == 1)
            def _():
                a_pass(k, j).start()

        return j

    def ag_copy(k, s, j):
        if s < 4:
            part, target = unit(zj(j), p), xnb
        elif s < 8:
            part, target = unit(zj(j), p), ynb
        elif s < 10:
            part, target = unit(zj(j), px), ynb
        else:
            part, target = unit(zj(j), py), xnb
        index = s // 4 * 4 + j
        return remote(weights[k].at[part], weights[k].at[part], p_s.at[k], p_r.at[k, index], target)

    def ag_unit(k, n):
        j = a_wait(k, n)
        ag_copy(k, 0, j).start()
        ag_copy(k, 4, j).start()

    def ag_send(k, first=0):
        for n in range(first, LINES):
            ag_unit(k, n)
        pending["ag", k, "leave"] = lambda: left(weights[k].at[pl.ds(0, 24 * rows)], p_s.at[k])

    def ag_relay(k):
        for j in range(4):
            ag_copy(k, 0 if j < 2 else 4, j).wait_recv()
            ag_copy(k, 8 + j, j).start()

    def ag_finish(k):
        for s, j in ((0, 2), (0, 3), (4, 0), (4, 1), (8, 0), (8, 1), (10, 2), (10, 3)):
            ag_copy(k, s, j).wait_recv()

    def ag_sent(k):
        settle(("ag", k, "leave"))
        if k < 2:
            settle(("a_pass", k, "leave"))

    def tok_copy(which, kind, j):
        buf = (hn, gb)[which]
        part = tokens_of(zj(0 if kind == "own" else j), c)
        if kind == "own":
            send, recv, target = t_s.at[which, 0], j, dev(zj(j), p, c)
        elif kind == "pair":
            send, recv, target = t_s.at[which, 0], 4 + j, sib
        else:
            send, recv, target = t_s.at[which, 1], 5 - j, dev(zj(1), p, c)
        return remote(buf.at[part], buf.at[part], send, t_r.at[which, recv], target)

    def tok_send(which):
        tok_copy(which, "own", 1).start()
        tok_copy(which, "own", 2 + inner).start()
        tok_copy(which, "pair", 0).start()

        def sent():
            buf = (hn, gb)[which]
            left(buf.at[pl.ds(0, 6 * block)], t_s.at[which, 0])

            @pl.when(inner == 1)
            def _():
                left(buf.at[pl.ds(0, 2 * block)], t_s.at[which, 1])

        pending["tok", which, "leave"] = sent

    def tok_forward(which):
        for j in (1, 2 + inner, 3 - inner):
            tok_copy(which, "own", j).wait_recv()
            if not isinstance(j, int):

                @pl.when(inner == 1)
                def _():
                    tok_copy(which, "pass", j).start()

            tok_copy(which, "pair", j).start()

    def tok_finish(which):
        for j in range(4):
            tok_copy(which, "pair", j).wait_recv()

    def e_copy(n, src, dst):
        return remote(src, dst, e_s.at[n], e_r.at[n], sib)

    own_rows = pl.ds(pl.multiple_of(c * block, block), block)

    def bias_in_copy(s):
        zz, cc = zj(s // 2), flip(c, s % 2)
        return remote(bias_in.at[cc], ba.at[f], b_s.at[0], b_r.at[0], dev(zz, p, cc))

    def bias_plane_copy(group, n, buf):
        target = dev(z, (px, py, pd)[n], c)
        return remote(buf.at[p], buf.at[p], b_s.at[group], b_r.at[group], target)

    def bias_out_copy(s):
        zz, cc = zj(s // 2), flip(c, s % 2)
        return remote(bsum, bg_out.at[f], b_s.at[3], b_r.at[3], dev(zz, p, cc))

    def bias_note(group, buf, count):
        pending["bias", group, "leave"] = lambda: left(buf.at[pl.ds(0, count)], b_s.at[group])
        pending["bias", group, "arrive"] = lambda: landed(buf.at[pl.ds(0, count)], b_r.at[group])

    def rs_copy(k, s, h):
        ref, cols, land = parts[k][:3]
        zz = zf((0, 1, 1, 0, 0, 1)[s], h)
        part = unit(zz, (pd, pd, px, py, px, py)[s])
        place = (0, 2, 6, 8, 4, 10)[s] + h
        target = (ynb, xnb, xnb, ynb, xnb, ynb)[s]
        return remote(ref.at[part, cols], land.at[slot(place), cols], r_s.at[k], r_r.at[k, place], target)

    def rs_start(k, left_ref, right_ref):
        ref, cols = parts[k][:2]

        @pl.loop(0, 2)
        def both(i):
            h = 1 - i
            for high in (1, 0):
                zz = zf(high, h)
                at = pl.multiple_of(zz * strip, 128)
                ref[pl.ds(at, strip), cols] = dot_tn(left_ref[:, pl.ds(at, strip)], right_ref[:, cols]).astype(BF16)
                for s in ((0, 3), (1, 2))[high]:
                    rs_copy(k, s, h).start()

        pending["rs", k, "leave"] = lambda: left(ref.at[pl.ds(0, 24 * rows), cols], r_s.at[k])

    def rs_middle(k):
        ref, cols, land = parts[k][:3]

        @pl.loop(0, 2)
        def both(i):
            h = 1 - i
            for high in (1, 0):
                rs_copy(k, high, h).wait_recv()
                part = unit(zf(high, h), (px, py)[high])
                got = land[slot(2 * high + h), cols]
                ref[part, cols] = (ref[part, cols].astype(F32) + got.astype(F32)).astype(BF16)
                rs_copy(k, 4 + high, h).start()

    def out_copy(k, j, other):
        ref, cols, _, out = parts[k]
        zz, cc = zj(j), flip(c, other)
        return remote(ref.at[piece(zz, p, cc), cols], out.at[f, :, cols], o_s.at[k], o_r.at[k], dev(zz, p, cc))

    def rs_finish(k):
        ref, cols, land, out = parts[k]
        for j in (3, 1, 2, 0):
            h, high = j % 2, j // 2
            rs_copy(k, (4, 2)[high], h).wait_recv()
            rs_copy(k, (3, 5)[high], h).wait_recv()
            part = unit(zj(j), p)
            got = land[slot(4 + j), cols].astype(F32) + land[slot(8 + j), cols].astype(F32)
            ref[part, cols] = (ref[part, cols].astype(F32) + got).astype(BF16)
            out_copy(k, j, 1).start()
            if j == 0:
                begin_local(("out_own", k), local(17 + k, ref.at[piece(z, p, c), cols], out.at[f, :, cols]))
            else:
                out_copy(k, j, 0).start()
        pending["out", k, "leave"] = lambda: left(ref.at[pl.ds(0, 7 * rows), cols], o_s.at[k])
        pending["out", k, "arrive"] = lambda: landed(ref.at[pl.ds(0, 7 * rows), cols], o_r.at[k])

    def pair_copy(which, j):
        return remote(
            pb.at[tokens_of(zj(j), 1 - c)], rb.at[pl.ds(pl.multiple_of(j * block, block), block)],
            d_s.at[which, 0], d_r.at[which, j], sib,
        )

    def line_copy(which, j):
        dst = fo_out.at[1] if which == 1 and isinstance(j, int) and j == 1 else rt.at[j - 1]
        return remote(
            pb.at[tokens_of(zj(j), c)], dst, d_s.at[which, 1], d_r.at[which, 4 + j], dev(zj(1), p, c)
        )

    def far_copy(which, j):
        dst = fo_out.at[2] if which == 1 else rt.at[3]
        return remote(pb.at[tokens_of(zj(j), c)], dst, d_s.at[which, 1], d_r.at[which, 4], dev(zj(j), p, c))

    def far_add(which, j):
        @pl.when(inner == 1)
        def _():
            line_copy(which, 5 - j).wait_recv()
            part = tokens_of(zj(j), c)
            pb[part] = (pb[part].astype(F32) + rt[4 - j].astype(F32)).astype(BF16)
            far_copy(which, j).start()

    def pair_add(which, j):
        pair_copy(which, j).wait_recv()
        part = tokens_of(zj(j), c)
        got = rb[pl.ds(pl.multiple_of(j * block, block), block)].astype(F32)
        pb[part] = (pb[part].astype(F32) + got).astype(BF16)

    def sum_loop(which, compute):
        @pl.loop(0, LINES)
        def chunk(i):
            j = LINES - 1 - i
            compute(chunk_of(zj(j)))
            pair_copy(which, j).start()

            @pl.when((i > 0) & (i < LINES - 1))
            def _():
                pair_add(which, j + 1)

                @pl.when(inner == 0)
                def _():
                    line_copy(which, j + 1).start()

            @pl.when(i == LINES - 1)
            def _():
                pair_add(which, 1)
                line_copy(which, 1).start()

        pair_add(which, 0)

        def sent():
            left(pb.at[pl.ds(0, LINES * block)], d_s.at[which, 0])
            left(pb.at[pl.ds(0, 3 * block)], d_s.at[which, 1])

        pending["sum", which, "leave"] = sent
        pending["sum", which, 1, "arrive"] = lambda: line_copy(which, 1).wait_recv()
        pending["sum", which, 2, "arrive"] = lambda: far_copy(which, 2).wait_recv()

    def rope(v, b):
        return v * cos[b] + pltpu.roll(v, HD // 2, 1) * sin[b]

    def rope_back(v, b):
        return v * cos[b] + pltpu.roll(v * sin[b], HD // 2, 1)

    row_id = lax.broadcasted_iota(jnp.int32, (block, block), 0)
    lane_id = lax.broadcasted_iota(jnp.int32, (block, block), 1)

    def column(row):
        return jnp.sum(jnp.where(row_id == lane_id, row, 0.0), axis=1, keepdims=True)

    tile = 3 * HD
    last = lax.div(f, GROUP - 1)
    keep = jnp.where(lax.broadcasted_iota(jnp.int32, (1, tile), 1) < last * short, 0.0, 1.0)

    def enter():
        begin_local(("aux",), local(0, aux_in, aux.at[c]))
        begin_local(("pos",), local(25, pos_in, ids.at[0]))
        begin_local(("seg",), local(22, seg_in, ids.at[1]))
        begin_local(("x",), local(1, x_in, xs.at[c]))
        for side in range(2):
            begin_local(("wq", side), local(2 + side, wq_in.at[:, pl.ds(side * half, half)], sa.at[side, :, pl.ds(0, half)]))
            begin_local(("wk", side), local(4 + side, wk_in.at[:, pl.ds(side * HD, HD)], sa.at[side, :, pl.ds(half, HD)]))
            begin_local(("wv", side), local(6 + side, wv_in.at[:, pl.ds(side * HD, HD)], sa.at[side, :, pl.ds(half + HD, HD)]))
        begin_local(("wg",), local(8, wg_in, wgs))
        begin_local(("wu",), local(9, wu_in, wus))
        begin_local(("cot",), local(10, cot_in, gb.at[tokens_of(z, c)]))
        barrier = pltpu.get_barrier_semaphore()
        friends = [dev(zj(j // 2), p, flip(c, j % 2)) for j in range(1, GROUP)] + [xnb, ynb, dev(z, pd, c)]
        for friend in friends:
            signal(barrier, friend)
        settle(("aux",), ("pos",), ("seg",), ("x",), *[(name, side) for side in range(2) for name in ("wq", "wk", "wv")])
        aux[c, 0:1] = ids[0].astype(F32)
        aux[c, 1:2] = ids[1].astype(F32)
        gain_one = column(aux[c][2:3])[:rows]
        for side in range(2):
            sa[side] = (sa[side].astype(F32) * gain_one).astype(BF16)
        pl.semaphore_wait(barrier, len(friends))

    def exchange_inputs():
        begin(("e", 0), e_copy(0, aux.at[c], aux.at[c]))
        begin(("e", 1), e_copy(1, xs.at[c], xs.at[c]))

    def bias_first():
        step = lax.rem(me, 2 * plane * LINES // 2)
        info = aux[c]

        def placed(row, count, size):
            wide = jnp.concatenate([row] + [jnp.zeros_like(row)] * (size // HD - 1), axis=1) if size > HD else row
            wide = jnp.broadcast_to(wide, (8, size))
            return pltpu.roll(wide, step * count, 1)[0:1]

        own = jnp.concatenate(
            [placed(info[4:5], rows, half), placed(info[5:6], rows // KEYS, HD), placed(info[6:7], rows // KEYS, HD)], axis=1
        )
        side = lax.div(me, plane * LINES)
        bias_in[side] = own
        bias_in[1 - side] = jnp.zeros_like(own)
        begin_local(("bias_own",), local(16, bias_in.at[c], ba.at[f]))
        for s in range(1, GROUP):
            bias_in_copy(s).start()
        bias_note(0, ba, GROUP - 1)

    def bias_second():
        settle(("bias_own",), ("bias", 0, "arrive"))
        total = ba[0]
        for s in range(1, GROUP):
            total = total + ba[s]
        bp[p] = total
        for n in range(3):
            bias_plane_copy(1, n, bp).start()
        bias_note(1, bp, 3)

    def scale_feed():
        gain_two = column(aux[c][3:4])[:rows]
        for name, ref in (("wg", wgs), ("wu", wus)):
            settle((name,))
            for n in range(0, hidden, 1792):
                cols = pl.ds(n, min(1792, hidden - n))
                ref[:, cols] = (ref[:, cols].astype(F32) * gain_two).astype(BF16)

    def mask_upstream():
        settle(("cot",))
        live = jnp.where(column(aux[c][1:2]) >= 0.0, 1.0, 0.0)
        gb[tokens_of(z, c)] = (gb[tokens_of(z, c)].astype(F32) * live).astype(BF16)

    def norm_tokens():
        settle(("e", 0, "arrive"), ("e", 1, "arrive"))
        lanes = lax.broadcasted_iota(jnp.int32, (1, HD), 1)
        freq_index = jnp.where(lanes < HD // 2, lanes, lanes - HD // 2).astype(F32)
        frequency = jnp.exp(freq_index * (-2.0 * math.log(ROPE_BASE) / HD))
        for b in range(2):
            values = xs[b].astype(F32)
            scale = lax.rsqrt(jnp.mean(values * values, axis=1, keepdims=True) + EPSILON)
            xh[pl.ds(b * block, block)] = (values * scale).astype(BF16)
            info = aux[b]
            angles = column(info[0:1]) * frequency
            cos[b] = jnp.cos(angles)
            sine = jnp.sin(angles)
            sin[b] = jnp.where(lane_id < HD // 2, -sine, sine)
            same = column(info[1:2]) == info[1:2]
            msk[b] = jnp.where(same & (lane_id <= row_id), 1.0, 0.0)

    def project():
        settle(("bias", 1, "arrive"))
        bias_row = (bp[0] + bp[1]) + (bp[2] + bp[3])
        for n in range(heads // 2 + 1):
            cols = pl.ds(n * 2 * HD, 2 * HD)
            out = dot_nn(xh[...], w1[:, cols]) + bias_row[:, n * 2 * HD : (n + 1) * 2 * HD]
            for b in range(2):
                part = out[b * block : (b + 1) * block]
                if n < heads // 2:
                    for i in range(2):
                        qr[b, pl.ds((2 * n + i) * block, block)] = rope(part[:, i * HD : (i + 1) * HD], b).astype(BF16)
                else:
                    kr[b] = rope(part[:, :HD], b).astype(BF16)
                    vr[b] = part[:, HD:].astype(BF16)

    def attend():
        for b in range(2):
            scores = dot_nt(qr[b], kr[b]) * factor
            scores = jnp.where(msk[b][None] > 0.0, scores.reshape(heads, block, block), -jnp.inf)
            weight = jnp.exp(scores - jnp.max(scores, axis=-1, keepdims=True))
            weight = weight / jnp.sum(weight, axis=-1, keepdims=True)
            weight = weight.reshape(heads * block, block)
            pr[b] = weight
            mixed = dot_nn(weight.astype(BF16), vr[b]).astype(BF16)
            for i in range(heads):
                ob[pl.ds(b * block, block), pl.ds(i * HD, HD)] = mixed[i * block : (i + 1) * block]

    def attend_out():
        for n in range(0, width, 512):
            part = dot_nt(ob[...], w2[pl.ds(n, 512), :])
            zb[0, :, pl.ds(n, 512)] = part[:block]
            zb[1, :, pl.ds(n, 512)] = part[block:]
        begin(("e", 2), e_copy(2, zb.at[1 - c], zr))

    def hidden_state():
        settle(("e", 2, "arrive"))
        state = xs[c].astype(F32) + zb[c] + zr[...]
        hs[...] = state
        scale_two = lax.rsqrt(jnp.mean(state * state, axis=1, keepdims=True) + EPSILON)
        hn[tokens_of(z, c)] = (state * scale_two).astype(BF16)

    def feed_forward(first, end):
        @pl.loop(first, end)
        def chunk(i):
            rows_here = chunk_of(zj(i))
            left = hn[rows_here]
            for n in range(0, shard, tile):
                cols = pl.ds(n, tile)
                gate = dot_nn(left, w3[:, cols])
                lift = dot_nn(left, w4[:, cols])
                if n == 0:
                    gate = gate * keep
                    lift = lift * keep
                gt[rows_here, cols] = gate.astype(BF16)
                up[rows_here, cols] = lift.astype(BF16)
                act[rows_here, cols] = (gate * jax.nn.sigmoid(gate) * lift).astype(BF16)

    def feed_backward():
        def compute(rows_here):
            left = gb[rows_here]
            for n in range(0, shard, tile):
                cols = pl.ds(n, tile)
                d_act = dot_nn(left, w5[:, cols])
                gate = gt[rows_here, cols].astype(F32)
                lift = up[rows_here, cols].astype(F32)
                sig = jax.nn.sigmoid(gate)
                gt[rows_here, cols] = (d_act * lift * sig * (1.0 + gate * (1.0 - sig))).astype(BF16)
                up[rows_here, cols] = (d_act * gate * sig).astype(BF16)
            for n in range(0, width, 512):
                part = pl.ds(n, 512)
                back = dot_nt(gt[rows_here], w3[part, :]) + dot_nt(up[rows_here], w4[part, :])
                pb[rows_here, part] = back.astype(BF16)

        sum_loop(0, compute)
        signal(pair_credit, sib)

    def line_ready():
        @pl.when(inner == 1)
        def _():
            signal(line_credit, dev(zj(1), p, c))

    def feed_output():
        settle(("sum", 0, "leave"))
        pl.semaphore_wait(pair_credit, 1)

        @pl.when(inner == 0)
        def _():
            pl.semaphore_wait(line_credit, 1)

        def compute(rows_here):
            for n in range(0, width, 512):
                part = pl.ds(n, 512)
                pb[rows_here, part] = dot_nt(act[rows_here], w5[part, :]).astype(BF16)

        sum_loop(1, compute)

    def block_result():
        settle(("sum", 1, 1, "arrive"), ("sum", 1, 2, "arrive"))
        for n in range(2):
            begin_local(("fetch", n), local(2 + n, fo_out.at[1 + n], rb.at[pl.ds(n * block, block)]))
        settle(("fetch", 0), ("fetch", 1))
        live = jnp.where(column(aux[c][1:2]) >= 0.0, 1.0, 0.0)
        total = hs[...] + pb[tokens_of(z, c)].astype(F32)
        total = total + rb[pl.ds(0, block)].astype(F32) + rb[pl.ds(block, block)].astype(F32)
        bo_out[...] = (live * total).astype(BF16)

    def landing_free():
        for target in (xnb, ynb):
            signal(credit, target)

    def landing_wait():
        pl.semaphore_wait(credit, 2)

    def hidden_gradient():
        settle(("sum", 0, 1, "arrive"), ("sum", 0, 2, "arrive"))
        weighted = pb[tokens_of(z, c)].astype(F32) + rt[0].astype(F32) + rt[3].astype(F32)
        state = hs[...]
        scale_two = lax.rsqrt(jnp.mean(state * state, axis=1, keepdims=True) + EPSILON)
        spread = jnp.mean(weighted * state, axis=1, keepdims=True)
        grad = (
            gb[tokens_of(z, c)].astype(F32)
            + scale_two * weighted
            - state * (scale_two * scale_two * scale_two) * spread
        )
        dh[...] = grad
        dz[own_rows] = grad.astype(BF16)
        begin(("e", 3), e_copy(3, dz.at[own_rows], dz.at[own_rows]))

    def attend_out_back():
        settle(("e", 3, "arrive"))
        for n in range(0, heads, 2):
            part = dot_nn(dz[...], w2[:, pl.ds(n * HD, 2 * HD)]).astype(BF16)
            for b in range(2):
                for i in range(2):
                    dob[b, pl.ds((n + i) * block, block)] = part[b * block : (b + 1) * block, i * HD : (i + 1) * HD]

    def attend_back():
        for b in range(2):
            weight = pr[b]
            d_weight = dot_nt(dob[b], vr[b])
            d_score = weight * (d_weight - jnp.sum(weight * d_weight, axis=-1, keepdims=True))
            d_score = d_score.astype(BF16)
            d_query = dot_nn(d_score, kr[b]) * factor
            here = pl.ds(b * block, block)
            for i in range(heads):
                dq[here, pl.ds(i * HD, HD)] = rope_back(d_query[i * block : (i + 1) * block], b).astype(BF16)
            dq[here, pl.ds(half, HD)] = rope_back(dot_tn(d_score, qr[b]) * factor, b).astype(BF16)
            dq[here, pl.ds(half + HD, HD)] = dot_tn(weight.astype(BF16), dob[b]).astype(BF16)

    def project_back():
        settle(("e", 2, "leave"))
        for n in range(0, width, 512):
            part = dot_nt(dq[...], w1[pl.ds(n, 512), :])
            zb[0, :, pl.ds(n, 512)] = part[:block]
            zb[1, :, pl.ds(n, 512)] = part[block:]
        begin(("e", 4), e_copy(4, zb.at[1 - c], zr))

    def bias_back():
        bgp[p] = jnp.sum(dq[...].astype(F32), axis=0, keepdims=True)
        for n in range(3):
            bias_plane_copy(2, n, bgp).start()
        bias_note(2, bgp, 3)

    def bias_last():
        settle(("bias", 2, "arrive"))
        bsum[...] = (bgp[0] + bgp[1]) + (bgp[2] + bgp[3])
        begin_local(("bias_sum",), local(24, bsum, bg_out.at[f]))
        for s in range(1, GROUP):
            bias_out_copy(s).start()
        bias_note(3, ba, GROUP - 1)

    def token_gradient():
        settle(("e", 4, "arrive"))
        weighted = zb[c] + zr[...]
        values = xs[c].astype(F32)
        scale = lax.rsqrt(jnp.mean(values * values, axis=1, keepdims=True) + EPSILON)
        spread = jnp.mean(weighted * values, axis=1, keepdims=True)
        tg_out[...] = (dh[...] + scale * weighted - values * (scale * scale * scale) * spread).astype(BF16)

    enter()
    exchange_inputs()
    a_pair(0)
    a_line(0)
    bias_first()
    a_pair(1)
    a_line(1)
    ag_unit(0,0)
    a_pair(4)
    scale_feed()
    a_pair(2)
    a_pair(3)
    ag_unit(0,1)
    ag_unit(1,0)
    mask_upstream()
    ag_unit(2,0)
    ag_unit(3,0)
    ag_send(0,2)
    a_line(2)
    norm_tokens()
    ag_relay(0)
    bias_second()
    ag_send(1,1)
    a_line(3)
    ag_finish(0)
    project()
    ag_relay(1)
    ag_send(2,1)
    attend()
    ag_finish(1)
    attend_out()
    hidden_state()
    tok_send(0)
    ag_send(3,1)
    a_line(4)
    tok_send(1)
    ag_relay(2)
    ag_relay(3)
    tok_forward(0)
    ag_send(4, 0)
    tok_finish(0)
    ag_finish(2)
    ag_finish(3)
    feed_forward(0, LINES)
    ag_relay(4)
    tok_forward(1)
    ag_finish(4)
    tok_finish(1)
    rs_start(4, gb, act)
    feed_backward()
    far_add(0, 2)
    rs_middle(4)
    ag_sent(2)
    rs_start(2, hn, gt)
    far_add(0, 3)
    line_ready()
    rs_finish(4)
    landing_free()
    ag_sent(3)
    landing_wait()
    rs_start(3, hn, up)
    hidden_gradient()
    rs_middle(2)
    feed_output()
    far_add(1, 2)
    attend_out_back()
    ag_sent(1)
    rs_start(1, dz, ob)
    far_add(1, 3)
    rs_finish(2)
    rs_middle(3)
    attend_back()
    project_back()
    ag_sent(0)
    rs_start(0, xh, dq)
    rs_start(5, xh, dq)
    rs_start(6, xh, dq)
    rs_finish(3)
    rs_middle(1)
    bias_back()
    token_gradient()
    rs_middle(0)
    rs_finish(1)
    rs_middle(5)
    rs_middle(6)
    bias_last()
    block_result()
    rs_finish(0)
    rs_finish(5)
    rs_finish(6)
    settle(*list(pending))


def kernel_call(rows, plane, block, width, hidden, aux, tokens, cotangent, position, segment, *weights):
    half = width // 2
    blocks = hidden // 128
    shard = -(-blocks // GROUP) * 128
    inner = half + 2 * HD
    heads = half // HD
    columns = (inner, half, shard, shard, shard)
    dma = pltpu.SemaphoreType.DMA
    vm = pltpu.VMEM
    group_tokens = GROUP * block
    any_space = pl.BlockSpec(memory_space=pl.ANY)
    vmem_space = pl.BlockSpec(memory_space=pltpu.VMEM)
    out_shape = [jax.ShapeDtypeStruct((GROUP, rows, n), BF16) for n in columns]
    out_shape += [
        jax.ShapeDtypeStruct((3, block, width), BF16),
        jax.ShapeDtypeStruct((GROUP, 1, inner), F32),
        jax.ShapeDtypeStruct((block, width), BF16),
        jax.ShapeDtypeStruct((block, width), BF16),
    ]
    scratch = [
        vm((2, block, width), BF16), vm((2 * block, width), BF16), vm((2, 8, 128), F32), vm((2, 1, 128), jnp.int32),
        vm((2, rows, inner), BF16),
        vm((rows, hidden), BF16), vm((rows, hidden), BF16),
    ]
    scratch += [vm((width, n), BF16) for n in columns] + [vm((width, shard), BF16)]
    scratch += [vm((12 * 2 * rows, n), BF16) for n in columns[:4]]
    scratch += [vm((group_tokens, width), BF16)] * 2 + [vm((group_tokens, shard), BF16)] * 3
    scratch += [vm((group_tokens, width), BF16), vm((LINES * block, width), BF16), vm((LINES, block, width), BF16)]
    scratch += [
        vm((2, block, width), F32), vm((block, width), F32), vm((block, width), F32), vm((block, width), F32),
        vm((2 * block, width), BF16),
        vm((2 * block, half), BF16), vm((2, heads * block, HD), BF16), vm((2, block, HD), BF16), vm((2, block, HD), BF16),
        vm((2, heads * block, block), F32), vm((2, heads * block, HD), BF16), vm((2 * block, inner), BF16),
        vm((2, block, HD), F32), vm((2, block, HD), F32), vm((2, block, block), F32),
        vm((2, 1, inner), F32), vm((GROUP, 1, inner), F32), vm((4, 1, inner), F32), vm((4, 1, inner), F32), vm((1, inner), F32),
    ]
    scratch += [dma((26,))]
    scratch += [dma((7,)), dma((5, 4)), dma((5,)), dma((5, 12)), dma((7,)), dma((7, 12)), dma((7,)), dma((7,))]
    scratch += [dma((2, 2)), dma((2, 8)), dma((2, 2)), dma((2, 8)), dma((4,)), dma((4,)), dma((5,)), dma((5,))]
    scratch += [pltpu.SemaphoreType.REGULAR] * 3
    return pl.pallas_call(
        functools.partial(mega, rows, plane),
        out_shape=out_shape,
        in_specs=[any_space] * 12,
        out_specs=[any_space] * 7 + [vmem_space] * 2,
        scratch_shapes=scratch,
        compiler_params=pltpu.CompilerParams(
            collective_id=0, has_side_effects=True, vmem_limit_bytes=64 * 2**20 - 2**17
        ),
        name="layer",
    )(tokens, cotangent, position, segment, aux, *weights)


def gather_outputs(rows, plane, hidden, *refs):
    (
        o1, o2, o3, o4, o5, bg, tg, bo, aux, wq, wk, wv, wg, wu,
        bo_out, tg_out, gain_one_out, wq_out, bq_out, wk_out, bk_out, wv_out, bv_out, wo_out, gain_two_out,
        wg_out, wu_out, wd_out, total,
    ) = refs
    step = pl.program_id(0)
    steps = pl.num_programs(0)
    half = wo_out.shape[1] // 2
    shard = o3.shape[2]
    per = o3.shape[0]
    short = GROUP * shard - hidden
    me = lax.axis_index(AXIS)
    row_id = lax.broadcasted_iota(jnp.int32, (128, 128), 0)
    lane_id = lax.broadcasted_iota(jnp.int32, (128, 128), 1)

    def column(row):
        return jnp.sum(jnp.where(row_id == lane_id, row, 0.0), axis=1, keepdims=True)[:rows]

    def as_row(col):
        return jnp.sum(jnp.where(row_id[:rows, :rows] == lane_id[:rows, :rows], col, 0.0), axis=0, keepdims=True)

    gain_one = column(aux[2:3])
    gain_two = column(aux[3:4])

    @pl.when(step == 0)
    def _():
        bo_out[...] = bo[...]
        tg_out[...] = tg[...]
        sums = jnp.zeros((rows, 1), F32)
        for side in range(2):
            part = o1[side].astype(F32)
            for zz in range(1, LINES):
                part = part + o1[2 * zz + side].astype(F32)
            q_part, k_part, v_part = part[:, :half], part[:, half : half + HD], part[:, half + HD :]
            here, keys = pl.ds(side * half, half), pl.ds(side * HD, HD)
            sums = sums + jnp.sum(q_part * wq[:, here].astype(F32), axis=1, keepdims=True)
            sums = sums + jnp.sum(k_part * wk[:, keys].astype(F32), axis=1, keepdims=True)
            sums = sums + jnp.sum(v_part * wv[:, keys].astype(F32), axis=1, keepdims=True)
            wq_out[:, here] = q_part * gain_one
            wk_out[:, keys] = k_part * gain_one
            wv_out[:, keys] = v_part * gain_one
            part = o2[side].astype(F32)
            for zz in range(1, LINES):
                part = part + o2[2 * zz + side].astype(F32)
            wo_out[:, here] = part
        gain_one_out[...] = as_row(sums)
        sides = [(bg[side] + bg[2 + side]) + (bg[4 + side] + bg[6 + side]) for side in range(2)]
        bk_out[:, 0:HD] = sides[0][:, half : half + HD]
        bk_out[:, HD : 2 * HD] = sides[1][:, half : half + HD]
        mine = jnp.where(lax.div(me, plane * LINES) == 0, sides[0], sides[1])
        place = lax.rem(me, plane * LINES)

        def taken(row, count):
            size = row.shape[1]
            wide = jnp.broadcast_to(row, (8, size))
            return pltpu.roll(wide, lax.rem(size - place * count, size), 1)[0:1, :count]

        bq_out[...] = taken(mine[:, :half], rows)
        bv_out[...] = taken(mine[:, half + HD :], rows // KEYS)
        total[...] = jnp.zeros_like(total)

    def put(first):
        sums = jnp.zeros((rows, 1), F32)
        for i in range(per):
            skip = first if i == per - 1 else 0
            cols = pl.ds(i * shard, shard - skip)
            gate = o3[i][:, skip:].astype(F32)
            lift = o4[i][:, skip:].astype(F32)
            sums = sums + jnp.sum(gate * wg[:, cols].astype(F32) + lift * wu[:, cols].astype(F32), axis=1, keepdims=True)
            wg_out[:, cols] = gate * gain_two
            wu_out[:, cols] = lift * gain_two
            wd_out[:, cols] = o5[i][:, skip:].astype(F32)
        total[...] = total[...] + sums

    @pl.when(step < steps - 1)
    def _():
        put(0)

    @pl.when(step == steps - 1)
    def _():
        put(short)
        gain_two_out[...] = as_row(total[...])


def output_call(rows, plane, block, width, hidden, pieces, bias_sum, token_grad, block_output, aux, weights):
    per = 2
    shard = pieces[2].shape[2]
    key_width = weights[1].shape[1]

    def whole(shape):
        return pl.BlockSpec(shape, lambda i: (0,) * len(shape))

    feed = pl.BlockSpec((per, rows, shard), lambda i: (i, 0, 0))
    wide = pl.BlockSpec((rows, per * shard), lambda i: (0, i))
    shapes = [
        ((block, width), BF16), ((block, width), BF16), ((1, rows), F32), ((rows, width), F32), ((1, rows), F32),
        ((rows, key_width), F32), ((1, key_width), F32), ((rows, key_width), F32), ((1, rows // KEYS), F32),
        ((rows, width), F32), ((1, rows), F32),
        ((rows, hidden), F32), ((rows, hidden), F32), ((rows, hidden), F32),
    ]
    return pl.pallas_call(
        functools.partial(gather_outputs, rows, plane, hidden),
        grid=(GROUP // per,),
        out_shape=[jax.ShapeDtypeStruct(*shape) for shape in shapes],
        in_specs=[whole(pieces[0].shape), whole(pieces[1].shape), feed, feed, feed, whole(bias_sum.shape)]
        + [whole((block, width))] * 2 + [whole(aux.shape)]
        + [whole((rows, width)), whole((rows, key_width)), whole((rows, key_width)), wide, wide],
        out_specs=[whole(shape) for shape, _ in shapes[:11]] + [wide] * 3,
        scratch_shapes=[pltpu.VMEM((rows, 1), F32)],
        compiler_params=pltpu.CompilerParams(vmem_limit_bytes=64 * 2**20 - 2**17),
        name="outputs",
    )(*pieces, bias_sum, token_grad, block_output, aux, *weights)


def kernel_body(
    tokens, segment, position, first_gain, query_weight, query_bias, key_weight, key_bias, value_weight, value_bias,
    out_weight, second_gain, gate_weight, up_weight, down_weight, cotangent,
):
    count = lax.axis_size(AXIS)
    plane = count // GROUP
    rows, width = query_weight.shape
    block = tokens.shape[0]
    hidden = gate_weight.shape[1]

    aux = jnp.zeros((1024,), F32)
    for n, vector in enumerate((first_gain, second_gain, query_bias, key_bias, value_bias), 2):
        aux = aux + jnp.pad(vector.astype(F32), (128 * n, 1024 - 128 * n - vector.shape[0]))
    aux = aux.reshape(8, 128)
    *pieces, _, bias_sum, token_grad, block_output = kernel_call(
        rows, plane, block, width, hidden, aux, tokens, cotangent, position[None], segment[None],
        query_weight, key_weight, value_weight, out_weight, gate_weight, up_weight, down_weight,
    )
    outs = output_call(
        rows, plane, block, width, hidden, pieces, bias_sum, token_grad, block_output, aux,
        (query_weight, key_weight, value_weight, gate_weight, up_weight),
    )
    return tuple(out.reshape(-1) if out.shape[0] == 1 else out for out in outs)


def layer(*args):
    tokens, query_weight, key_weight, gate_weight = args[0], args[4], args[6], args[12]
    rows, width = query_weight.shape
    fits = (
        lax.axis_size(AXIS) == 4 * GROUP
        and rows % 16 == 0
        and rows * lax.axis_size(AXIS) == width
        and width == H * HD
        and key_weight.shape[1] == KV * HD
        and KV == 2
        and tokens.shape[0] == 128
        and gate_weight.shape[1] % 128 == 0
    )
    return kernel_body(*args) if fits else array_body(*args)


def solution(mesh):
    split = P(AXIS)
    split_rows = P(AXIS, None)
    return jax.shard_map(
        layer,
        mesh=mesh,
        in_specs=(
            split_rows, split, split, split, split_rows, split, split_rows, split,
            split_rows, split, split_rows, split, split_rows, split_rows, split_rows, split_rows,
        ),
        out_specs=(
            split_rows, split_rows, split, split_rows, split, split_rows, P(),
            split_rows, split, split_rows, split, split_rows, split_rows, split_rows,
        ),
        check_vma=False,
    )
```

```python
import functools
import math

import jax
import jax.numpy as jnp
from jax import lax
from jax.experimental import pallas as pl
from jax.experimental.pallas import tpu as pltpu
from jax.sharding import PartitionSpec as P

H = 12
KV = 2
HD = 128
GROUP = 8
LINES = GROUP // 2
KEYS = H // KV

EPSILON = 1e-06
ROPE_BASE = 1000000.0
AXIS = "fsdp"
F32 = jnp.float32
BF16 = jnp.bfloat16


def tables(position):
    freq_index = jnp.arange(HD // 2).astype(F32)
    frequency = jnp.exp(freq_index * (-2.0 * math.log(ROPE_BASE) / HD))
    angles = position.astype(F32)[:, None] * frequency[None, :]
    angles = jnp.concatenate([angles, angles], axis=-1)
    return (jnp.cos(angles)[:, None, :], jnp.sin(angles)[:, None, :])


def rotary(values, cosine_table, sine_table):
    middle = values.shape[-1] // 2
    turned = jnp.concatenate([-values[..., middle:], values[..., :middle]], axis=-1)
    return values * cosine_table + turned * sine_table


def rotary_back(gradient, cosine_table, sine_table):
    middle = gradient.shape[-1] // 2
    weighted = gradient * sine_table
    return gradient * cosine_table + jnp.concatenate(
        [weighted[..., middle:], -weighted[..., :middle]], axis=-1
    )


def norm_back(weighted, values, row_scale):
    return row_scale * weighted - values * row_scale**3 * jnp.mean(
        weighted * values, axis=-1, keepdims=True
    )


def dot(left, right, dims):
    return lax.dot_general(left, right, ((dims[:1], dims[1:]), ((), ())), preferred_element_type=F32)


def groups_of(count):
    plane = count // GROUP
    lines = GROUP // 2
    token = [[(z * plane + p) * 2 + c for z in range(lines) for c in range(2)] for p in range(plane)]
    other = [[(z * plane + p) * 2 + c for p in range(plane)] for z in range(lines) for c in range(2)]
    return token, other


def array_body(
    tokens,
    segment,
    position,
    first_gain,
    query_weight,
    query_bias,
    key_weight,
    key_bias,
    value_weight,
    value_bias,
    out_weight,
    second_gain,
    gate_weight,
    up_weight,
    down_weight,
    cotangent,
):
    count = lax.axis_size(AXIS)
    me = lax.axis_index(AXIS)
    token_groups, plane_groups = groups_of(count)
    plane = count // GROUP
    lines = GROUP // 2
    rows, width = query_weight.shape
    hidden = gate_weight.shape[1]
    shard = hidden // GROUP
    key_width = key_weight.shape[1]
    length = tokens.shape[0]
    heads_per_key = H // KV
    factor = 1.0 / math.sqrt(HD)

    gain_one = first_gain.astype(F32)[:, None]
    gain_two = second_gain.astype(F32)[:, None]

    def scaled(weight, gain):
        return (weight.astype(F32) * gain).astype(BF16)

    attention_own = jnp.concatenate(
        [scaled(query_weight, gain_one), scaled(key_weight, gain_one), scaled(value_weight, gain_one), out_weight], axis=1
    )
    attention_all = lax.all_gather(attention_own, AXIS, axis=0, tiled=True)
    input_width = width + 2 * key_width
    weight_input = attention_all[:, :input_width]
    weight_out = attention_all[:, input_width:]
    biases = lax.all_gather(jnp.concatenate([query_bias, key_bias, value_bias]), AXIS, axis=0, tiled=False).astype(F32)
    cut = (rows, rows + key_bias.shape[0])
    bias_input = jnp.concatenate(
        [biases[:, : cut[0]].reshape(-1), biases[:, cut[0] : cut[1]].reshape(-1), biases[:, cut[1] :].reshape(-1)]
    )

    def spread(weight):
        pieces = weight.reshape(rows, GROUP, shard).transpose(1, 0, 2)
        got = lax.all_to_all(pieces, AXIS, split_axis=0, concat_axis=0, tiled=True, axis_index_groups=token_groups)
        full = lax.all_gather(got, AXIS, axis=0, tiled=False, axis_index_groups=plane_groups)
        full = full.reshape(plane, lines, 2, rows, shard).transpose(1, 0, 2, 3, 4)
        return full.reshape(count * rows, shard)

    weight_gate = spread(scaled(gate_weight, gain_two))
    weight_up = spread(scaled(up_weight, gain_two))
    weight_down = spread(down_weight)

    live_rows = (segment >= 0).astype(F32)[:, None]
    slot_order = jnp.arange(length)
    visible = (segment[:, None] == segment[None, :]) & (slot_order[None, :] <= slot_order[:, None])
    cosine_table, sine_table = tables(position)
    token_float = tokens.astype(F32)
    scale_one = lax.rsqrt(jnp.mean(token_float * token_float, axis=-1, keepdims=True) + EPSILON)
    normed_one = (token_float * scale_one).astype(BF16)
    projected = dot(normed_one, weight_input, (1, 0)) + bias_input
    queries = rotary(projected[:, :width].reshape(length, H, HD), cosine_table, sine_table).astype(BF16)
    queries = queries.reshape(length, KV, heads_per_key, HD)
    key_rows = rotary(
        projected[:, width : width + key_width].reshape(length, KV, HD), cosine_table, sine_table
    ).astype(BF16)
    value_rows = projected[:, width + key_width :].astype(BF16).reshape(length, KV, HD)
    scores = jnp.einsum("qkgd,skd->kgqs", queries, key_rows, preferred_element_type=F32) * factor
    probs = jax.nn.softmax(jnp.where(visible, scores, -jnp.inf), axis=-1)
    probs_low = probs.astype(BF16)
    mixed_heads = jnp.einsum("kgqs,skd->qkgd", probs_low, value_rows, preferred_element_type=F32)
    mixed_heads = mixed_heads.reshape(length, H * HD).astype(BF16)
    hidden_state = token_float + dot(mixed_heads, weight_out, (1, 1))
    scale_two = lax.rsqrt(jnp.mean(hidden_state * hidden_state, axis=-1, keepdims=True) + EPSILON)
    normed_two = (hidden_state * scale_two).astype(BF16)
    upstream = cotangent.astype(F32) * live_rows
    group_tokens = lax.all_gather(normed_two, AXIS, axis=0, tiled=True, axis_index_groups=token_groups)
    group_upstream = lax.all_gather(
        upstream.astype(BF16), AXIS, axis=0, tiled=True, axis_index_groups=token_groups
    )

    gate_value = dot(group_tokens, weight_gate, (1, 0))
    up_value = dot(group_tokens, weight_up, (1, 0))
    sigmoid_gate = jax.nn.sigmoid(gate_value)
    activated = (gate_value * sigmoid_gate * up_value).astype(BF16)
    act_grad = dot(group_upstream, weight_down, (1, 0))
    gate_grad = (act_grad * up_value * sigmoid_gate * (1.0 + gate_value * (1.0 - sigmoid_gate))).astype(BF16)
    up_grad = (act_grad * gate_value * sigmoid_gate).astype(BF16)

    def fold_tokens(term):
        return lax.psum_scatter(
            term.astype(BF16), AXIS, scatter_dimension=0, tiled=True, axis_index_groups=token_groups
        ).astype(F32)

    weighted_two = fold_tokens(dot(gate_grad, weight_gate, (1, 1)) + dot(up_grad, weight_up, (1, 1)))
    feed_out = fold_tokens(dot(activated, weight_down, (1, 1)))
    block_output = (live_rows * (hidden_state + feed_out)).astype(BF16)

    def fold_feed(term):
        pieces = term.astype(BF16).reshape(lines, plane, 2, rows, shard).transpose(1, 0, 2, 3, 4)
        pieces = lax.all_to_all(
            pieces.reshape(plane, GROUP * rows, shard), AXIS, split_axis=0, concat_axis=0, tiled=True,
            axis_index_groups=plane_groups,
        )
        mine = jnp.sum(pieces.astype(F32), axis=0).astype(BF16).reshape(GROUP, rows, shard)
        mine = lax.all_to_all(mine, AXIS, split_axis=0, concat_axis=0, tiled=True, axis_index_groups=token_groups)
        return mine.transpose(1, 0, 2).reshape(rows, hidden).astype(F32)

    down_sum = fold_feed(dot(group_upstream, activated, (0, 0)))
    gate_raw = fold_feed(dot(group_tokens, gate_grad, (0, 0)))
    up_raw = fold_feed(dot(group_tokens, up_grad, (0, 0)))
    gain_two_sum = jnp.sum(gate_raw * gate_weight.astype(F32) + up_raw * up_weight.astype(F32), axis=1)

    hidden_grad = upstream + norm_back(weighted_two, hidden_state, scale_two)
    branch_grad = hidden_grad.astype(BF16)
    mixed_grad = dot(branch_grad, weight_out, (1, 0)).astype(BF16).reshape(length, KV, heads_per_key, HD)
    prob_grad = jnp.einsum("qkgd,skd->kgqs", mixed_grad, value_rows, preferred_element_type=F32)
    value_grad = jnp.einsum("kgqs,qkgd->skd", probs_low, mixed_grad, preferred_element_type=F32)
    score_grad = probs * (prob_grad - jnp.sum(probs * prob_grad, axis=-1, keepdims=True))
    score_grad = score_grad.astype(BF16)
    query_grad = jnp.einsum("kgqs,skd->qkgd", score_grad, key_rows, preferred_element_type=F32) * factor
    key_grad = jnp.einsum("kgqs,qkgd->skd", score_grad, queries, preferred_element_type=F32) * factor
    query_low = rotary_back(query_grad.reshape(length, H, HD), cosine_table, sine_table)
    key_low = rotary_back(key_grad, cosine_table, sine_table)
    input_low = jnp.concatenate(
        [query_low.reshape(length, width), key_low.reshape(length, key_width), value_grad.reshape(length, key_width)],
        axis=1,
    ).astype(BF16)
    attention_term = jnp.concatenate(
        [dot(normed_one, input_low, (0, 0)), dot(branch_grad, mixed_heads, (0, 0))], axis=1
    ).astype(BF16)
    attention_sum = lax.psum_scatter(attention_term, AXIS, scatter_dimension=0, tiled=True).astype(F32)
    bias_sum = lax.psum(jnp.sum(input_low, axis=0, dtype=F32), AXIS)
    input_raw = attention_sum[:, :input_width]
    out_sum = attention_sum[:, input_width:]
    input_sum = input_raw * gain_one
    own_weight = jnp.concatenate([query_weight, key_weight, value_weight], axis=1).astype(F32)
    gain_one_sum = jnp.sum(input_raw * own_weight, axis=1)
    weighted_one = dot(input_low, weight_input, (1, 1))
    token_grad = hidden_grad + norm_back(weighted_one, token_float, scale_one)
    query_bias_sum = lax.dynamic_slice(bias_sum, (me * rows,), (rows,))
    value_bias_sum = lax.dynamic_slice(
        bias_sum, (width + key_width + me * value_bias.shape[0],), (value_bias.shape[0],)
    )
    return (
        block_output,
        token_grad.astype(BF16),
        gain_one_sum,
        input_sum[:, :width],
        query_bias_sum,
        input_sum[:, width : width + key_width],
        bias_sum[width : width + key_width],
        input_sum[:, width + key_width :],
        value_bias_sum,
        out_sum,
        gain_two_sum,
        gate_raw * gain_two,
        up_raw * gain_two,
        down_sum,
    )


def mega(rows, plane, *refs):
    (
        x_in, cot_in, pos_in, seg_in, aux_in, wq_in, wk_in, wv_in, wo_in, wg_in, wu_in, wd_in,
        o1, o2, o3, o4, o5, fo_out, bg_out, tg_out, bo_out,
        xs, xh, aux, ids, sa, wgs, wus, w1, w2, w3, w4, w5, g5,
        r1, r2, r3, r4, hn, gb, gt, up, act, pb, rb, rt,
        zb, zr, hs, dz, ob, qr, kr, vr, pr, dob, dq, cos, sin, msk, bias_in, ba, bp, bgp, bsum,
        lsem, a_s, a_r, p_s, p_r, r_s, r_r, o_s, o_r, t_s, t_r, d_s, d_r, b_s, b_r, e_s, e_r, credit, pair_credit, line_credit,
    ) = refs
    weights = (w1, w2, w3, w4, w5)
    block, width = x_in.shape
    shard = w3.shape[1]
    half = w2.shape[1]
    heads = half // HD
    every = pl.ds(0, shard)
    parts = (
        (w1, pl.ds(0, 512), r1, o1), (w2, pl.ds(0, half), r2, o2), (w3, every, r3, o3), (w4, every, r4, o4),
        (g5, every, r4, o5), (w1, pl.ds(512, half - 512), r1, o1), (w1, pl.ds(half, 2 * HD), r1, o1),
    )
    strip = width // LINES
    hidden = wg_in.shape[1]
    short = GROUP * shard - hidden
    factor = 1.0 / math.sqrt(HD)

    me = lax.axis_index(AXIS)
    c = lax.rem(me, 2)
    p = lax.rem(lax.div(me, 2), plane)
    z = lax.div(me, 2 * plane)
    f = z * 2 + c
    xbit, ybit = lax.rem(p, 2), lax.div(p, 2)
    px = p + 1 - 2 * xbit
    py = p + 2 - 4 * ybit
    pd = px + 2 - 4 * ybit
    zlow, zhigh = lax.rem(z, 2), lax.div(z, 2)
    inner = zlow + zhigh - 2 * zlow * zhigh

    def flip(bit, on):
        return bit + on - 2 * bit * on

    def zf(high, low):
        return flip(zhigh, high) * 2 + flip(zlow, low)

    def zj(j):
        if isinstance(j, int):
            return zf(j // 2, j % 2)
        return zf(lax.div(j, 2), lax.rem(j, 2))

    def dev(zz, pp, cc):
        return (zz * plane + pp) * 2 + cc

    sib, xnb, ynb = dev(z, p, 1 - c), dev(z, px, c), dev(z, py, c)

    def unit(zz, pp):
        return pl.ds(pl.multiple_of((zz * plane + pp) * 2 * rows, 16), 2 * rows)

    def piece(zz, pp, cc):
        return pl.ds(pl.multiple_of(((zz * plane + pp) * 2 + cc) * rows, 16), rows)

    def slot(s):
        return pl.ds(pl.multiple_of(s * 2 * rows, 16), 2 * rows)

    def tokens_of(zz, cc):
        return pl.ds(pl.multiple_of((zz * 2 + cc) * block, block), block)

    def chunk_of(zz):
        return pl.ds(pl.multiple_of(zz * 2 * block, 2 * block), 2 * block)

    def remote(src, dst, send, recv, target):
        return pltpu.make_async_remote_copy(
            src_ref=src, dst_ref=dst, send_sem=send, recv_sem=recv,
            device_id=(target,), device_id_type=pl.DeviceIdType.MESH,
        )

    def dot_nn(a, b):
        return lax.dot_general(a, b, (((1,), (0,)), ((), ())), preferred_element_type=F32)

    def dot_nt(a, b):
        return lax.dot_general(a, b, (((1,), (1,)), ((), ())), preferred_element_type=F32)

    def dot_tn(a, b):
        return lax.dot_general(a, b, (((0,), (0,)), ((), ())), preferred_element_type=F32)

    pending = {}

    def begin(key, copy, leave=True, arrive=True):
        copy.start()
        if leave:
            pending[key + ("leave",)] = copy.wait_send
        if arrive:
            pending[key + ("arrive",)] = copy.wait_recv

    def left(ref, send):
        remote(ref, ref, send, send, sib).wait_send()

    def landed(ref, recv):
        remote(ref, ref, recv, recv, sib).wait_recv()

    def begin_local(key, copy):
        copy.start()
        pending[key] = copy.wait

    def settle(*keys):
        for key in keys:
            pending.pop(key)()

    def settle_all(match):
        settle(*[key for key in pending if match(key)])

    def local(n, src, dst):
        return pltpu.make_async_copy(src, dst, lsem.at[n])

    def signal(semaphore, target):
        pl.semaphore_signal(semaphore, inc=1, device_id=(target,), device_id_type=pl.DeviceIdType.MESH)

    def source(k, ff, cc):
        if k == 0:
            return sa.at[cc]
        if k == 1:
            return wo_in.at[:, pl.ds(pl.multiple_of(cc * half, 128), half)]
        start = pl.multiple_of((ff * (shard // 128) - lax.div(ff, GROUP - 1) * (short // 128)) * 128, 128)
        return (wgs, wus, wd_in)[k - 2].at[:, pl.ds(start, shard)]

    def a_copy(k, j):
        zz, cc = zj(j // 2 if isinstance(j, int) else lax.div(j, 2)), flip(c, j % 2 if isinstance(j, int) else lax.rem(j, 2))
        return remote(
            source(k, zz * 2 + cc, cc), weights[k].at[piece(z, p, c)], a_s.at[k],
            a_r.at[k, j // 2 if isinstance(j, int) else lax.div(j, 2)], dev(zz, p, cc),
        )

    def a_unit(k, j):
        return weights[k].at[unit(zj(j), p)]

    def a_pass(k, j):
        return remote(a_unit(k, j), a_unit(k, j), a_s.at[5 + k], a_r.at[k, 5 - j], dev(zj(1), p, c))

    def a_pair(k):
        begin_local(("a_own", k), local(11 + k, source(k, f, c), weights[k].at[piece(z, p, c)]))
        a_copy(k, 1).start()

    def a_line(k):
        through = k < 2
        for j in (2, 3):
            a_copy(k, j).start()
        if through:
            for j in (0, 1):
                a_copy(k, 4 + 2 * inner + j).start()
        else:
            for j in (4, 5, 6, 7):
                a_copy(k, j).start()
        pending["a", k, "leave"] = lambda: left(weights[k].at[pl.ds(0, (5 if through else 7) * rows)], a_s.at[k])
        if through:

            def passed():
                @pl.when(inner == 1)
                def _():
                    left(weights[k].at[pl.ds(0, 4 * rows)], a_s.at[5 + k])

            pending["a_pass", k, "leave"] = passed

    def a_wait(k, n):
        if n == 0:
            settle(("a_own", k))
            landed(weights[k].at[piece(z, p, 1 - c)], a_r.at[k, 0])
            return 0
        j = n if k >= 2 or n == 1 else (2 + inner if n == 2 else 3 - inner)
        landed(a_unit(k, j), a_r.at[k, j])
        if k < 2 and n > 1:

            @pl.when(inner == 1)
            def _():
                a_pass(k, j).start()

        return j

    def ag_copy(k, s, j):
        if s < 4:
            part, target = unit(zj(j), p), xnb
        elif s < 8:
            part, target = unit(zj(j), p), ynb
        elif s < 10:
            part, target = unit(zj(j), px), ynb
        else:
            part, target = unit(zj(j), py), xnb
        index = s // 4 * 4 + j
        return remote(weights[k].at[part], weights[k].at[part], p_s.at[k], p_r.at[k, index], target)

    def ag_unit(k, n):
        j = a_wait(k, n)
        ag_copy(k, 0, j).start()
        ag_copy(k, 4, j).start()

    def ag_send(k, first=0):
        for n in range(first, LINES):
            ag_unit(k, n)
        pending["ag", k, "leave"] = lambda: left(weights[k].at[pl.ds(0, 24 * rows)], p_s.at[k])

    def ag_relay(k):
        for j in range(4):
            ag_copy(k, 0 if j < 2 else 4, j).wait_recv()
            ag_copy(k, 8 + j, j).start()

    def ag_finish(k):
        for s, j in ((0, 2), (0, 3), (4, 0), (4, 1), (8, 0), (8, 1), (10, 2), (10, 3)):
            ag_copy(k, s, j).wait_recv()

    def ag_sent(k):
        settle(("ag", k, "leave"))
        if k < 2:
            settle(("a_pass", k, "leave"))

    def tok_copy(which, kind, j):
        buf = (hn, gb)[which]
        part = tokens_of(zj(0 if kind == "own" else j), c)
        if kind == "own":
            send, recv, target = t_s.at[which, 0], j, dev(zj(j), p, c)
        elif kind == "pair":
            send, recv, target = t_s.at[which, 0], 4 + j, sib
        else:
            send, recv, target = t_s.at[which, 1], 5 - j, dev(zj(1), p, c)
        return remote(buf.at[part], buf.at[part], send, t_r.at[which, recv], target)

    def tok_send(which):
        tok_copy(which, "own", 1).start()
        tok_copy(which, "own", 2 + inner).start()
        tok_copy(which, "pair", 0).start()

        def sent():
            buf = (hn, gb)[which]
            left(buf.at[pl.ds(0, 6 * block)], t_s.at[which, 0])

            @pl.when(inner == 1)
            def _():
                left(buf.at[pl.ds(0, 2 * block)], t_s.at[which, 1])

        pending["tok", which, "leave"] = sent

    def tok_forward(which):
        for j in (1, 2 + inner, 3 - inner):
            tok_copy(which, "own", j).wait_recv()
            if not isinstance(j, int):

                @pl.when(inner == 1)
                def _():
                    tok_copy(which, "pass", j).start()

            tok_copy(which, "pair", j).start()

    def tok_finish(which):
        for j in range(4):
            tok_copy(which, "pair", j).wait_recv()

    def e_copy(n, src, dst):
        return remote(src, dst, e_s.at[n], e_r.at[n], sib)

    own_rows = pl.ds(pl.multiple_of(c * block, block), block)

    def bias_in_copy(s):
        zz, cc = zj(s // 2), flip(c, s % 2)
        return remote(bias_in.at[cc], ba.at[f], b_s.at[0], b_r.at[0], dev(zz, p, cc))

    def bias_plane_copy(group, n, buf):
        target = dev(z, (px, py, pd)[n], c)
        return remote(buf.at[p], buf.at[p], b_s.at[group], b_r.at[group], target)

    def bias_out_copy(s):
        zz, cc = zj(s // 2), flip(c, s % 2)
        return remote(bsum, bg_out.at[f], b_s.at[3], b_r.at[3], dev(zz, p, cc))

    def bias_note(group, buf, count):
        pending["bias", group, "leave"] = lambda: left(buf.at[pl.ds(0, count)], b_s.at[group])
        pending["bias", group, "arrive"] = lambda: landed(buf.at[pl.ds(0, count)], b_r.at[group])

    def rs_copy(k, s, h):
        ref, cols, land = parts[k][:3]
        zz = zf((0, 1, 1, 0, 0, 1)[s], h)
        part = unit(zz, (pd, pd, px, py, px, py)[s])
        place = (0, 2, 6, 8, 4, 10)[s] + h
        target = (ynb, xnb, xnb, ynb, xnb, ynb)[s]
        return remote(ref.at[part, cols], land.at[slot(place), cols], r_s.at[k], r_r.at[k, place], target)

    def rs_step(k, left_ref, right_ref, h):
        ref, cols = parts[k][:2]
        for high in (1, 0):
            at = pl.multiple_of(zf(high, h) * strip, 128)
            ref[pl.ds(at, strip), cols] = dot_tn(left_ref[:, pl.ds(at, strip)], right_ref[:, cols]).astype(BF16)
            for s in ((0, 3), (1, 2))[high]:
                rs_copy(k, s, h).start()
        pending["rs", k, "leave"] = lambda: left(ref.at[pl.ds(0, 24 * rows), cols], r_s.at[k])

    def rs_start(k, left_ref, right_ref, steps=(0, 1)):
        @pl.loop(steps[0], steps[-1] + 1)
        def both(i):
            rs_step(k, left_ref, right_ref, 1 - i)

    def rs_middle(k):
        ref, cols, land = parts[k][:3]

        @pl.loop(0, 2)
        def both(i):
            h = 1 - i
            for high in (1, 0):
                rs_copy(k, high, h).wait_recv()
                part = unit(zf(high, h), (px, py)[high])
                got = land[slot(2 * high + h), cols]
                ref[part, cols] = (ref[part, cols].astype(F32) + got.astype(F32)).astype(BF16)
                rs_copy(k, 4 + high, h).start()

    def out_copy(k, j, other):
        ref, cols, _, out = parts[k]
        zz, cc = zj(j), flip(c, other)
        return remote(ref.at[piece(zz, p, cc), cols], out.at[f, :, cols], o_s.at[k], o_r.at[k], dev(zz, p, cc))

    def rs_finish(k):
        ref, cols, land, out = parts[k]
        for j in (3, 1, 2, 0):
            h, high = j % 2, j // 2
            rs_copy(k, (4, 2)[high], h).wait_recv()
            rs_copy(k, (3, 5)[high], h).wait_recv()
            part = unit(zj(j), p)
            got = land[slot(4 + j), cols].astype(F32) + land[slot(8 + j), cols].astype(F32)
            ref[part, cols] = (ref[part, cols].astype(F32) + got).astype(BF16)
            out_copy(k, j, 1).start()
            if j == 0:
                begin_local(("out_own", k), local(17 + k, ref.at[piece(z, p, c), cols], out.at[f, :, cols]))
            else:
                out_copy(k, j, 0).start()
        pending["out", k, "leave"] = lambda: left(ref.at[pl.ds(0, 7 * rows), cols], o_s.at[k])
        pending["out", k, "arrive"] = lambda: landed(ref.at[pl.ds(0, 7 * rows), cols], o_r.at[k])

    def pair_copy(which, j):
        return remote(
            pb.at[tokens_of(zj(j), 1 - c)], rb.at[pl.ds(pl.multiple_of(j * block, block), block)],
            d_s.at[which, 0], d_r.at[which, j], sib,
        )

    def line_copy(which, j):
        dst = fo_out.at[1] if which == 1 and isinstance(j, int) and j == 1 else rt.at[j - 1]
        return remote(
            pb.at[tokens_of(zj(j), c)], dst, d_s.at[which, 1], d_r.at[which, 4 + j], dev(zj(1), p, c)
        )

    def far_copy(which, j):
        dst = fo_out.at[2] if which == 1 else rt.at[3]
        return remote(pb.at[tokens_of(zj(j), c)], dst, d_s.at[which, 1], d_r.at[which, 4], dev(zj(j), p, c))

    def far_add(which, j):
        @pl.when(inner == 1)
        def _():
            line_copy(which, 5 - j).wait_recv()
            part = tokens_of(zj(j), c)
            pb[part] = (pb[part].astype(F32) + rt[4 - j].astype(F32)).astype(BF16)
            far_copy(which, j).start()

    def pair_add(which, j):
        pair_copy(which, j).wait_recv()
        part = tokens_of(zj(j), c)
        got = rb[pl.ds(pl.multiple_of(j * block, block), block)].astype(F32)
        pb[part] = (pb[part].astype(F32) + got).astype(BF16)

    def sum_loop(which, compute, beside=None):
        @pl.loop(0, LINES)
        def chunk(i):
            j = LINES - 1 - i
            if beside is not None:
                beside(i)
            compute(chunk_of(zj(j)))
            pair_copy(which, j).start()

            @pl.when((i > 0) & (i < LINES - 1))
            def _():
                pair_add(which, j + 1)

                @pl.when(inner == 0)
                def _():
                    line_copy(which, j + 1).start()

            @pl.when(i == LINES - 1)
            def _():
                pair_add(which, 1)
                line_copy(which, 1).start()

        pair_add(which, 0)

        def sent():
            left(pb.at[pl.ds(0, LINES * block)], d_s.at[which, 0])
            left(pb.at[pl.ds(0, 3 * block)], d_s.at[which, 1])

        pending["sum", which, "leave"] = sent
        pending["sum", which, 1, "arrive"] = lambda: line_copy(which, 1).wait_recv()
        pending["sum", which, 2, "arrive"] = lambda: far_copy(which, 2).wait_recv()

    def rope(v, b):
        return v * cos[b] + pltpu.roll(v, HD // 2, 1) * sin[b]

    def rope_back(v, b):
        return v * cos[b] + pltpu.roll(v * sin[b], HD // 2, 1)

    row_id = lax.broadcasted_iota(jnp.int32, (block, block), 0)
    lane_id = lax.broadcasted_iota(jnp.int32, (block, block), 1)

    def column(row):
        return jnp.sum(jnp.where(row_id == lane_id, row, 0.0), axis=1, keepdims=True)

    tile = 3 * HD
    last = lax.div(f, GROUP - 1)
    keep = jnp.where(lax.broadcasted_iota(jnp.int32, (1, tile), 1) < last * short, 0.0, 1.0)

    def enter():
        begin_local(("aux",), local(0, aux_in, aux.at[c]))
        begin_local(("pos",), local(25, pos_in, ids.at[0]))
        begin_local(("seg",), local(22, seg_in, ids.at[1]))
        begin_local(("x",), local(1, x_in, xs.at[c]))
        for side in range(2):
            begin_local(("wq", side), local(2 + side, wq_in.at[:, pl.ds(side * half, half)], sa.at[side, :, pl.ds(0, half)]))
            begin_local(("wk", side), local(4 + side, wk_in.at[:, pl.ds(side * HD, HD)], sa.at[side, :, pl.ds(half, HD)]))
            begin_local(("wv", side), local(6 + side, wv_in.at[:, pl.ds(side * HD, HD)], sa.at[side, :, pl.ds(half + HD, HD)]))
        begin_local(("wg",), local(8, wg_in, wgs))
        begin_local(("wu",), local(9, wu_in, wus))
        begin_local(("cot",), local(10, cot_in, gb.at[tokens_of(z, c)]))
        barrier = pltpu.get_barrier_semaphore()
        friends = [dev(zj(j // 2), p, flip(c, j % 2)) for j in range(1, GROUP)] + [xnb, ynb, dev(z, pd, c)]
        for friend in friends:
            signal(barrier, friend)
        settle(("aux",), ("pos",), ("seg",), ("x",), *[(name, side) for side in range(2) for name in ("wq", "wk", "wv")])
        aux[c, 0:1] = ids[0].astype(F32)
        aux[c, 1:2] = ids[1].astype(F32)
        gain_one = column(aux[c][2:3])[:rows]
        for side in range(2):
            sa[side] = (sa[side].astype(F32) * gain_one).astype(BF16)
        pl.semaphore_wait(barrier, len(friends))

    def exchange_inputs():
        begin(("e", 0), e_copy(0, aux.at[c], aux.at[c]))
        begin(("e", 1), e_copy(1, xs.at[c], xs.at[c]))

    def bias_first():
        step = lax.rem(me, 2 * plane * LINES // 2)
        info = aux[c]

        def placed(row, count, size):
            wide = jnp.concatenate([row] + [jnp.zeros_like(row)] * (size // HD - 1), axis=1) if size > HD else row
            wide = jnp.broadcast_to(wide, (8, size))
            return pltpu.roll(wide, step * count, 1)[0:1]

        own = jnp.concatenate(
            [placed(info[4:5], rows, half), placed(info[5:6], rows // KEYS, HD), placed(info[6:7], rows // KEYS, HD)], axis=1
        )
        side = lax.div(me, plane * LINES)
        bias_in[side] = own
        bias_in[1 - side] = jnp.zeros_like(own)
        begin_local(("bias_own",), local(16, bias_in.at[c], ba.at[f]))
        for s in range(1, GROUP):
            bias_in_copy(s).start()
        bias_note(0, ba, GROUP - 1)

    def bias_second():
        settle(("bias_own",), ("bias", 0, "arrive"))
        total = ba[0]
        for s in range(1, GROUP):
            total = total + ba[s]
        bp[p] = total
        for n in range(3):
            bias_plane_copy(1, n, bp).start()
        bias_note(1, bp, 3)

    def scale_feed():
        gain_two = column(aux[c][3:4])[:rows]
        for name, ref in (("wg", wgs), ("wu", wus)):
            settle((name,))
            for n in range(0, hidden, 1792):
                cols = pl.ds(n, min(1792, hidden - n))
                ref[:, cols] = (ref[:, cols].astype(F32) * gain_two).astype(BF16)

    def mask_upstream():
        settle(("cot",))
        live = jnp.where(column(aux[c][1:2]) >= 0.0, 1.0, 0.0)
        gb[tokens_of(z, c)] = (gb[tokens_of(z, c)].astype(F32) * live).astype(BF16)

    def norm_tokens():
        settle(("e", 0, "arrive"), ("e", 1, "arrive"))
        lanes = lax.broadcasted_iota(jnp.int32, (1, HD), 1)
        freq_index = jnp.where(lanes < HD // 2, lanes, lanes - HD // 2).astype(F32)
        frequency = jnp.exp(freq_index * (-2.0 * math.log(ROPE_BASE) / HD))
        for b in range(2):
            values = xs[b].astype(F32)
            scale = lax.rsqrt(jnp.mean(values * values, axis=1, keepdims=True) + EPSILON)
            xh[pl.ds(b * block, block)] = (values * scale).astype(BF16)
            info = aux[b]
            angles = column(info[0:1]) * frequency
            cos[b] = jnp.cos(angles)
            sine = jnp.sin(angles)
            sin[b] = jnp.where(lane_id < HD // 2, -sine, sine)
            same = column(info[1:2]) == info[1:2]
            msk[b] = jnp.where(same & (lane_id <= row_id), 1.0, 0.0)

    def project():
        settle(("bias", 1, "arrive"))
        bias_row = (bp[0] + bp[1]) + (bp[2] + bp[3])
        for n in range(heads // 2 + 1):
            cols = pl.ds(n * 2 * HD, 2 * HD)
            out = dot_nn(xh[...], w1[:, cols]) + bias_row[:, n * 2 * HD : (n + 1) * 2 * HD]
            for b in range(2):
                part = out[b * block : (b + 1) * block]
                if n < heads // 2:
                    for i in range(2):
                        qr[b, pl.ds((2 * n + i) * block, block)] = rope(part[:, i * HD : (i + 1) * HD], b).astype(BF16)
                else:
                    kr[b] = rope(part[:, :HD], b).astype(BF16)
                    vr[b] = part[:, HD:].astype(BF16)

    def attend():
        for b in range(2):
            scores = dot_nt(qr[b], kr[b]) * factor
            scores = jnp.where(msk[b][None] > 0.0, scores.reshape(heads, block, block), -jnp.inf)
            weight = jnp.exp(scores - jnp.max(scores, axis=-1, keepdims=True))
            weight = weight / jnp.sum(weight, axis=-1, keepdims=True)
            weight = weight.reshape(heads * block, block)
            pr[b] = weight
            mixed = dot_nn(weight.astype(BF16), vr[b]).astype(BF16)
            for i in range(heads):
                ob[pl.ds(b * block, block), pl.ds(i * HD, HD)] = mixed[i * block : (i + 1) * block]

    def attend_out():
        for n in range(0, width, 512):
            part = dot_nt(ob[...], w2[pl.ds(n, 512), :])
            zb[0, :, pl.ds(n, 512)] = part[:block]
            zb[1, :, pl.ds(n, 512)] = part[block:]
        begin(("e", 2), e_copy(2, zb.at[1 - c], zr))

    def hidden_state():
        settle(("e", 2, "arrive"))
        state = xs[c].astype(F32) + zb[c] + zr[...]
        hs[...] = state
        scale_two = lax.rsqrt(jnp.mean(state * state, axis=1, keepdims=True) + EPSILON)
        hn[tokens_of(z, c)] = (state * scale_two).astype(BF16)

    def feed_forward(first, end):
        @pl.loop(first, end)
        def chunk(i):
            rows_here = chunk_of(zj(i))
            left = hn[rows_here]
            for n in range(0, shard, tile):
                cols = pl.ds(n, tile)
                gate = dot_nn(left, w3[:, cols])
                lift = dot_nn(left, w4[:, cols])
                if n == 0:
                    gate = gate * keep
                    lift = lift * keep
                gt[rows_here, cols] = gate.astype(BF16)
                up[rows_here, cols] = lift.astype(BF16)
                act[rows_here, cols] = (gate * jax.nn.sigmoid(gate) * lift).astype(BF16)

    def feed_backward(together=False):
        def beside(i):
            @pl.when(lax.rem(i, 2) == 0)
            def _():
                rs_step(4, gb, act, 1 - lax.div(i, 2))

        def compute(rows_here):
            left = gb[rows_here]
            for n in range(0, shard, tile):
                cols = pl.ds(n, tile)
                d_act = dot_nn(left, w5[:, cols])
                gate = gt[rows_here, cols].astype(F32)
                lift = up[rows_here, cols].astype(F32)
                sig = jax.nn.sigmoid(gate)
                gt[rows_here, cols] = (d_act * lift * sig * (1.0 + gate * (1.0 - sig))).astype(BF16)
                up[rows_here, cols] = (d_act * gate * sig).astype(BF16)
            for n in range(0, width, 512):
                part = pl.ds(n, 512)
                back = dot_nt(gt[rows_here], w3[part, :]) + dot_nt(up[rows_here], w4[part, :])
                pb[rows_here, part] = back.astype(BF16)

        sum_loop(0, compute, beside if together else None)
        signal(pair_credit, sib)

    def line_ready():
        @pl.when(inner == 1)
        def _():
            signal(line_credit, dev(zj(1), p, c))

    def feed_output():
        settle(("sum", 0, "leave"))
        pl.semaphore_wait(pair_credit, 1)

        @pl.when(inner == 0)
        def _():
            pl.semaphore_wait(line_credit, 1)

        def compute(rows_here):
            for n in range(0, width, 512):
                part = pl.ds(n, 512)
                pb[rows_here, part] = dot_nt(act[rows_here], w5[part, :]).astype(BF16)

        sum_loop(1, compute)

    def block_result():
        settle(("sum", 1, 1, "arrive"), ("sum", 1, 2, "arrive"))
        for n in range(2):
            begin_local(("fetch", n), local(2 + n, fo_out.at[1 + n], rb.at[pl.ds(n * block, block)]))
        settle(("fetch", 0), ("fetch", 1))
        live = jnp.where(column(aux[c][1:2]) >= 0.0, 1.0, 0.0)
        total = hs[...] + pb[tokens_of(z, c)].astype(F32)
        total = total + rb[pl.ds(0, block)].astype(F32) + rb[pl.ds(block, block)].astype(F32)
        xs[1 - c] = (live * total).astype(BF16)
        begin_local(("bo",), local(1, xs.at[1 - c], bo_out))

    def landing_free():
        for target in (xnb, ynb):
            signal(credit, target)

    def landing_wait():
        pl.semaphore_wait(credit, 2)

    def hidden_gradient():
        settle(("sum", 0, 1, "arrive"), ("sum", 0, 2, "arrive"))
        weighted = pb[tokens_of(z, c)].astype(F32) + rt[0].astype(F32) + rt[3].astype(F32)
        state = hs[...]
        scale_two = lax.rsqrt(jnp.mean(state * state, axis=1, keepdims=True) + EPSILON)
        spread = jnp.mean(weighted * state, axis=1, keepdims=True)
        grad = (
            gb[tokens_of(z, c)].astype(F32)
            + scale_two * weighted
            - state * (scale_two * scale_two * scale_two) * spread
        )
        dz[own_rows] = grad.astype(BF16)
        begin(("e", 3), e_copy(3, dz.at[own_rows], dz.at[own_rows]))

    def attend_out_back():
        settle(("e", 3, "arrive"))
        for n in range(0, heads, 2):
            part = dot_nn(dz[...], w2[:, pl.ds(n * HD, 2 * HD)]).astype(BF16)
            for b in range(2):
                for i in range(2):
                    dob[b, pl.ds((n + i) * block, block)] = part[b * block : (b + 1) * block, i * HD : (i + 1) * HD]

    def attend_back():
        for b in range(2):
            weight = pr[b]
            d_weight = dot_nt(dob[b], vr[b])
            d_score = weight * (d_weight - jnp.sum(weight * d_weight, axis=-1, keepdims=True))
            d_score = d_score.astype(BF16)
            d_query = dot_nn(d_score, kr[b]) * factor
            here = pl.ds(b * block, block)
            for i in range(heads):
                dq[here, pl.ds(i * HD, HD)] = rope_back(d_query[i * block : (i + 1) * block], b).astype(BF16)
            dq[here, pl.ds(half, HD)] = rope_back(dot_tn(d_score, qr[b]) * factor, b).astype(BF16)
            dq[here, pl.ds(half + HD, HD)] = dot_tn(weight.astype(BF16), dob[b]).astype(BF16)

    def project_back():
        settle(("e", 2, "leave"))
        for n in range(0, width, 512):
            part = dot_nt(dq[...], w1[pl.ds(n, 512), :])
            zb[0, :, pl.ds(n, 512)] = part[:block]
            zb[1, :, pl.ds(n, 512)] = part[block:]
        begin(("e", 4), e_copy(4, zb.at[1 - c], zr))

    def bias_back():
        bgp[p] = jnp.sum(dq[...].astype(F32), axis=0, keepdims=True)
        for n in range(3):
            bias_plane_copy(2, n, bgp).start()
        bias_note(2, bgp, 3)

    def bias_last():
        settle(("bias", 2, "arrive"))
        bsum[...] = (bgp[0] + bgp[1]) + (bgp[2] + bgp[3])
        begin_local(("bias_sum",), local(24, bsum, bg_out.at[f]))
        for s in range(1, GROUP):
            bias_out_copy(s).start()
        bias_note(3, ba, GROUP - 1)

    def token_gradient():
        settle(("e", 4, "arrive"))
        weighted = zb[c] + zr[...]
        values = xs[c].astype(F32)
        scale = lax.rsqrt(jnp.mean(values * values, axis=1, keepdims=True) + EPSILON)
        spread = jnp.mean(weighted * values, axis=1, keepdims=True)
        grad = dz[own_rows].astype(F32) + scale * weighted - values * (scale * scale * scale) * spread
        settle(("e", 1, "leave"))
        xs[c] = grad.astype(BF16)
        begin_local(("tg",), local(0, xs.at[c], tg_out))

    enter()
    exchange_inputs()
    a_pair(0)
    a_line(0)
    bias_first()
    a_pair(1)
    a_line(1)
    ag_unit(0,0)
    a_pair(4)
    scale_feed()
    a_pair(2)
    a_pair(3)
    ag_unit(0,1)
    ag_unit(1,0)
    mask_upstream()
    ag_unit(2,0)
    ag_unit(3,0)
    ag_send(0,2)
    a_line(2)
    norm_tokens()
    ag_relay(0)
    bias_second()
    ag_send(1,1)
    a_line(3)
    ag_finish(0)
    project()
    ag_relay(1)
    ag_send(2,1)
    attend()
    ag_finish(1)
    attend_out()
    hidden_state()
    tok_send(0)
    ag_send(3,1)
    a_line(4)
    tok_send(1)
    ag_relay(2)
    ag_relay(3)
    tok_forward(0)
    ag_send(4, 0)
    tok_finish(0)
    ag_finish(2)
    ag_finish(3)
    feed_forward(0, LINES)
    ag_relay(4)
    tok_forward(1)
    ag_finish(4)
    tok_finish(1)
    feed_backward(True)
    far_add(0, 2)
    rs_middle(4)
    ag_sent(2)
    rs_start(2, hn, gt)
    far_add(0, 3)
    line_ready()
    rs_finish(4)
    landing_free()
    ag_sent(3)
    landing_wait()
    rs_start(3, hn, up)
    hidden_gradient()
    rs_middle(2)
    feed_output()
    far_add(1, 2)
    attend_out_back()
    ag_sent(1)
    rs_start(1, dz, ob)
    far_add(1, 3)
    rs_finish(2)
    rs_middle(3)
    attend_back()
    project_back()
    ag_sent(0)
    rs_start(0, xh, dq)
    rs_finish(3)
    rs_middle(1)
    rs_start(5, xh, dq)
    rs_start(6, xh, dq)
    rs_middle(0)
    rs_finish(1)
    bias_back()
    token_gradient()
    rs_middle(5)
    rs_middle(6)
    rs_finish(0)
    bias_last()
    block_result()
    rs_finish(5)
    rs_finish(6)
    settle(*list(pending))


def kernel_call(rows, plane, block, width, hidden, aux, tokens, cotangent, position, segment, *weights):
    half = width // 2
    blocks = hidden // 128
    shard = -(-blocks // GROUP) * 128
    inner = half + 2 * HD
    heads = half // HD
    columns = (inner, half, shard, shard, shard)
    dma = pltpu.SemaphoreType.DMA
    vm = pltpu.VMEM
    group_tokens = GROUP * block
    any_space = pl.BlockSpec(memory_space=pl.ANY)
    out_shape = [jax.ShapeDtypeStruct((GROUP, rows, n), BF16) for n in columns]
    out_shape += [
        jax.ShapeDtypeStruct((3, block, width), BF16),
        jax.ShapeDtypeStruct((GROUP, 1, inner), F32),
        jax.ShapeDtypeStruct((block, width), BF16),
        jax.ShapeDtypeStruct((block, width), BF16),
    ]
    scratch = [
        vm((2, block, width), BF16), vm((2 * block, width), BF16), vm((2, 8, 128), F32), vm((2, 1, 128), jnp.int32),
        vm((2, rows, inner), BF16),
        vm((rows, hidden), BF16), vm((rows, hidden), BF16),
    ]
    scratch += [vm((width, n), BF16) for n in columns] + [vm((width, shard), BF16)]
    scratch += [vm((12 * 2 * rows, n), BF16) for n in columns[:4]]
    scratch += [vm((group_tokens, width), BF16)] * 2 + [vm((group_tokens, shard), BF16)] * 3
    scratch += [vm((group_tokens, width), BF16), vm((LINES * block, width), BF16), vm((LINES, block, width), BF16)]
    scratch += [
        vm((2, block, width), F32), vm((block, width), F32), vm((block, width), F32),
        vm((2 * block, width), BF16),
        vm((2 * block, half), BF16), vm((2, heads * block, HD), BF16), vm((2, block, HD), BF16), vm((2, block, HD), BF16),
        vm((2, heads * block, block), F32), vm((2, heads * block, HD), BF16), vm((2 * block, inner), BF16),
        vm((2, block, HD), F32), vm((2, block, HD), F32), vm((2, block, block), F32),
        vm((2, 1, inner), F32), vm((GROUP, 1, inner), F32), vm((4, 1, inner), F32), vm((4, 1, inner), F32), vm((1, inner), F32),
    ]
    scratch += [dma((26,))]
    scratch += [dma((7,)), dma((5, 4)), dma((5,)), dma((5, 12)), dma((7,)), dma((7, 12)), dma((7,)), dma((7,))]
    scratch += [dma((2, 2)), dma((2, 8)), dma((2, 2)), dma((2, 8)), dma((4,)), dma((4,)), dma((5,)), dma((5,))]
    scratch += [pltpu.SemaphoreType.REGULAR] * 3
    return pl.pallas_call(
        functools.partial(mega, rows, plane),
        out_shape=out_shape,
        in_specs=[any_space] * 12,
        out_specs=[any_space] * 9,
        scratch_shapes=scratch,
        compiler_params=pltpu.CompilerParams(
            collective_id=0, has_side_effects=True, vmem_limit_bytes=64 * 2**20 - 2**17
        ),
        name="layer",
    )(tokens, cotangent, position, segment, aux, *weights)


def gather_outputs(rows, plane, hidden, *refs):
    (
        o1, o2, o3, o4, o5, bg, tg, bo, aux, wq, wk, wv, wg, wu,
        bo_out, tg_out, gain_one_out, wq_out, bq_out, wk_out, bk_out, wv_out, bv_out, wo_out, gain_two_out,
        wg_out, wu_out, wd_out, total,
    ) = refs
    step = pl.program_id(0)
    steps = pl.num_programs(0)
    half = wo_out.shape[1] // 2
    shard = o3.shape[2]
    per = o3.shape[0]
    short = GROUP * shard - hidden
    me = lax.axis_index(AXIS)
    row_id = lax.broadcasted_iota(jnp.int32, (128, 128), 0)
    lane_id = lax.broadcasted_iota(jnp.int32, (128, 128), 1)

    def column(row):
        return jnp.sum(jnp.where(row_id == lane_id, row, 0.0), axis=1, keepdims=True)[:rows]

    def as_row(col):
        return jnp.sum(jnp.where(row_id[:rows, :rows] == lane_id[:rows, :rows], col, 0.0), axis=0, keepdims=True)

    gain_one = column(aux[2:3])
    gain_two = column(aux[3:4])

    @pl.when(step == 0)
    def _():
        bo_out[...] = bo[...]
        tg_out[...] = tg[...]
        sums = jnp.zeros((rows, 1), F32)
        for side in range(2):
            part = o1[side].astype(F32)
            for zz in range(1, LINES):
                part = part + o1[2 * zz + side].astype(F32)
            q_part, k_part, v_part = part[:, :half], part[:, half : half + HD], part[:, half + HD :]
            here, keys = pl.ds(side * half, half), pl.ds(side * HD, HD)
            sums = sums + jnp.sum(q_part * wq[:, here].astype(F32), axis=1, keepdims=True)
            sums = sums + jnp.sum(k_part * wk[:, keys].astype(F32), axis=1, keepdims=True)
            sums = sums + jnp.sum(v_part * wv[:, keys].astype(F32), axis=1, keepdims=True)
            wq_out[:, here] = q_part * gain_one
            wk_out[:, keys] = k_part * gain_one
            wv_out[:, keys] = v_part * gain_one
            part = o2[side].astype(F32)
            for zz in range(1, LINES):
                part = part + o2[2 * zz + side].astype(F32)
            wo_out[:, here] = part
        gain_one_out[...] = as_row(sums)
        sides = [(bg[side] + bg[2 + side]) + (bg[4 + side] + bg[6 + side]) for side in range(2)]
        bk_out[:, 0:HD] = sides[0][:, half : half + HD]
        bk_out[:, HD : 2 * HD] = sides[1][:, half : half + HD]
        mine = jnp.where(lax.div(me, plane * LINES) == 0, sides[0], sides[1])
        place = lax.rem(me, plane * LINES)

        def taken(row, count):
            size = row.shape[1]
            wide = jnp.broadcast_to(row, (8, size))
            return pltpu.roll(wide, lax.rem(size - place * count, size), 1)[0:1, :count]

        bq_out[...] = taken(mine[:, :half], rows)
        bv_out[...] = taken(mine[:, half + HD :], rows // KEYS)
        total[...] = jnp.zeros_like(total)

    def put(first):
        sums = jnp.zeros((rows, 1), F32)
        for i in range(per):
            skip = first if i == per - 1 else 0
            cols = pl.ds(i * shard, shard - skip)
            gate = o3[i][:, skip:].astype(F32)
            lift = o4[i][:, skip:].astype(F32)
            sums = sums + jnp.sum(gate * wg[:, cols].astype(F32) + lift * wu[:, cols].astype(F32), axis=1, keepdims=True)
            wg_out[:, cols] = gate * gain_two
            wu_out[:, cols] = lift * gain_two
            wd_out[:, cols] = o5[i][:, skip:].astype(F32)
        total[...] = total[...] + sums

    @pl.when(step < steps - 1)
    def _():
        put(0)

    @pl.when(step == steps - 1)
    def _():
        put(short)
        gain_two_out[...] = as_row(total[...])


def output_call(rows, plane, block, width, hidden, pieces, bias_sum, token_grad, block_output, aux, weights):
    per = 4
    shard = pieces[2].shape[2]
    key_width = weights[1].shape[1]

    def whole(shape):
        return pl.BlockSpec(shape, lambda i: (0,) * len(shape))

    feed = pl.BlockSpec((per, rows, shard), lambda i: (i, 0, 0))
    wide = pl.BlockSpec((rows, per * shard), lambda i: (0, i))
    shapes = [
        ((block, width), BF16), ((block, width), BF16), ((1, rows), F32), ((rows, width), F32), ((1, rows), F32),
        ((rows, key_width), F32), ((1, key_width), F32), ((rows, key_width), F32), ((1, rows // KEYS), F32),
        ((rows, width), F32), ((1, rows), F32),
        ((rows, hidden), F32), ((rows, hidden), F32), ((rows, hidden), F32),
    ]
    return pl.pallas_call(
        functools.partial(gather_outputs, rows, plane, hidden),
        grid=(GROUP // per,),
        out_shape=[jax.ShapeDtypeStruct(*shape) for shape in shapes],
        in_specs=[whole(pieces[0].shape), whole(pieces[1].shape), feed, feed, feed, whole(bias_sum.shape)]
        + [whole((block, width))] * 2 + [whole(aux.shape)]
        + [whole((rows, width)), whole((rows, key_width)), whole((rows, key_width)), wide, wide],
        out_specs=[whole(shape) for shape, _ in shapes[:11]] + [wide] * 3,
        scratch_shapes=[pltpu.VMEM((rows, 1), F32)],
        compiler_params=pltpu.CompilerParams(vmem_limit_bytes=64 * 2**20 - 2**17),
        name="outputs",
    )(*pieces, bias_sum, token_grad, block_output, aux, *weights)


def kernel_body(
    tokens, segment, position, first_gain, query_weight, query_bias, key_weight, key_bias, value_weight, value_bias,
    out_weight, second_gain, gate_weight, up_weight, down_weight, cotangent,
):
    count = lax.axis_size(AXIS)
    plane = count // GROUP
    rows, width = query_weight.shape
    block = tokens.shape[0]
    hidden = gate_weight.shape[1]

    aux = jnp.zeros((1024,), F32)
    for n, vector in enumerate((first_gain, second_gain, query_bias, key_bias, value_bias), 2):
        aux = aux + jnp.pad(vector.astype(F32), (128 * n, 1024 - 128 * n - vector.shape[0]))
    aux = aux.reshape(8, 128)
    *pieces, _, bias_sum, token_grad, block_output = kernel_call(
        rows, plane, block, width, hidden, aux, tokens, cotangent, position[None], segment[None],
        query_weight, key_weight, value_weight, out_weight, gate_weight, up_weight, down_weight,
    )
    outs = output_call(
        rows, plane, block, width, hidden, pieces, bias_sum, token_grad, block_output, aux,
        (query_weight, key_weight, value_weight, gate_weight, up_weight),
    )
    return tuple(out.reshape(-1) if out.shape[0] == 1 else out for out in outs)


def layer(*args):
    tokens, query_weight, key_weight, gate_weight = args[0], args[4], args[6], args[12]
    rows, width = query_weight.shape
    fits = (
        lax.axis_size(AXIS) == 4 * GROUP
        and rows % 16 == 0
        and rows * lax.axis_size(AXIS) == width
        and width == H * HD
        and key_weight.shape[1] == KV * HD
        and KV == 2
        and tokens.shape[0] == 128
        and gate_weight.shape[1] % 128 == 0
    )
    return kernel_body(*args) if fits else array_body(*args)


def solution(mesh):
    split = P(AXIS)
    split_rows = P(AXIS, None)
    return jax.shard_map(
        layer,
        mesh=mesh,
        in_specs=(
            split_rows, split, split, split, split_rows, split, split_rows, split,
            split_rows, split, split_rows, split, split_rows, split_rows, split_rows, split_rows,
        ),
        out_specs=(
            split_rows, split_rows, split, split_rows, split, split_rows, P(),
            split_rows, split, split_rows, split, split_rows, split_rows, split_rows,
        ),
        check_vma=False,
    )
```

```python
import functools
import math

import jax
import jax.numpy as jnp
from jax import lax
from jax.experimental import pallas as pl
from jax.experimental.pallas import tpu as pltpu
from jax.sharding import PartitionSpec as P

H = 12
KV = 2
HD = 128
GROUP = 8
LINES = GROUP // 2
KEYS = H // KV

EPSILON = 1e-06
ROPE_BASE = 1000000.0
AXIS = "fsdp"
F32 = jnp.float32
BF16 = jnp.bfloat16


def tables(position):
    freq_index = jnp.arange(HD // 2).astype(F32)
    frequency = jnp.exp(freq_index * (-2.0 * math.log(ROPE_BASE) / HD))
    angles = position.astype(F32)[:, None] * frequency[None, :]
    angles = jnp.concatenate([angles, angles], axis=-1)
    return (jnp.cos(angles)[:, None, :], jnp.sin(angles)[:, None, :])


def rotary(values, cosine_table, sine_table):
    middle = values.shape[-1] // 2
    turned = jnp.concatenate([-values[..., middle:], values[..., :middle]], axis=-1)
    return values * cosine_table + turned * sine_table


def rotary_back(gradient, cosine_table, sine_table):
    middle = gradient.shape[-1] // 2
    weighted = gradient * sine_table
    return gradient * cosine_table + jnp.concatenate(
        [weighted[..., middle:], -weighted[..., :middle]], axis=-1
    )


def norm_back(weighted, values, row_scale):
    return row_scale * weighted - values * row_scale**3 * jnp.mean(
        weighted * values, axis=-1, keepdims=True
    )


def dot(left, right, dims):
    return lax.dot_general(left, right, ((dims[:1], dims[1:]), ((), ())), preferred_element_type=F32)


def groups_of(count):
    plane = count // GROUP
    lines = GROUP // 2
    token = [[(z * plane + p) * 2 + c for z in range(lines) for c in range(2)] for p in range(plane)]
    other = [[(z * plane + p) * 2 + c for p in range(plane)] for z in range(lines) for c in range(2)]
    return token, other


def array_body(
    tokens,
    segment,
    position,
    first_gain,
    query_weight,
    query_bias,
    key_weight,
    key_bias,
    value_weight,
    value_bias,
    out_weight,
    second_gain,
    gate_weight,
    up_weight,
    down_weight,
    cotangent,
):
    count = lax.axis_size(AXIS)
    me = lax.axis_index(AXIS)
    token_groups, plane_groups = groups_of(count)
    plane = count // GROUP
    lines = GROUP // 2
    rows, width = query_weight.shape
    hidden = gate_weight.shape[1]
    shard = hidden // GROUP
    key_width = key_weight.shape[1]
    length = tokens.shape[0]
    heads_per_key = H // KV
    factor = 1.0 / math.sqrt(HD)

    gain_one = first_gain.astype(F32)[:, None]
    gain_two = second_gain.astype(F32)[:, None]

    def scaled(weight, gain):
        return (weight.astype(F32) * gain).astype(BF16)

    attention_own = jnp.concatenate(
        [scaled(query_weight, gain_one), scaled(key_weight, gain_one), scaled(value_weight, gain_one), out_weight], axis=1
    )
    attention_all = lax.all_gather(attention_own, AXIS, axis=0, tiled=True)
    input_width = width + 2 * key_width
    weight_input = attention_all[:, :input_width]
    weight_out = attention_all[:, input_width:]
    biases = lax.all_gather(jnp.concatenate([query_bias, key_bias, value_bias]), AXIS, axis=0, tiled=False).astype(F32)
    cut = (rows, rows + key_bias.shape[0])
    bias_input = jnp.concatenate(
        [biases[:, : cut[0]].reshape(-1), biases[:, cut[0] : cut[1]].reshape(-1), biases[:, cut[1] :].reshape(-1)]
    )

    def spread(weight):
        pieces = weight.reshape(rows, GROUP, shard).transpose(1, 0, 2)
        got = lax.all_to_all(pieces, AXIS, split_axis=0, concat_axis=0, tiled=True, axis_index_groups=token_groups)
        full = lax.all_gather(got, AXIS, axis=0, tiled=False, axis_index_groups=plane_groups)
        full = full.reshape(plane, lines, 2, rows, shard).transpose(1, 0, 2, 3, 4)
        return full.reshape(count * rows, shard)

    weight_gate = spread(scaled(gate_weight, gain_two))
    weight_up = spread(scaled(up_weight, gain_two))
    weight_down = spread(down_weight)

    live_rows = (segment >= 0).astype(F32)[:, None]
    slot_order = jnp.arange(length)
    visible = (segment[:, None] == segment[None, :]) & (slot_order[None, :] <= slot_order[:, None])
    cosine_table, sine_table = tables(position)
    token_float = tokens.astype(F32)
    scale_one = lax.rsqrt(jnp.mean(token_float * token_float, axis=-1, keepdims=True) + EPSILON)
    normed_one = (token_float * scale_one).astype(BF16)
    projected = dot(normed_one, weight_input, (1, 0)) + bias_input
    queries = rotary(projected[:, :width].reshape(length, H, HD), cosine_table, sine_table).astype(BF16)
    queries = queries.reshape(length, KV, heads_per_key, HD)
    key_rows = rotary(
        projected[:, width : width + key_width].reshape(length, KV, HD), cosine_table, sine_table
    ).astype(BF16)
    value_rows = projected[:, width + key_width :].astype(BF16).reshape(length, KV, HD)
    scores = jnp.einsum("qkgd,skd->kgqs", queries, key_rows, preferred_element_type=F32) * factor
    probs = jax.nn.softmax(jnp.where(visible, scores, -jnp.inf), axis=-1)
    probs_low = probs.astype(BF16)
    mixed_heads = jnp.einsum("kgqs,skd->qkgd", probs_low, value_rows, preferred_element_type=F32)
    mixed_heads = mixed_heads.reshape(length, H * HD).astype(BF16)
    hidden_state = token_float + dot(mixed_heads, weight_out, (1, 1))
    scale_two = lax.rsqrt(jnp.mean(hidden_state * hidden_state, axis=-1, keepdims=True) + EPSILON)
    normed_two = (hidden_state * scale_two).astype(BF16)
    upstream = cotangent.astype(F32) * live_rows
    group_tokens = lax.all_gather(normed_two, AXIS, axis=0, tiled=True, axis_index_groups=token_groups)
    group_upstream = lax.all_gather(
        upstream.astype(BF16), AXIS, axis=0, tiled=True, axis_index_groups=token_groups
    )

    gate_value = dot(group_tokens, weight_gate, (1, 0))
    up_value = dot(group_tokens, weight_up, (1, 0))
    sigmoid_gate = jax.nn.sigmoid(gate_value)
    activated = (gate_value * sigmoid_gate * up_value).astype(BF16)
    act_grad = dot(group_upstream, weight_down, (1, 0))
    gate_grad = (act_grad * up_value * sigmoid_gate * (1.0 + gate_value * (1.0 - sigmoid_gate))).astype(BF16)
    up_grad = (act_grad * gate_value * sigmoid_gate).astype(BF16)

    def fold_tokens(term):
        return lax.psum_scatter(
            term.astype(BF16), AXIS, scatter_dimension=0, tiled=True, axis_index_groups=token_groups
        ).astype(F32)

    weighted_two = fold_tokens(dot(gate_grad, weight_gate, (1, 1)) + dot(up_grad, weight_up, (1, 1)))
    feed_out = fold_tokens(dot(activated, weight_down, (1, 1)))
    block_output = (live_rows * (hidden_state + feed_out)).astype(BF16)

    def fold_feed(term):
        pieces = term.astype(BF16).reshape(lines, plane, 2, rows, shard).transpose(1, 0, 2, 3, 4)
        pieces = lax.all_to_all(
            pieces.reshape(plane, GROUP * rows, shard), AXIS, split_axis=0, concat_axis=0, tiled=True,
            axis_index_groups=plane_groups,
        )
        mine = jnp.sum(pieces.astype(F32), axis=0).astype(BF16).reshape(GROUP, rows, shard)
        mine = lax.all_to_all(mine, AXIS, split_axis=0, concat_axis=0, tiled=True, axis_index_groups=token_groups)
        return mine.transpose(1, 0, 2).reshape(rows, hidden).astype(F32)

    down_sum = fold_feed(dot(group_upstream, activated, (0, 0)))
    gate_raw = fold_feed(dot(group_tokens, gate_grad, (0, 0)))
    up_raw = fold_feed(dot(group_tokens, up_grad, (0, 0)))
    gain_two_sum = jnp.sum(gate_raw * gate_weight.astype(F32) + up_raw * up_weight.astype(F32), axis=1)

    hidden_grad = upstream + norm_back(weighted_two, hidden_state, scale_two)
    branch_grad = hidden_grad.astype(BF16)
    mixed_grad = dot(branch_grad, weight_out, (1, 0)).astype(BF16).reshape(length, KV, heads_per_key, HD)
    prob_grad = jnp.einsum("qkgd,skd->kgqs", mixed_grad, value_rows, preferred_element_type=F32)
    value_grad = jnp.einsum("kgqs,qkgd->skd", probs_low, mixed_grad, preferred_element_type=F32)
    score_grad = probs * (prob_grad - jnp.sum(probs * prob_grad, axis=-1, keepdims=True))
    score_grad = score_grad.astype(BF16)
    query_grad = jnp.einsum("kgqs,skd->qkgd", score_grad, key_rows, preferred_element_type=F32) * factor
    key_grad = jnp.einsum("kgqs,qkgd->skd", score_grad, queries, preferred_element_type=F32) * factor
    query_low = rotary_back(query_grad.reshape(length, H, HD), cosine_table, sine_table)
    key_low = rotary_back(key_grad, cosine_table, sine_table)
    input_low = jnp.concatenate(
        [query_low.reshape(length, width), key_low.reshape(length, key_width), value_grad.reshape(length, key_width)],
        axis=1,
    ).astype(BF16)
    attention_term = jnp.concatenate(
        [dot(normed_one, input_low, (0, 0)), dot(branch_grad, mixed_heads, (0, 0))], axis=1
    ).astype(BF16)
    attention_sum = lax.psum_scatter(attention_term, AXIS, scatter_dimension=0, tiled=True).astype(F32)
    bias_sum = lax.psum(jnp.sum(input_low, axis=0, dtype=F32), AXIS)
    input_raw = attention_sum[:, :input_width]
    out_sum = attention_sum[:, input_width:]
    input_sum = input_raw * gain_one
    own_weight = jnp.concatenate([query_weight, key_weight, value_weight], axis=1).astype(F32)
    gain_one_sum = jnp.sum(input_raw * own_weight, axis=1)
    weighted_one = dot(input_low, weight_input, (1, 1))
    token_grad = hidden_grad + norm_back(weighted_one, token_float, scale_one)
    query_bias_sum = lax.dynamic_slice(bias_sum, (me * rows,), (rows,))
    value_bias_sum = lax.dynamic_slice(
        bias_sum, (width + key_width + me * value_bias.shape[0],), (value_bias.shape[0],)
    )
    return (
        block_output,
        token_grad.astype(BF16),
        gain_one_sum,
        input_sum[:, :width],
        query_bias_sum,
        input_sum[:, width : width + key_width],
        bias_sum[width : width + key_width],
        input_sum[:, width + key_width :],
        value_bias_sum,
        out_sum,
        gain_two_sum,
        gate_raw * gain_two,
        up_raw * gain_two,
        down_sum,
    )


def mega(rows, plane, *refs):
    (
        x_in, cot_in, pos_in, seg_in, aux_in, wq_in, wk_in, wv_in, wo_in, wg_in, wu_in, wd_in,
        o1, o2, o3, o4, o5, fo_out, bg_out, tg_out, bo_out,
        xs, xh, aux, ids, sa, wgs, wus, w1, w2, w3, w4, w5, g5,
        r1, r2, r3, r4, hn, gb, gt, up, act, pb, rb, rt,
        zb, zr, hs, dz, ob, qr, kr, vr, pr, dob, dq, cos, sin, msk, bias_in, ba, bp, bgp, bsum,
        lsem, a_s, a_r, p_s, p_r, r_s, r_r, o_s, o_r, t_s, t_r, d_s, d_r, b_s, b_r, e_s, e_r, credit, pair_credit, line_credit,
    ) = refs
    weights = (w1, w2, w3, w4, w5)
    block, width = x_in.shape
    shard = w3.shape[1]
    half = w2.shape[1]
    heads = half // HD
    every = pl.ds(0, shard)
    parts = (
        (w1, pl.ds(0, 512), r1, o1), (w2, pl.ds(0, half), r2, o2), (w3, every, r3, o3), (w4, every, r4, o4),
        (g5, every, r4, o5), (w1, pl.ds(512, half - 512), r1, o1), (w1, pl.ds(half, 2 * HD), r1, o1),
    )
    strip = width // LINES
    hidden = wg_in.shape[1]
    short = GROUP * shard - hidden
    factor = 1.0 / math.sqrt(HD)

    me = lax.axis_index(AXIS)
    c = lax.rem(me, 2)
    p = lax.rem(lax.div(me, 2), plane)
    z = lax.div(me, 2 * plane)
    f = z * 2 + c
    xbit, ybit = lax.rem(p, 2), lax.div(p, 2)
    px = p + 1 - 2 * xbit
    py = p + 2 - 4 * ybit
    pd = px + 2 - 4 * ybit
    zlow, zhigh = lax.rem(z, 2), lax.div(z, 2)
    inner = zlow + zhigh - 2 * zlow * zhigh

    def flip(bit, on):
        return bit + on - 2 * bit * on

    def zf(high, low):
        return flip(zhigh, high) * 2 + flip(zlow, low)

    def zj(j):
        if isinstance(j, int):
            return zf(j // 2, j % 2)
        return zf(lax.div(j, 2), lax.rem(j, 2))

    def dev(zz, pp, cc):
        return (zz * plane + pp) * 2 + cc

    sib, xnb, ynb = dev(z, p, 1 - c), dev(z, px, c), dev(z, py, c)

    def unit(zz, pp):
        return pl.ds(pl.multiple_of((zz * plane + pp) * 2 * rows, 16), 2 * rows)

    def piece(zz, pp, cc):
        return pl.ds(pl.multiple_of(((zz * plane + pp) * 2 + cc) * rows, 16), rows)

    def slot(s):
        return pl.ds(pl.multiple_of(s * 2 * rows, 16), 2 * rows)

    def tokens_of(zz, cc):
        return pl.ds(pl.multiple_of((zz * 2 + cc) * block, block), block)

    def chunk_of(zz):
        return pl.ds(pl.multiple_of(zz * 2 * block, 2 * block), 2 * block)

    def remote(src, dst, send, recv, target):
        return pltpu.make_async_remote_copy(
            src_ref=src, dst_ref=dst, send_sem=send, recv_sem=recv,
            device_id=(target,), device_id_type=pl.DeviceIdType.MESH,
        )

    def dot_nn(a, b):
        return lax.dot_general(a, b, (((1,), (0,)), ((), ())), preferred_element_type=F32)

    def dot_nt(a, b):
        return lax.dot_general(a, b, (((1,), (1,)), ((), ())), preferred_element_type=F32)

    def dot_tn(a, b):
        return lax.dot_general(a, b, (((0,), (0,)), ((), ())), preferred_element_type=F32)

    pending = {}

    def begin(key, copy, leave=True, arrive=True):
        copy.start()
        if leave:
            pending[key + ("leave",)] = copy.wait_send
        if arrive:
            pending[key + ("arrive",)] = copy.wait_recv

    def left(ref, send):
        remote(ref, ref, send, send, sib).wait_send()

    def landed(ref, recv):
        remote(ref, ref, recv, recv, sib).wait_recv()

    def begin_local(key, copy):
        copy.start()
        pending[key] = copy.wait

    def settle(*keys):
        for key in keys:
            pending.pop(key)()

    def settle_all(match):
        settle(*[key for key in pending if match(key)])

    def local(n, src, dst):
        return pltpu.make_async_copy(src, dst, lsem.at[n])

    def signal(semaphore, target):
        pl.semaphore_signal(semaphore, inc=1, device_id=(target,), device_id_type=pl.DeviceIdType.MESH)

    def source(k, ff, cc):
        if k == 0:
            return sa.at[cc]
        if k == 1:
            return wo_in.at[:, pl.ds(pl.multiple_of(cc * half, 128), half)]
        start = pl.multiple_of((ff * (shard // 128) - lax.div(ff, GROUP - 1) * (short // 128)) * 128, 128)
        return (wgs, wus, wd_in)[k - 2].at[:, pl.ds(start, shard)]

    def a_copy(k, j):
        zz, cc = zj(j // 2 if isinstance(j, int) else lax.div(j, 2)), flip(c, j % 2 if isinstance(j, int) else lax.rem(j, 2))
        return remote(
            source(k, zz * 2 + cc, cc), weights[k].at[piece(z, p, c)], a_s.at[k],
            a_r.at[k, j // 2 if isinstance(j, int) else lax.div(j, 2)], dev(zz, p, cc),
        )

    def a_unit(k, j):
        return weights[k].at[unit(zj(j), p)]

    def a_pass(k, j):
        return remote(a_unit(k, j), a_unit(k, j), a_s.at[5 + k], a_r.at[k, 5 - j], dev(zj(1), p, c))

    def a_pair(k):
        begin_local(("a_own", k), local(11 + k, source(k, f, c), weights[k].at[piece(z, p, c)]))
        a_copy(k, 1).start()

    def a_line(k):
        through = k < 2
        for j in (2, 3):
            a_copy(k, j).start()
        if through:
            for j in (0, 1):
                a_copy(k, 4 + 2 * inner + j).start()
        else:
            for j in (4, 5, 6, 7):
                a_copy(k, j).start()
        pending["a", k, "leave"] = lambda: left(weights[k].at[pl.ds(0, (5 if through else 7) * rows)], a_s.at[k])
        if through:

            def passed():
                @pl.when(inner == 1)
                def _():
                    left(weights[k].at[pl.ds(0, 4 * rows)], a_s.at[5 + k])

            pending["a_pass", k, "leave"] = passed

    def a_wait(k, n):
        if n == 0:
            settle(("a_own", k))
            landed(weights[k].at[piece(z, p, 1 - c)], a_r.at[k, 0])
            return 0
        j = n if k >= 2 or n == 1 else (2 + inner if n == 2 else 3 - inner)
        landed(a_unit(k, j), a_r.at[k, j])
        if k < 2 and n > 1:

            @pl.when(inner == 1)
            def _():
                a_pass(k, j).start()

        return j

    def ag_copy(k, s, j):
        if s < 4:
            part, target = unit(zj(j), p), xnb
        elif s < 8:
            part, target = unit(zj(j), p), ynb
        elif s < 10:
            part, target = unit(zj(j), px), ynb
        else:
            part, target = unit(zj(j), py), xnb
        low = isinstance(j, int) and j < 2
        index = j if (s < 4 and low) or (4 <= s < 8 and not low) else 4
        return remote(weights[k].at[part], weights[k].at[part], p_s.at[k], p_r.at[k, index], target)

    def ag_unit(k, n):
        j = a_wait(k, n)
        ag_copy(k, 0, j).start()
        ag_copy(k, 4, j).start()

    def ag_send(k, first=0):
        for n in range(first, LINES):
            ag_unit(k, n)
        pending["ag", k, "leave"] = lambda: left(weights[k].at[pl.ds(0, 24 * rows)], p_s.at[k])

    def ag_relay(k):
        for j in range(4):
            ag_copy(k, 0 if j < 2 else 4, j).wait_recv()
            ag_copy(k, 8 + j, j).start()

    def ag_finish(k):
        landed(weights[k].at[pl.ds(0, 16 * rows)], p_r.at[k, 4])

    def ag_sent(k):
        settle(("ag", k, "leave"))
        if k < 2:
            settle(("a_pass", k, "leave"))

    def tok_copy(which, kind, j):
        buf = (hn, gb)[which]
        part = tokens_of(zj(0 if kind == "own" else j), c)
        if kind == "own":
            send, recv, target = t_s.at[which, 0], j, dev(zj(j), p, c)
        elif kind == "pair":
            send, recv, target = t_s.at[which, 0], 4 + j, sib
        else:
            send, recv, target = t_s.at[which, 1], 5 - j, dev(zj(1), p, c)
        return remote(buf.at[part], buf.at[part], send, t_r.at[which, recv], target)

    def tok_send(which):
        tok_copy(which, "own", 1).start()
        tok_copy(which, "own", 2 + inner).start()
        tok_copy(which, "pair", 0).start()

        def sent():
            buf = (hn, gb)[which]
            left(buf.at[pl.ds(0, 6 * block)], t_s.at[which, 0])

            @pl.when(inner == 1)
            def _():
                left(buf.at[pl.ds(0, 2 * block)], t_s.at[which, 1])

        pending["tok", which, "leave"] = sent

    def tok_forward(which):
        for j in (1, 2 + inner, 3 - inner):
            tok_copy(which, "own", j).wait_recv()
            if not isinstance(j, int):

                @pl.when(inner == 1)
                def _():
                    tok_copy(which, "pass", j).start()

            tok_copy(which, "pair", j).start()

    def tok_finish(which):
        for j in range(4):
            tok_copy(which, "pair", j).wait_recv()

    def e_copy(n, src, dst):
        return remote(src, dst, e_s.at[n], e_r.at[n], sib)

    own_rows = pl.ds(pl.multiple_of(c * block, block), block)

    def bias_in_copy(s):
        zz, cc = zj(s // 2), flip(c, s % 2)
        return remote(bias_in.at[cc], ba.at[f], b_s.at[0], b_r.at[0], dev(zz, p, cc))

    def bias_plane_copy(group, n, buf):
        target = dev(z, (px, py, pd)[n], c)
        return remote(buf.at[p], buf.at[p], b_s.at[group], b_r.at[group], target)

    def bias_out_copy(s):
        zz, cc = zj(s // 2), flip(c, s % 2)
        return remote(bsum, bg_out.at[f], b_s.at[3], b_r.at[3], dev(zz, p, cc))

    def bias_note(group, buf, count):
        pending["bias", group, "leave"] = lambda: left(buf.at[pl.ds(0, count)], b_s.at[group])
        pending["bias", group, "arrive"] = lambda: landed(buf.at[pl.ds(0, count)], b_r.at[group])

    def rs_copy(k, s, h):
        ref, cols, land = parts[k][:3]
        zz = zf((0, 1, 1, 0, 0, 1)[s], h)
        part = unit(zz, (pd, pd, px, py, px, py)[s])
        place = (0, 2, 6, 8, 4, 10)[s] + h
        target = (ynb, xnb, xnb, ynb, xnb, ynb)[s]
        return remote(ref.at[part, cols], land.at[slot(place), cols], r_s.at[k], r_r.at[k, (0, 2, 6, 4, 4, 6)[s] + h], target)

    def rs_step(k, left_ref, right_ref, h):
        ref, cols = parts[k][:2]
        for high in (1, 0):
            at = pl.multiple_of(zf(high, h) * strip, 128)
            ref[pl.ds(at, strip), cols] = dot_tn(left_ref[:, pl.ds(at, strip)], right_ref[:, cols]).astype(BF16)
            for s in ((0, 3), (1, 2))[high]:
                rs_copy(k, s, h).start()
        pending["rs", k, "leave"] = lambda: left(ref.at[pl.ds(0, 24 * rows), cols], r_s.at[k])

    def rs_start(k, left_ref, right_ref, steps=(0, 1)):
        @pl.loop(steps[0], steps[-1] + 1)
        def both(i):
            rs_step(k, left_ref, right_ref, 1 - i)

    def rs_middle(k):
        ref, cols, land = parts[k][:3]

        @pl.loop(0, 2)
        def both(i):
            h = 1 - i
            for high in (1, 0):
                rs_copy(k, high, h).wait_recv()
                part = unit(zf(high, h), (px, py)[high])
                got = land[slot(2 * high + h), cols]
                ref[part, cols] = (ref[part, cols].astype(F32) + got.astype(F32)).astype(BF16)
                rs_copy(k, 4 + high, h).start()

    def out_copy(k, j, other):
        ref, cols, _, out = parts[k]
        zz, cc = zj(j), flip(c, other)
        return remote(ref.at[piece(zz, p, cc), cols], out.at[f, :, cols], o_s.at[k], o_r.at[k], dev(zz, p, cc))

    def rs_finish(k):
        ref, cols, land, out = parts[k]
        for j in (3, 1, 2, 0):
            h, high = j % 2, j // 2
            landed(land.at[pl.ds(0, 4 * rows), cols], r_r.at[k, 4 + j])
            part = unit(zj(j), p)
            got = land[slot(4 + j), cols].astype(F32) + land[slot(8 + j), cols].astype(F32)
            ref[part, cols] = (ref[part, cols].astype(F32) + got).astype(BF16)
            out_copy(k, j, 1).start()
            if j == 0:
                begin_local(("out_own", k), local(17 + k, ref.at[piece(z, p, c), cols], out.at[f, :, cols]))
            else:
                out_copy(k, j, 0).start()
        pending["out", k, "leave"] = lambda: left(ref.at[pl.ds(0, 7 * rows), cols], o_s.at[k])
        pending["out", k, "arrive"] = lambda: landed(ref.at[pl.ds(0, 7 * rows), cols], o_r.at[k])

    def pair_copy(which, j):
        return remote(
            pb.at[tokens_of(zj(j), 1 - c)], rb.at[pl.ds(pl.multiple_of(j * block, block), block)],
            d_s.at[which, 0], d_r.at[which, j], sib,
        )

    def line_copy(which, j):
        dst = fo_out.at[1] if which == 1 and isinstance(j, int) and j == 1 else rt.at[j - 1]
        return remote(
            pb.at[tokens_of(zj(j), c)], dst, d_s.at[which, 1], d_r.at[which, 4 + j], dev(zj(1), p, c)
        )

    def far_copy(which, j):
        dst = fo_out.at[2] if which == 1 else rt.at[3]
        return remote(pb.at[tokens_of(zj(j), c)], dst, d_s.at[which, 1], d_r.at[which, 4], dev(zj(j), p, c))

    def far_add(which, j):
        @pl.when(inner == 1)
        def _():
            line_copy(which, 5 - j).wait_recv()
            part = tokens_of(zj(j), c)
            pb[part] = (pb[part].astype(F32) + rt[4 - j].astype(F32)).astype(BF16)
            far_copy(which, j).start()

    def pair_add(which, j):
        pair_copy(which, j).wait_recv()
        part = tokens_of(zj(j), c)
        got = rb[pl.ds(pl.multiple_of(j * block, block), block)].astype(F32)
        pb[part] = (pb[part].astype(F32) + got).astype(BF16)

    def sum_loop(which, compute, beside=None):
        @pl.loop(0, LINES)
        def chunk(i):
            j = LINES - 1 - i
            if beside is not None:
                beside(i)
            compute(chunk_of(zj(j)))
            pair_copy(which, j).start()

            @pl.when((i > 0) & (i < LINES - 1))
            def _():
                pair_add(which, j + 1)

                @pl.when(inner == 0)
                def _():
                    line_copy(which, j + 1).start()

            @pl.when(i == LINES - 1)
            def _():
                pair_add(which, 1)
                line_copy(which, 1).start()

        pair_add(which, 0)

        def sent():
            left(pb.at[pl.ds(0, LINES * block)], d_s.at[which, 0])
            left(pb.at[pl.ds(0, 3 * block)], d_s.at[which, 1])

        pending["sum", which, "leave"] = sent
        pending["sum", which, 1, "arrive"] = lambda: line_copy(which, 1).wait_recv()
        pending["sum", which, 2, "arrive"] = lambda: far_copy(which, 2).wait_recv()

    def rope(v, b):
        return v * cos[b] + pltpu.roll(v, HD // 2, 1) * sin[b]

    def rope_back(v, b):
        return v * cos[b] + pltpu.roll(v * sin[b], HD // 2, 1)

    row_id = lax.broadcasted_iota(jnp.int32, (block, block), 0)
    lane_id = lax.broadcasted_iota(jnp.int32, (block, block), 1)

    def column(row):
        return jnp.sum(jnp.where(row_id == lane_id, row, 0.0), axis=1, keepdims=True)

    tile = 3 * HD
    last = lax.div(f, GROUP - 1)
    keep = jnp.where(lax.broadcasted_iota(jnp.int32, (1, tile), 1) < last * short, 0.0, 1.0)

    def enter():
        begin_local(("aux",), local(0, aux_in, aux.at[c]))
        begin_local(("pos",), local(25, pos_in, ids.at[0]))
        begin_local(("seg",), local(22, seg_in, ids.at[1]))
        begin_local(("x",), local(1, x_in, xs.at[c]))
        for side in range(2):
            begin_local(("wq", side), local(2 + side, wq_in.at[:, pl.ds(side * half, half)], sa.at[side, :, pl.ds(0, half)]))
            begin_local(("wk", side), local(4 + side, wk_in.at[:, pl.ds(side * HD, HD)], sa.at[side, :, pl.ds(half, HD)]))
            begin_local(("wv", side), local(6 + side, wv_in.at[:, pl.ds(side * HD, HD)], sa.at[side, :, pl.ds(half + HD, HD)]))
        begin_local(("wg",), local(8, wg_in, wgs))
        begin_local(("wu",), local(9, wu_in, wus))
        begin_local(("cot",), local(10, cot_in, gb.at[tokens_of(z, c)]))
        barrier = pltpu.get_barrier_semaphore()
        friends = [dev(zj(j // 2), p, flip(c, j % 2)) for j in range(1, GROUP)] + [xnb, ynb, dev(z, pd, c)]
        for friend in friends:
            signal(barrier, friend)
        settle(("aux",), ("pos",), ("seg",), ("x",), *[(name, side) for side in range(2) for name in ("wq", "wk", "wv")])
        aux[c, 0:1] = ids[0].astype(F32)
        aux[c, 1:2] = ids[1].astype(F32)
        gain_one = column(aux[c][2:3])[:rows]
        for side in range(2):
            sa[side] = (sa[side].astype(F32) * gain_one).astype(BF16)
        pl.semaphore_wait(barrier, len(friends))

    def exchange_inputs():
        begin(("e", 0), e_copy(0, aux.at[c], aux.at[c]))
        begin(("e", 1), e_copy(1, xs.at[c], xs.at[c]))

    def bias_first():
        step = lax.rem(me, 2 * plane * LINES // 2)
        info = aux[c]

        def placed(row, count, size):
            wide = jnp.concatenate([row] + [jnp.zeros_like(row)] * (size // HD - 1), axis=1) if size > HD else row
            wide = jnp.broadcast_to(wide, (8, size))
            return pltpu.roll(wide, step * count, 1)[0:1]

        own = jnp.concatenate(
            [placed(info[4:5], rows, half), placed(info[5:6], rows // KEYS, HD), placed(info[6:7], rows // KEYS, HD)], axis=1
        )
        side = lax.div(me, plane * LINES)
        bias_in[side] = own
        bias_in[1 - side] = jnp.zeros_like(own)
        begin_local(("bias_own",), local(16, bias_in.at[c], ba.at[f]))
        for s in range(1, GROUP):
            bias_in_copy(s).start()
        bias_note(0, ba, GROUP - 1)

    def bias_second():
        settle(("bias_own",), ("bias", 0, "arrive"))
        total = ba[0]
        for s in range(1, GROUP):
            total = total + ba[s]
        bp[p] = total
        for n in range(3):
            bias_plane_copy(1, n, bp).start()
        bias_note(1, bp, 3)

    def scale_feed():
        gain_two = column(aux[c][3:4])[:rows]
        for name, ref in (("wg", wgs), ("wu", wus)):
            settle((name,))
            for n in range(0, hidden, 1792):
                cols = pl.ds(n, min(1792, hidden - n))
                ref[:, cols] = (ref[:, cols].astype(F32) * gain_two).astype(BF16)

    def mask_upstream():
        settle(("cot",))
        live = jnp.where(column(aux[c][1:2]) >= 0.0, 1.0, 0.0)
        gb[tokens_of(z, c)] = (gb[tokens_of(z, c)].astype(F32) * live).astype(BF16)

    def norm_tokens():
        settle(("e", 0, "arrive"), ("e", 1, "arrive"))
        lanes = lax.broadcasted_iota(jnp.int32, (1, HD), 1)
        freq_index = jnp.where(lanes < HD // 2, lanes, lanes - HD // 2).astype(F32)
        frequency = jnp.exp(freq_index * (-2.0 * math.log(ROPE_BASE) / HD))
        for b in range(2):
            values = xs[b].astype(F32)
            scale = lax.rsqrt(jnp.mean(values * values, axis=1, keepdims=True) + EPSILON)
            xh[pl.ds(b * block, block)] = (values * scale).astype(BF16)
            info = aux[b]
            angles = column(info[0:1]) * frequency
            cos[b] = jnp.cos(angles)
            sine = jnp.sin(angles)
            sin[b] = jnp.where(lane_id < HD // 2, -sine, sine)
            same = column(info[1:2]) == info[1:2]
            msk[b] = jnp.where(same & (lane_id <= row_id), 1.0, 0.0)

    def project():
        settle(("bias", 1, "arrive"))
        bias_row = (bp[0] + bp[1]) + (bp[2] + bp[3])
        for n in range(heads // 2 + 1):
            cols = pl.ds(n * 2 * HD, 2 * HD)
            out = dot_nn(xh[...], w1[:, cols]) + bias_row[:, n * 2 * HD : (n + 1) * 2 * HD]
            for b in range(2):
                part = out[b * block : (b + 1) * block]
                if n < heads // 2:
                    for i in range(2):
                        qr[b, pl.ds((2 * n + i) * block, block)] = rope(part[:, i * HD : (i + 1) * HD], b).astype(BF16)
                else:
                    kr[b] = rope(part[:, :HD], b).astype(BF16)
                    vr[b] = part[:, HD:].astype(BF16)

    def attend():
        for b in range(2):
            scores = dot_nt(qr[b], kr[b]) * factor
            scores = jnp.where(msk[b][None] > 0.0, scores.reshape(heads, block, block), -jnp.inf)
            weight = jnp.exp(scores - jnp.max(scores, axis=-1, keepdims=True))
            weight = weight / jnp.sum(weight, axis=-1, keepdims=True)
            weight = weight.reshape(heads * block, block)
            pr[b] = weight
            mixed = dot_nn(weight.astype(BF16), vr[b]).astype(BF16)
            for i in range(heads):
                ob[pl.ds(b * block, block), pl.ds(i * HD, HD)] = mixed[i * block : (i + 1) * block]

    def attend_out():
        for n in range(0, width, 512):
            part = dot_nt(ob[...], w2[pl.ds(n, 512), :])
            zb[0, :, pl.ds(n, 512)] = part[:block]
            zb[1, :, pl.ds(n, 512)] = part[block:]
        begin(("e", 2), e_copy(2, zb.at[1 - c], zr))

    def hidden_state():
        settle(("e", 2, "arrive"))
        state = xs[c].astype(F32) + zb[c] + zr[...]
        hs[...] = state
        scale_two = lax.rsqrt(jnp.mean(state * state, axis=1, keepdims=True) + EPSILON)
        hn[tokens_of(z, c)] = (state * scale_two).astype(BF16)

    def feed_forward(first, end):
        @pl.loop(first, end)
        def chunk(i):
            rows_here = chunk_of(zj(i))
            left = hn[rows_here]
            for n in range(0, shard, tile):
                cols = pl.ds(n, tile)
                gate = dot_nn(left, w3[:, cols])
                lift = dot_nn(left, w4[:, cols])
                if n == 0:
                    gate = gate * keep
                    lift = lift * keep
                gt[rows_here, cols] = gate.astype(BF16)
                up[rows_here, cols] = lift.astype(BF16)
                act[rows_here, cols] = (gate * jax.nn.sigmoid(gate) * lift).astype(BF16)

    def feed_backward(together=False):
        def beside(i):
            @pl.when(lax.rem(i, 2) == 0)
            def _():
                rs_step(4, gb, act, 1 - lax.div(i, 2))

        def compute(rows_here):
            left = gb[rows_here]
            for n in range(0, shard, tile):
                cols = pl.ds(n, tile)
                d_act = dot_nn(left, w5[:, cols])
                gate = gt[rows_here, cols].astype(F32)
                lift = up[rows_here, cols].astype(F32)
                sig = jax.nn.sigmoid(gate)
                gt[rows_here, cols] = (d_act * lift * sig * (1.0 + gate * (1.0 - sig))).astype(BF16)
                up[rows_here, cols] = (d_act * gate * sig).astype(BF16)
            for n in range(0, width, 512):
                part = pl.ds(n, 512)
                back = dot_nt(gt[rows_here], w3[part, :]) + dot_nt(up[rows_here], w4[part, :])
                pb[rows_here, part] = back.astype(BF16)

        sum_loop(0, compute, beside if together else None)
        signal(pair_credit, sib)

    def line_ready():
        @pl.when(inner == 1)
        def _():
            signal(line_credit, dev(zj(1), p, c))

    def feed_output():
        settle(("sum", 0, "leave"))
        pl.semaphore_wait(pair_credit, 1)

        @pl.when(inner == 0)
        def _():
            pl.semaphore_wait(line_credit, 1)

        def compute(rows_here):
            for n in range(0, width, 512):
                part = pl.ds(n, 512)
                pb[rows_here, part] = dot_nt(act[rows_here], w5[part, :]).astype(BF16)

        sum_loop(1, compute)

    def block_result():
        settle(("sum", 1, 1, "arrive"), ("sum", 1, 2, "arrive"))
        for n in range(2):
            begin_local(("fetch", n), local(2 + n, fo_out.at[1 + n], rb.at[pl.ds(n * block, block)]))
        settle(("fetch", 0), ("fetch", 1))
        live = jnp.where(column(aux[c][1:2]) >= 0.0, 1.0, 0.0)
        total = hs[...] + pb[tokens_of(z, c)].astype(F32)
        total = total + rb[pl.ds(0, block)].astype(F32) + rb[pl.ds(block, block)].astype(F32)
        xs[1 - c] = (live * total).astype(BF16)
        begin_local(("bo",), local(1, xs.at[1 - c], bo_out))

    def landing_free():
        for target in (xnb, ynb):
            signal(credit, target)

    def landing_wait():
        pl.semaphore_wait(credit, 2)

    def hidden_gradient():
        settle(("sum", 0, 1, "arrive"), ("sum", 0, 2, "arrive"))
        weighted = pb[tokens_of(z, c)].astype(F32) + rt[0].astype(F32) + rt[3].astype(F32)
        state = hs[...]
        scale_two = lax.rsqrt(jnp.mean(state * state, axis=1, keepdims=True) + EPSILON)
        spread = jnp.mean(weighted * state, axis=1, keepdims=True)
        grad = (
            gb[tokens_of(z, c)].astype(F32)
            + scale_two * weighted
            - state * (scale_two * scale_two * scale_two) * spread
        )
        dz[own_rows] = grad.astype(BF16)
        begin(("e", 3), e_copy(3, dz.at[own_rows], dz.at[own_rows]))

    def attend_out_back():
        settle(("e", 3, "arrive"))
        for n in range(0, heads, 2):
            part = dot_nn(dz[...], w2[:, pl.ds(n * HD, 2 * HD)]).astype(BF16)
            for b in range(2):
                for i in range(2):
                    dob[b, pl.ds((n + i) * block, block)] = part[b * block : (b + 1) * block, i * HD : (i + 1) * HD]

    def attend_back():
        for b in range(2):
            weight = pr[b]
            d_weight = dot_nt(dob[b], vr[b])
            d_score = weight * (d_weight - jnp.sum(weight * d_weight, axis=-1, keepdims=True))
            d_score = d_score.astype(BF16)
            d_query = dot_nn(d_score, kr[b]) * factor
            here = pl.ds(b * block, block)
            for i in range(heads):
                dq[here, pl.ds(i * HD, HD)] = rope_back(d_query[i * block : (i + 1) * block], b).astype(BF16)
            dq[here, pl.ds(half, HD)] = rope_back(dot_tn(d_score, qr[b]) * factor, b).astype(BF16)
            dq[here, pl.ds(half + HD, HD)] = dot_tn(weight.astype(BF16), dob[b]).astype(BF16)

    def project_back():
        settle(("e", 2, "leave"))
        for n in range(0, width, 512):
            part = dot_nt(dq[...], w1[pl.ds(n, 512), :])
            zb[0, :, pl.ds(n, 512)] = part[:block]
            zb[1, :, pl.ds(n, 512)] = part[block:]
        begin(("e", 4), e_copy(4, zb.at[1 - c], zr))

    def bias_back():
        bgp[p] = jnp.sum(dq[...].astype(F32), axis=0, keepdims=True)
        for n in range(3):
            bias_plane_copy(2, n, bgp).start()
        bias_note(2, bgp, 3)

    def bias_last():
        settle(("bias", 2, "arrive"))
        bsum[...] = (bgp[0] + bgp[1]) + (bgp[2] + bgp[3])
        begin_local(("bias_sum",), local(24, bsum, bg_out.at[f]))
        for s in range(1, GROUP):
            bias_out_copy(s).start()
        bias_note(3, ba, GROUP - 1)

    def token_gradient():
        settle(("e", 4, "arrive"))
        weighted = zb[c] + zr[...]
        values = xs[c].astype(F32)
        scale = lax.rsqrt(jnp.mean(values * values, axis=1, keepdims=True) + EPSILON)
        spread = jnp.mean(weighted * values, axis=1, keepdims=True)
        grad = dz[own_rows].astype(F32) + scale * weighted - values * (scale * scale * scale) * spread
        settle(("e", 1, "leave"))
        xs[c] = grad.astype(BF16)
        begin_local(("tg",), local(0, xs.at[c], tg_out))

    enter()
    exchange_inputs()
    a_pair(0)
    a_line(0)
    bias_first()
    a_pair(1)
    a_line(1)
    ag_unit(0,0)
    a_pair(4)
    scale_feed()
    a_pair(2)
    a_pair(3)
    ag_unit(0,1)
    ag_unit(1,0)
    mask_upstream()
    ag_unit(2,0)
    ag_unit(3,0)
    ag_send(0,2)
    a_line(2)
    norm_tokens()
    ag_relay(0)
    bias_second()
    ag_send(1,1)
    a_line(3)
    ag_finish(0)
    project()
    ag_relay(1)
    ag_send(2,1)
    attend()
    ag_finish(1)
    attend_out()
    hidden_state()
    tok_send(0)
    ag_send(3,1)
    a_line(4)
    tok_send(1)
    ag_relay(2)
    ag_relay(3)
    tok_forward(0)
    ag_send(4, 0)
    tok_finish(0)
    ag_finish(2)
    ag_finish(3)
    feed_forward(0, LINES)
    ag_relay(4)
    tok_forward(1)
    ag_finish(4)
    tok_finish(1)
    feed_backward(True)
    far_add(0, 2)
    rs_middle(4)
    ag_sent(2)
    rs_start(2, hn, gt)
    far_add(0, 3)
    line_ready()
    rs_finish(4)
    landing_free()
    hidden_gradient()
    ag_sent(3)
    landing_wait()
    rs_start(3, hn, up)
    rs_middle(2)
    feed_output()
    far_add(1, 2)
    attend_out_back()
    ag_sent(1)
    rs_start(1, dz, ob)
    far_add(1, 3)
    rs_finish(2)
    rs_middle(3)
    attend_back()
    project_back()
    ag_sent(0)
    rs_start(0, xh, dq)
    rs_finish(3)
    rs_middle(1)
    rs_start(5, xh, dq)
    rs_start(6, xh, dq)
    rs_middle(0)
    rs_finish(1)
    bias_back()
    token_gradient()
    rs_middle(5)
    rs_middle(6)
    rs_finish(0)
    bias_last()
    block_result()
    rs_finish(5)
    rs_finish(6)
    settle(*list(pending))


def kernel_call(rows, plane, block, width, hidden, aux, tokens, cotangent, position, segment, *weights):
    half = width // 2
    blocks = hidden // 128
    shard = -(-blocks // GROUP) * 128
    inner = half + 2 * HD
    heads = half // HD
    columns = (inner, half, shard, shard, shard)
    dma = pltpu.SemaphoreType.DMA
    vm = pltpu.VMEM
    group_tokens = GROUP * block
    any_space = pl.BlockSpec(memory_space=pl.ANY)
    out_shape = [jax.ShapeDtypeStruct((GROUP, rows, n), BF16) for n in columns]
    out_shape += [
        jax.ShapeDtypeStruct((3, block, width), BF16),
        jax.ShapeDtypeStruct((GROUP, 1, inner), F32),
        jax.ShapeDtypeStruct((block, width), BF16),
        jax.ShapeDtypeStruct((block, width), BF16),
    ]
    scratch = [
        vm((2, block, width), BF16), vm((2 * block, width), BF16), vm((2, 8, 128), F32), vm((2, 1, 128), jnp.int32),
        vm((2, rows, inner), BF16),
        vm((rows, hidden), BF16), vm((rows, hidden), BF16),
    ]
    scratch += [vm((width, n), BF16) for n in columns] + [vm((width, shard), BF16)]
    scratch += [vm((12 * 2 * rows, n), BF16) for n in columns[:4]]
    scratch += [vm((group_tokens, width), BF16)] * 2 + [vm((group_tokens, shard), BF16)] * 3
    scratch += [vm((group_tokens, width), BF16), vm((LINES * block, width), BF16), vm((LINES, block, width), BF16)]
    scratch += [
        vm((2, block, width), F32), vm((block, width), F32), vm((block, width), F32),
        vm((2 * block, width), BF16),
        vm((2 * block, half), BF16), vm((2, heads * block, HD), BF16), vm((2, block, HD), BF16), vm((2, block, HD), BF16),
        vm((2, heads * block, block), F32), vm((2, heads * block, HD), BF16), vm((2 * block, inner), BF16),
        vm((2, block, HD), F32), vm((2, block, HD), F32), vm((2, block, block), F32),
        vm((2, 1, inner), F32), vm((GROUP, 1, inner), F32), vm((4, 1, inner), F32), vm((4, 1, inner), F32), vm((1, inner), F32),
    ]
    scratch += [dma((26,))]
    scratch += [dma((7,)), dma((5, 4)), dma((5,)), dma((5, 5)), dma((7,)), dma((7, 8)), dma((7,)), dma((7,))]
    scratch += [dma((2, 2)), dma((2, 8)), dma((2, 2)), dma((2, 8)), dma((4,)), dma((4,)), dma((5,)), dma((5,))]
    scratch += [pltpu.SemaphoreType.REGULAR] * 3
    return pl.pallas_call(
        functools.partial(mega, rows, plane),
        out_shape=out_shape,
        in_specs=[any_space] * 12,
        out_specs=[any_space] * 9,
        scratch_shapes=scratch,
        compiler_params=pltpu.CompilerParams(
            collective_id=0, has_side_effects=True, vmem_limit_bytes=64 * 2**20 - 2**17
        ),
        name="layer",
    )(tokens, cotangent, position, segment, aux, *weights)


def gather_outputs(rows, plane, hidden, *refs):
    (
        o1, o2, o3, o4, o5, bg, tg, bo, aux, wq, wk, wv, wg, wu,
        bo_out, tg_out, gain_one_out, wq_out, bq_out, wk_out, bk_out, wv_out, bv_out, wo_out, gain_two_out,
        wg_out, wu_out, wd_out, total,
    ) = refs
    step = pl.program_id(0)
    steps = pl.num_programs(0)
    half = wo_out.shape[1] // 2
    shard = o3.shape[2]
    per = o3.shape[0]
    short = GROUP * shard - hidden
    me = lax.axis_index(AXIS)
    row_id = lax.broadcasted_iota(jnp.int32, (128, 128), 0)
    lane_id = lax.broadcasted_iota(jnp.int32, (128, 128), 1)

    def column(row):
        return jnp.sum(jnp.where(row_id == lane_id, row, 0.0), axis=1, keepdims=True)[:rows]

    def as_row(col):
        return jnp.sum(jnp.where(row_id[:rows, :rows] == lane_id[:rows, :rows], col, 0.0), axis=0, keepdims=True)

    gain_one = column(aux[2:3])
    gain_two = column(aux[3:4])

    @pl.when(step == 0)
    def _():
        bo_out[...] = bo[...]
        tg_out[...] = tg[...]
        sums = jnp.zeros((rows, 1), F32)
        for side in range(2):
            part = o1[side].astype(F32)
            for zz in range(1, LINES):
                part = part + o1[2 * zz + side].astype(F32)
            q_part, k_part, v_part = part[:, :half], part[:, half : half + HD], part[:, half + HD :]
            here, keys = pl.ds(side * half, half), pl.ds(side * HD, HD)
            sums = sums + jnp.sum(q_part * wq[:, here].astype(F32), axis=1, keepdims=True)
            sums = sums + jnp.sum(k_part * wk[:, keys].astype(F32), axis=1, keepdims=True)
            sums = sums + jnp.sum(v_part * wv[:, keys].astype(F32), axis=1, keepdims=True)
            wq_out[:, here] = q_part * gain_one
            wk_out[:, keys] = k_part * gain_one
            wv_out[:, keys] = v_part * gain_one
            part = o2[side].astype(F32)
            for zz in range(1, LINES):
                part = part + o2[2 * zz + side].astype(F32)
            wo_out[:, here] = part
        gain_one_out[...] = as_row(sums)
        sides = [(bg[side] + bg[2 + side]) + (bg[4 + side] + bg[6 + side]) for side in range(2)]
        bk_out[:, 0:HD] = sides[0][:, half : half + HD]
        bk_out[:, HD : 2 * HD] = sides[1][:, half : half + HD]
        mine = jnp.where(lax.div(me, plane * LINES) == 0, sides[0], sides[1])
        place = lax.rem(me, plane * LINES)

        def taken(row, count):
            size = row.shape[1]
            wide = jnp.broadcast_to(row, (8, size))
            return pltpu.roll(wide, lax.rem(size - place * count, size), 1)[0:1, :count]

        bq_out[...] = taken(mine[:, :half], rows)
        bv_out[...] = taken(mine[:, half + HD :], rows // KEYS)
        total[...] = jnp.zeros_like(total)

    def put(first):
        sums = jnp.zeros((rows, 1), F32)
        for i in range(per):
            skip = first if i == per - 1 else 0
            cols = pl.ds(i * shard, shard - skip)
            gate = o3[i][:, skip:].astype(F32)
            lift = o4[i][:, skip:].astype(F32)
            sums = sums + jnp.sum(gate * wg[:, cols].astype(F32) + lift * wu[:, cols].astype(F32), axis=1, keepdims=True)
            wg_out[:, cols] = gate * gain_two
            wu_out[:, cols] = lift * gain_two
            wd_out[:, cols] = o5[i][:, skip:].astype(F32)
        total[...] = total[...] + sums

    @pl.when(step < steps - 1)
    def _():
        put(0)

    @pl.when(step == steps - 1)
    def _():
        put(short)
        gain_two_out[...] = as_row(total[...])


def output_call(rows, plane, block, width, hidden, pieces, bias_sum, token_grad, block_output, aux, weights):
    per = 4
    shard = pieces[2].shape[2]
    key_width = weights[1].shape[1]

    def whole(shape):
        return pl.BlockSpec(shape, lambda i: (0,) * len(shape))

    feed = pl.BlockSpec((per, rows, shard), lambda i: (i, 0, 0))
    wide = pl.BlockSpec((rows, per * shard), lambda i: (0, i))
    shapes = [
        ((block, width), BF16), ((block, width), BF16), ((1, rows), F32), ((rows, width), F32), ((1, rows), F32),
        ((rows, key_width), F32), ((1, key_width), F32), ((rows, key_width), F32), ((1, rows // KEYS), F32),
        ((rows, width), F32), ((1, rows), F32),
        ((rows, hidden), F32), ((rows, hidden), F32), ((rows, hidden), F32),
    ]
    return pl.pallas_call(
        functools.partial(gather_outputs, rows, plane, hidden),
        grid=(GROUP // per,),
        out_shape=[jax.ShapeDtypeStruct(*shape) for shape in shapes],
        in_specs=[whole(pieces[0].shape), whole(pieces[1].shape), feed, feed, feed, whole(bias_sum.shape)]
        + [whole((block, width))] * 2 + [whole(aux.shape)]
        + [whole((rows, width)), whole((rows, key_width)), whole((rows, key_width)), wide, wide],
        out_specs=[whole(shape) for shape, _ in shapes[:11]] + [wide] * 3,
        scratch_shapes=[pltpu.VMEM((rows, 1), F32)],
        compiler_params=pltpu.CompilerParams(vmem_limit_bytes=64 * 2**20 - 2**17),
        name="outputs",
    )(*pieces, bias_sum, token_grad, block_output, aux, *weights)


def kernel_body(
    tokens, segment, position, first_gain, query_weight, query_bias, key_weight, key_bias, value_weight, value_bias,
    out_weight, second_gain, gate_weight, up_weight, down_weight, cotangent,
):
    count = lax.axis_size(AXIS)
    plane = count // GROUP
    rows, width = query_weight.shape
    block = tokens.shape[0]
    hidden = gate_weight.shape[1]

    aux = jnp.zeros((1024,), F32)
    for n, vector in enumerate((first_gain, second_gain, query_bias, key_bias, value_bias), 2):
        aux = aux + jnp.pad(vector.astype(F32), (128 * n, 1024 - 128 * n - vector.shape[0]))
    aux = aux.reshape(8, 128)
    *pieces, _, bias_sum, token_grad, block_output = kernel_call(
        rows, plane, block, width, hidden, aux, tokens, cotangent, position[None], segment[None],
        query_weight, key_weight, value_weight, out_weight, gate_weight, up_weight, down_weight,
    )
    outs = output_call(
        rows, plane, block, width, hidden, pieces, bias_sum, token_grad, block_output, aux,
        (query_weight, key_weight, value_weight, gate_weight, up_weight),
    )
    return tuple(out.reshape(-1) if out.shape[0] == 1 else out for out in outs)


def layer(*args):
    tokens, query_weight, key_weight, gate_weight = args[0], args[4], args[6], args[12]
    rows, width = query_weight.shape
    fits = (
        lax.axis_size(AXIS) == 4 * GROUP
        and rows % 16 == 0
        and rows * lax.axis_size(AXIS) == width
        and width == H * HD
        and key_weight.shape[1] == KV * HD
        and KV == 2
        and tokens.shape[0] == 128
        and gate_weight.shape[1] % 128 == 0
    )
    return kernel_body(*args) if fits else array_body(*args)


def solution(mesh):
    split = P(AXIS)
    split_rows = P(AXIS, None)
    return jax.shard_map(
        layer,
        mesh=mesh,
        in_specs=(
            split_rows, split, split, split, split_rows, split, split_rows, split,
            split_rows, split, split_rows, split, split_rows, split_rows, split_rows, split_rows,
        ),
        out_specs=(
            split_rows, split_rows, split, split_rows, split, split_rows, P(),
            split_rows, split, split_rows, split, split_rows, split_rows, split_rows,
        ),
        check_vma=False,
    )
```
